32 devices in a mesh: seq: 32 (over z, y, x, core).
Axes of the slice: x: 2, y: 2, z: 4, core: 2. Of those that a mesh axis runs over, the one named last changes fastest.
Arguments:
- queries: bfloat16 [12288, 1024], P('seq'), may hold values from -125 to 125, as said below
- keys_values: bfloat16 [2, 12288, 1024], P(None, 'seq'), may hold values from -6 to 6, as said below
- rand_blocks: int32 [96, 3], P('seq'), may hold values from 0 to 47, as said below
- global_ids: int32 [2], replicated, may hold values from 0 to 95
- out_weight: bfloat16 [1024, 2048], replicated, may hold values from -0.1875 to 0.1875
Outputs:
- layer_out: bfloat16 [12288, 2048], P('seq')
The draws below stay inside these ranges and needn't reach their ends.
Inputs may be any that keep to these rules, and one draw needn't show every extreme that they name: queries stay within the range. `keys_values`: keys and values stay within the range. `rand_blocks`: entry e names the block held by the segment's device number e // 3. Among the 9 entries of the rows of one device (aligned blocks of 3 rows), no segment device is named more than 1 times, and some segment device is named exactly 1 times.
All inputs are finite; a program needn't handle non-finite values.
Results may differ from the reference program's by a relative error of at most 0.0057.
Values may be sent and summed in bfloat16 or wider, within the bound.
No kernel may reach another device: no remote copies, remote signals or barrier semaphores. Data moves between devices by JAX's collectives and lax.ppermute only.
A program may use at most 192 MiB of HBM per device.

```python
import math
import jax
import jax.numpy as jnp
from jax import lax

D = 2048
HEADS = 8
HEAD_DIM = 128
BLOCK = 128
RAND = 3
GLOB = 2
SEG_DEV = 16
INNER = 1024
BLK_DEV = 3
SEG_BLK = 48
TOKENS = 12288
NBLK = 96


def shared_fields(key):
    keys_part = jnp.clip(jax.random.normal(jax.random.fold_in(key, 11), (TOKENS, INNER), jnp.float32), -6.0, 6.0)
    query_part = jnp.clip(jax.random.normal(jax.random.fold_in(key, 12), (TOKENS, INNER), jnp.float32), -6.0, 6.0)
    return (keys_part, query_part)


def draw_keys_values(key, part):
    keys_part, query_part = shared_fields(key)
    value_part = jnp.clip(jax.random.normal(jax.random.fold_in(key, 13), (TOKENS, INNER), jnp.float32), -6.0, 6.0)
    return jnp.stack([keys_part, value_part]).astype(jnp.bfloat16)


def draw_queries(key, part):
    keys_part, query_part = shared_fields(key)
    return query_part.astype(jnp.bfloat16)


def draw_rand_blocks(key, part):
    device_count = NBLK // BLK_DEV
    slot_count = BLK_DEV * RAND
    order_keys = jax.random.split(jax.random.fold_in(key, 21), device_count)

    def device_owners(one_key):
        ordering = jax.random.permutation(one_key, SEG_DEV).astype(jnp.int32)
        slot_index = jnp.arange(slot_count, dtype=jnp.int32)
        return jnp.take(ordering, slot_index % SEG_DEV)
    owners = jax.vmap(device_owners)(order_keys)
    local_ids = jax.random.randint(jax.random.fold_in(key, 22), (device_count, slot_count), 0, BLK_DEV).astype(jnp.int32)
    return (owners * BLK_DEV + local_ids).reshape(NBLK, RAND).astype(jnp.int32)


def centred(key, shape, scale, limit, held_as=jnp.bfloat16):
    entries = scale * jax.random.normal(key, shape, jnp.float32)
    return jnp.clip(entries, min=-limit, max=limit).astype(held_as)


def setup_inputs(seed: int = 0) -> dict:
    seeds = jax.random.split(jax.random.key(seed), 6)
    queries = draw_queries(jax.random.fold_in(seeds[5], 71), 0)
    keys_values = draw_keys_values(jax.random.fold_in(seeds[5], 71), 0)
    rand_blocks = draw_rand_blocks(jax.random.fold_in(seeds[5], 71), 0)
    global_ids = jax.random.randint(seeds[3], (GLOB,), 0, NBLK).astype(jnp.int32)
    out_weight = centred(seeds[4], (INNER, D), INNER ** -0.5, 0.1875)
    return dict(queries=queries, keys_values=keys_values, rand_blocks=rand_blocks, global_ids=global_ids, out_weight=out_weight)


def reference(queries, keys_values, rand_blocks, global_ids, out_weight):
    inner_width = queries.shape[1]
    scale_factor = 1.0 / math.sqrt(HEAD_DIM)
    query_blocks = queries.reshape(NBLK, BLOCK, HEADS, HEAD_DIM)
    pair_blocks = keys_values.reshape(2, NBLK, BLOCK, inner_width)

    def attend_block(block_index):
        seg_start = block_index // SEG_BLK * SEG_BLK
        window_ids = jnp.stack([(block_index - 1) % NBLK, block_index, (block_index + 1) % NBLK]).astype(jnp.int32)
        key_blocks = jnp.concatenate([window_ids, global_ids.astype(jnp.int32), (seg_start + rand_blocks[block_index]).astype(jnp.int32)])
        chosen = pair_blocks[:, key_blocks].reshape(2, 8 * BLOCK, HEADS, HEAD_DIM)
        query_now = query_blocks[block_index]
        scores = jnp.einsum('qhd,khd->hqk', query_now.astype(jnp.float32), chosen[0].astype(jnp.float32)) * scale_factor
        probs = jax.nn.softmax(scores, axis=-1).astype(jnp.bfloat16)
        attended = jnp.einsum('hqk,khd->qhd', probs.astype(jnp.float32), chosen[1].astype(jnp.float32))
        return attended.astype(jnp.bfloat16).reshape(BLOCK, inner_width)
    attended_all = lax.map(attend_block, jnp.arange(NBLK, dtype=jnp.int32))
    attended_all = attended_all.reshape(NBLK * BLOCK, inner_width)
    return jnp.dot(attended_all, out_weight, preferred_element_type=jnp.float32).astype(jnp.bfloat16)
```

```python
import functools
import math

import jax
import jax.numpy as jnp
from jax import lax
from jax.experimental import pallas as pl
from jax.experimental.pallas import tpu as pltpu
from jax.sharding import PartitionSpec as P

HEADS = 8
HEAD_DIM = 128
BLOCK = 128
RAND = 3
GLOB = 2
SEG_CHIPS = 8
HERE = 3
CHIP = 2 * HERE
HALF = HEADS // 2
SLAB = 2 * HALF * BLOCK

CUT = 80
PART_ROWS = (256 + CUT, 256 + CUT, 256 + 2 * (BLOCK - CUT))
PART_AT = (0, PART_ROWS[0], PART_ROWS[0] + PART_ROWS[1])
PART_DIMS = ((1, 2, 4), (2, 4, 1), (4, 1, 2))
N_ENTRY = CHIP + 2 + GLOB + CHIP * RAND


def swap(value, mask):
    n = lax.axis_size("seq")
    return lax.ppermute(value, "seq", [(i, i ^ mask) for i in range(n)])


def pack_kernel(core_ref, kv_ref, q_ref, own_ref, mate_ref, q_own_ref, q_mate_ref):
    core = core_ref[0]
    for which, kv_out, q_out in ((core, own_ref, q_own_ref), (1 - core, mate_ref, q_mate_ref)):
        first = pl.multiple_of(which * (HALF * HEAD_DIM), HEAD_DIM)

        def unit(pair, block, head, low, high):
            cols = pl.ds(first + head * HEAD_DIM, HEAD_DIM)
            return kv_ref[pair, block * BLOCK + low : block * BLOCK + high, cols]

        for block in range(HERE):
            for head in range(HALF):
                cols = pl.ds(first + head * HEAD_DIM, HEAD_DIM)
                q_out[block, head] = q_ref[block * BLOCK : (block + 1) * BLOCK, cols]
            for part in range(3):
                at = PART_AT[part]
                kv_out[block, at : at + BLOCK] = unit(0, block, part, 0, BLOCK)
                kv_out[block, at + BLOCK : at + 2 * BLOCK] = unit(1, block, part, 0, BLOCK)
            last = HALF - 1
            a, b, c = (at + 2 * BLOCK for at in PART_AT)
            kv_out[block, a : a + CUT] = unit(0, block, last, 0, CUT)
            kv_out[block, b : b + CUT] = unit(1, block, last, 0, CUT)
            rest = BLOCK - CUT
            kv_out[block, c : c + rest] = unit(0, block, last, CUT, BLOCK)
            kv_out[block, c + rest : c + 2 * rest] = unit(1, block, last, CUT, BLOCK)


def pack(core, keys_values, queries):
    slab = jax.ShapeDtypeStruct((HERE, SLAB, HEAD_DIM), jnp.bfloat16)
    q_slab = jax.ShapeDtypeStruct((HERE, HALF, BLOCK, HEAD_DIM), jnp.bfloat16)
    vmem = pl.BlockSpec(memory_space=pltpu.VMEM)
    return pl.pallas_call(
        pack_kernel,
        out_shape=(slab, slab, q_slab, q_slab),
        in_specs=[pl.BlockSpec(memory_space=pltpu.SMEM), vmem, vmem],
        out_specs=(vmem,) * 4,
        compiler_params=pltpu.CompilerParams(vmem_limit_bytes=24 * 2**20),
    )(core.reshape(1), keys_values, queries)


def attend_kernel(
    where_ref, rand_ref, q_own, q_mate,
    near0, near1, near2, side0, side1, side2, far0, far1, far2, glob, edge,
    out_own, out_mate, buf0, buf1, buf2, sems,
):
    chip, core = where_ref[0], where_ref[1]
    nears, sides, fars, bufs = (near0, near1, near2), (side0, side1, side2), (far0, far1, far2), (buf0, buf1, buf2)

    def slot_of(block):
        return ((block // HERE) ^ core) * HERE + lax.rem(block, HERE)

    def fetch(block, entry, sem):
        there = block // CHIP
        slot = slot_of(block - there * CHIP)
        apart = chip ^ there
        for part in range(3):
            d1, d2, d3 = PART_DIMS[part]
            b1 = jnp.where(apart & d1 != 0, CHIP, 0)
            b2 = apart & d2 != 0
            b3 = apart & d3 != 0

            @pl.when(jnp.logical_and(jnp.logical_not(b2), jnp.logical_not(b3)))
            def _():
                pltpu.make_async_copy(nears[part].at[b1 + slot], bufs[part].at[entry], sem).start()

            @pl.when(jnp.logical_and(b2, jnp.logical_not(b3)))
            def _():
                pltpu.make_async_copy(sides[part].at[b1 + slot], bufs[part].at[entry], sem).start()

            @pl.when(b3)
            def _():
                place = b1 + jnp.where(b2, 2 * CHIP, 0) + slot
                pltpu.make_async_copy(fars[part].at[place], bufs[part].at[entry], sem).start()

    def fetch_slab(slab, entry, sem):
        for part in range(3):
            rows = pl.ds(PART_AT[part], PART_ROWS[part])
            pltpu.make_async_copy(slab.at[rows], bufs[part].at[entry], sem).start()

    shared = sems.at[CHIP]
    for part in range(3):
        pltpu.make_async_copy(nears[part].at[pl.ds(0, CHIP)], bufs[part].at[pl.ds(0, CHIP)], shared).start()
    for g in range(GLOB):
        fetch_slab(glob.at[g], CHIP + 2 + g, shared)
    first, last = chip == 0, chip == SEG_CHIPS - 1

    @pl.when(first)
    def _():
        fetch_slab(edge, CHIP, shared)

    @pl.when(jnp.logical_not(first))
    def _():
        fetch(chip * CHIP - 1, CHIP, shared)

    @pl.when(last)
    def _():
        fetch_slab(edge, CHIP + 1, shared)

    @pl.when(jnp.logical_not(last))
    def _():
        fetch(chip * CHIP + CHIP, CHIP + 1, shared)

    @pl.loop(0, CHIP * RAND)
    def _(k):
        row = k // RAND
        fetch(rand_ref[row, k - row * RAND], CHIP + 2 + GLOB + k, sems.at[row])

    for part in range(3):
        pltpu.make_async_copy(
            fars[part].at[pl.ds(0, CHIP + 2 + GLOB)], bufs[part].at[pl.ds(0, CHIP + 2 + GLOB)], shared
        ).wait()

    factor = math.log2(math.e) / math.sqrt(HEAD_DIM)

    def one_block(e, q_ref, out_ref, local):
        for part in range(3):
            pltpu.make_async_copy(
                fars[part].at[pl.ds(0, RAND)], bufs[part].at[pl.ds(0, RAND)], sems.at[e]
            ).wait()
        block = slot_of(e)
        prev = jnp.where(block == 0, CHIP, slot_of(jnp.maximum(block - 1, 0)))
        nxt = jnp.where(block == CHIP - 1, CHIP + 1, slot_of(jnp.minimum(block + 1, CHIP - 1)))
        at = CHIP + 2 + GLOB + e * RAND
        entries = [prev, e, nxt, CHIP + 2, CHIP + 3, at, at + 1, at + 2]
        rest = BLOCK - CUT
        for head in range(HALF):
            if head < 3:
                keys = [bufs[head][i, 0:BLOCK] for i in entries]
                values = [bufs[head][i, BLOCK : 2 * BLOCK] for i in entries]
            else:
                t = 2 * BLOCK
                keys, values = [], []
                for i in entries:
                    keys += [buf0[i, t : t + CUT], buf2[i, t : t + rest]]
                    values += [buf1[i, t : t + CUT], buf2[i, t + rest : t + 2 * rest]]
            keys = jnp.concatenate(keys, axis=0)
            values = jnp.concatenate(values, axis=0)
            scores = lax.dot_general(
                q_ref[local, head], keys, (((1,), (1,)), ((), ())), preferred_element_type=jnp.float32
            )
            top = jnp.max(scores, axis=-1, keepdims=True)
            probs = jnp.exp2((scores - top) * factor)
            probs = probs * (1.0 / jnp.sum(probs, axis=-1, keepdims=True))
            mixed = jnp.dot(probs.astype(jnp.bfloat16), values, preferred_element_type=jnp.float32)
            cols = slice(head * HEAD_DIM, (head + 1) * HEAD_DIM)
            out_ref[pl.ds(pl.multiple_of(local * BLOCK, BLOCK), BLOCK), cols] = mixed.astype(jnp.bfloat16)

    @pl.loop(0, HERE)
    def _(local):
        one_block(HERE + local, q_mate, out_mate, local)

    @pl.loop(0, HERE)
    def _(local):
        one_block(local, q_own, out_own, local)


def attend(where, rand, q_own, q_mate, nears, sides, fars, glob, edge):
    vmem = pl.BlockSpec(memory_space=pltpu.VMEM)
    smem = pl.BlockSpec(memory_space=pltpu.SMEM)
    anywhere = pl.BlockSpec(memory_space=pl.ANY)
    out = jax.ShapeDtypeStruct((HERE * BLOCK, HALF * HEAD_DIM), jnp.bfloat16)
    return pl.pallas_call(
        attend_kernel,
        out_shape=(out, out),
        in_specs=[smem, smem, vmem, vmem] + [anywhere] * 11,
        out_specs=(vmem, vmem),
        scratch_shapes=[pltpu.VMEM((N_ENTRY, rows, HEAD_DIM), jnp.bfloat16) for rows in PART_ROWS]
        + [pltpu.SemaphoreType.DMA((CHIP + 1,))],
        compiler_params=pltpu.CompilerParams(vmem_limit_bytes=40 * 2**20),
    )(where, rand, q_own, q_mate, *nears, *sides, *fars, glob, edge)


def pick(low, a, b):
    return jnp.where(low, a, b)


def global_slabs(slabs, global_ids, device, core):
    n = lax.axis_size("seq")
    chip = device // 2
    owned = []
    for g in range(GLOB):
        block = global_ids[g]
        inside = block % CHIP
        slot = ((inside // HERE) ^ core) * HERE + inside % HERE
        slab = lax.dynamic_index_in_dim(slabs, slot, 0, keepdims=False)
        owned.append(jnp.where(block // CHIP == chip, slab, jnp.zeros_like(slab)))
    low_x, low_y = chip & 1 == 0, chip & 2 == 0
    got = swap(pick(low_x, owned[1], owned[0]), 2)
    one = pick(low_x, owned[0], owned[1]) + got
    top, bottom = one[: SLAB // 2], one[SLAB // 2 :]
    got = swap(pick(low_y, bottom, top), 4)
    quarter = pick(low_y, top, bottom) + got
    mask = 8
    while mask < n:
        quarter = quarter + swap(quarter, mask)
        mask *= 2
    got = swap(quarter, 4)
    one = jnp.concatenate([pick(low_y, quarter, got), pick(low_y, got, quarter)], axis=0)
    got = swap(one, 2)
    return jnp.stack([pick(low_x, one, got), pick(low_x, got, one)])


def local(queries, keys_values, rand_blocks, global_ids, out_weight):
    n = lax.axis_size("seq")
    device = lax.axis_index("seq")
    core = device % 2
    chip = (device // 2) % SEG_CHIPS
    own, mate, q_own, q_mate = pack(core, keys_values, queries)
    got = swap(mate, 1)
    slabs = jnp.concatenate([own, got], axis=0)

    nears, sides, fars = [], [], []
    firsts = []
    for part in range(3):
        piece = slabs[:, PART_AT[part] : PART_AT[part] + PART_ROWS[part]]
        firsts.append((piece, swap(piece, 2 * PART_DIMS[part][0])))
    rand = jnp.concatenate([rand_blocks, swap(rand_blocks, 1)], axis=0)
    q_got = swap(q_mate, 1)
    at = jnp.where(chip == SEG_CHIPS - 1, (1 - core) * HERE + HERE - 1, core * HERE)
    pairs = []
    chips = n // 2
    for c in range(chips):
        if c % SEG_CHIPS == SEG_CHIPS - 1:
            pairs += [(2 * c + k, 2 * ((c + 1) % chips) + k) for k in range(2)]
        if c % SEG_CHIPS == 0:
            pairs += [(2 * c + k, 2 * ((c - 1) % chips) + k) for k in range(2)]
    edge = lax.ppermute(lax.dynamic_index_in_dim(slabs, at, 0, keepdims=False), "seq", pairs)
    glob = global_slabs(slabs, global_ids, device, core)

    for part in range(3):
        piece, first = firsts[part]
        nears.append(jnp.concatenate([piece, first], axis=0))
        sides.append(swap(nears[part], 2 * PART_DIMS[part][1]))
    for part in range(3):
        whole = jnp.concatenate([nears[part], sides[part]], axis=0)
        fars.append(swap(whole, 2 * PART_DIMS[part][2]))

    where = jnp.stack([chip, core])
    out_own, out_mate = attend(where, rand, q_own, q_got, nears, sides, fars, glob, edge)
    got = swap(out_mate, 1)
    low = core == 0
    attended = jnp.concatenate([pick(low, out_own, got), pick(low, got, out_own)], axis=1)
    return jnp.dot(attended, out_weight, preferred_element_type=jnp.float32).astype(jnp.bfloat16)


def solution(mesh):
    placed = (P("seq", None), P(None, "seq", None), P("seq", None), P(), P())
    return jax.shard_map(
        local, mesh=mesh, in_specs=placed, out_specs=P("seq", None), check_vma=False
    )
```

```python
import functools
import math

import jax
import jax.numpy as jnp
from jax import lax
from jax.experimental import pallas as pl
from jax.experimental.pallas import tpu as pltpu
from jax.sharding import PartitionSpec as P

HEADS = 8
HEAD_DIM = 128
BLOCK = 128
RAND = 3
GLOB = 2
SEG_CHIPS = 8
HERE = 3
CHIP = 2 * HERE
HALF = HEADS // 2
SLAB = 2 * HALF * BLOCK

CUT = 80
PART_ROWS = (256 + CUT, 256 + CUT, 256 + 2 * (BLOCK - CUT))
PART_AT = (0, PART_ROWS[0], PART_ROWS[0] + PART_ROWS[1])
PART_DIMS = ((1, 2, 4), (2, 4, 1), (4, 1, 2))


def swap(value, mask):
    n = lax.axis_size("seq")
    return lax.ppermute(value, "seq", [(i, i ^ mask) for i in range(n)])


def pack_kernel(core_ref, kv_ref, own_ref, mate_ref):
    core = core_ref[0]
    for which, kv_out in ((1 - core, mate_ref), (core, own_ref)):
        first = pl.multiple_of(which * (HALF * HEAD_DIM), HEAD_DIM)

        def unit(pair, block, head, low, high):
            cols = pl.ds(first + head * HEAD_DIM, HEAD_DIM)
            return kv_ref[pair, block * BLOCK + low : block * BLOCK + high, cols]

        for block in range(HERE):
            for part in range(3):
                at = PART_AT[part]
                kv_out[block, at : at + BLOCK] = unit(0, block, part, 0, BLOCK)
                kv_out[block, at + BLOCK : at + 2 * BLOCK] = unit(1, block, part, 0, BLOCK)
            last = HALF - 1
            a, b, c = (at + 2 * BLOCK for at in PART_AT)
            kv_out[block, a : a + CUT] = unit(0, block, last, 0, CUT)
            kv_out[block, b : b + CUT] = unit(1, block, last, 0, CUT)
            rest = BLOCK - CUT
            kv_out[block, c : c + rest] = unit(0, block, last, CUT, BLOCK)
            kv_out[block, c + rest : c + 2 * rest] = unit(1, block, last, CUT, BLOCK)


def pack(core, keys_values):
    slab = jax.ShapeDtypeStruct((HERE, SLAB, HEAD_DIM), jnp.bfloat16)
    vmem = pl.BlockSpec(memory_space=pltpu.VMEM)
    return pl.pallas_call(
        pack_kernel,
        out_shape=(slab, slab),
        in_specs=[pl.BlockSpec(memory_space=pltpu.SMEM), vmem],
        out_specs=(vmem,) * 2,
        compiler_params=pltpu.CompilerParams(vmem_limit_bytes=24 * 2**20),
    )(core.reshape(1), keys_values)


OUTER, INNER, OWN, GLOBAL, RANDOM = 0, 1, 2, 2 + HERE, 2 + HERE + GLOB
N_ENTRY = RANDOM + HERE * RAND


def attend_kernel(
    mine, where_ref, rand_ref, q_ref,
    near0, near1, near2, side0, side1, side2, far0, far1, far2, quad0, quad1, quad2, quad3, edge,
    out_ref, buf0, buf1, buf2, sems,
):
    chip, core = where_ref[0], where_ref[1]
    nears, sides, fars = (near0, near1, near2), (side0, side1, side2), (far0, far1, far2)
    bufs, quads = (buf0, buf1, buf2), (quad0, quad1, quad2, quad3)
    half = core if mine else 1 - core
    base = 0 if mine else HERE

    def slot_of(block):
        return ((block // HERE) ^ core) * HERE + lax.rem(block, HERE)

    def fetch(block, entry, sem):
        there = block // CHIP
        slot = slot_of(block - there * CHIP)
        apart = chip ^ there
        for part in range(3):
            d1, d2, d3 = PART_DIMS[part]
            b1 = jnp.where(apart & d1 != 0, CHIP, 0)
            b2 = apart & d2 != 0
            b3 = apart & d3 != 0

            @pl.when(jnp.logical_and(jnp.logical_not(b2), jnp.logical_not(b3)))
            def _():
                pltpu.make_async_copy(nears[part].at[b1 + slot], bufs[part].at[entry], sem).start()

            @pl.when(jnp.logical_and(b2, jnp.logical_not(b3)))
            def _():
                pltpu.make_async_copy(sides[part].at[b1 + slot], bufs[part].at[entry], sem).start()

            @pl.when(b3)
            def _():
                place = b1 + jnp.where(b2, 2 * CHIP, 0) + slot
                pltpu.make_async_copy(fars[part].at[place], bufs[part].at[entry], sem).start()

    def fetch_rows(source, low, high, entry, sem):
        for part in range(3):
            a, b = max(low, PART_AT[part]), min(high, PART_AT[part] + PART_ROWS[part])
            if a < b:
                to = bufs[part].at[entry, pl.ds(a - PART_AT[part], b - a)]
                pltpu.make_async_copy(source.at[pl.ds(a - low, b - a)], to, sem).start()

    def wait(low, count, sem):
        for part in range(3):
            of = bufs[part].at[pl.ds(low, count)]
            pltpu.make_async_copy(fars[part].at[pl.ds(0, count)], of, sem).wait()

    shared = sems.at[HERE]
    for part in range(3):
        of = nears[part].at[pl.ds(base, HERE)]
        pltpu.make_async_copy(of, bufs[part].at[pl.ds(OWN, HERE)], shared).start()
        inner = (HERE - base) + jnp.where(half == 0, 0, HERE - 1)
        pltpu.make_async_copy(nears[part].at[inner], bufs[part].at[INNER], shared).start()
    at_edge = chip == jnp.where(half == 0, 0, SEG_CHIPS - 1)

    @pl.when(at_edge)
    def _():
        fetch_rows(edge, 0, SLAB, OUTER, shared)

    @pl.when(jnp.logical_not(at_edge))
    def _():
        fetch(chip * CHIP + jnp.where(half == 0, -1, CHIP), OUTER, shared)

    for k in range(4):
        entry = GLOBAL + ((chip & 1) ^ (k & 1))
        row = ((chip >> 1) & 1) ^ (k >> 1)
        for value in range(2):

            @pl.when(row == value)
            def _():
                fetch_rows(quads[k], value * (SLAB // 2), (value + 1) * (SLAB // 2), entry, shared)

    for row in range(HERE):
        for k in range(RAND):
            fetch(rand_ref[row, k], RANDOM + row * RAND + k, sems.at[row])
    wait(0, RANDOM, shared)

    factor = math.log2(math.e) / math.sqrt(HEAD_DIM)
    rest, tail = BLOCK - CUT, 2 * BLOCK
    for row in range(HERE):
        wait(RANDOM, RAND, sems.at[row])
        outer_first = half == 0
        before = OWN + row - 1 if row else jnp.where(outer_first, OUTER, INNER)
        after = OWN + row + 1 if row < HERE - 1 else jnp.where(outer_first, INNER, OUTER)
        at = RANDOM + row * RAND
        entries = [before, OWN + row, after, GLOBAL, GLOBAL + 1, at, at + 1, at + 2]
        keys, values = [], []
        for head in range(HALF - 1):
            keys.append([bufs[head][i, 0:BLOCK] for i in entries])
            values.append([bufs[head][i, BLOCK : 2 * BLOCK] for i in entries])
        keys.append([v for i in entries for v in (buf0[i, tail : tail + CUT], buf2[i, tail : tail + rest])])
        values.append(
            [v for i in entries for v in (buf1[i, tail : tail + CUT], buf2[i, tail + rest : tail + 2 * rest])]
        )
        scores = [
            lax.dot_general(
                q_ref[row, h], jnp.concatenate(keys[h], axis=0), (((1,), (1,)), ((), ())),
                preferred_element_type=jnp.float32,
            )
            for h in range(HALF)
        ]
        probs = []
        for h in range(HALF):
            top = jnp.max(scores[h], axis=-1, keepdims=True)
            one = jnp.exp2((scores[h] - top) * factor)
            one = one * (1.0 / jnp.sum(one, axis=-1, keepdims=True))
            probs.append(one.astype(jnp.bfloat16))
        for h in range(HALF):
            mixed = jnp.dot(probs[h], jnp.concatenate(values[h], axis=0), preferred_element_type=jnp.float32)
            out_ref[row * BLOCK : (row + 1) * BLOCK, h * HEAD_DIM : (h + 1) * HEAD_DIM] = mixed.astype(jnp.bfloat16)


def attend(mine, where, rand, q, nears, sides, fars, quads, edge):
    vmem = pl.BlockSpec(memory_space=pltpu.VMEM)
    smem = pl.BlockSpec(memory_space=pltpu.SMEM)
    anywhere = pl.BlockSpec(memory_space=pl.ANY)
    flops = HERE * BLOCK * HALF * (RANDOM + RAND) * BLOCK * HEAD_DIM * 4
    return pl.pallas_call(
        functools.partial(attend_kernel, mine),
        out_shape=jax.ShapeDtypeStruct((HERE * BLOCK, HALF * HEAD_DIM), jnp.bfloat16),
        in_specs=[smem, smem, vmem] + [anywhere] * 14,
        out_specs=vmem,
        scratch_shapes=[pltpu.VMEM((N_ENTRY, rows, HEAD_DIM), jnp.bfloat16) for rows in PART_ROWS]
        + [pltpu.SemaphoreType.DMA((HERE + 1,))],
        compiler_params=pltpu.CompilerParams(vmem_limit_bytes=32 * 2**20),
        cost_estimate=pl.CostEstimate(flops=flops, bytes_accessed=N_ENTRY * SLAB * 256, transcendentals=0),
    )(where, rand, q, *nears, *sides, *fars, *quads, edge)


def project_kernel(core_ref, own_ref, got_ref, weight_ref, out_ref):
    core = core_ref[0]
    half = HALF * HEAD_DIM
    mine = weight_ref[pl.ds(pl.multiple_of(core * half, half), half), :]
    other = weight_ref[pl.ds(pl.multiple_of((1 - core) * half, half), half), :]
    total = jnp.dot(own_ref[...], mine, preferred_element_type=jnp.float32)
    total += jnp.dot(got_ref[...], other, preferred_element_type=jnp.float32)
    out_ref[...] = total.astype(out_ref.dtype)


def project(core, own, got, weight, tiles=4):
    depth, width = weight.shape
    rows, half = own.shape
    return pl.pallas_call(
        project_kernel,
        grid=(tiles,),
        out_shape=jax.ShapeDtypeStruct((rows, width), jnp.bfloat16),
        in_specs=[
            pl.BlockSpec(memory_space=pltpu.SMEM),
            pl.BlockSpec((rows, half), lambda i: (0, 0)),
            pl.BlockSpec((rows, half), lambda i: (0, 0)),
            pl.BlockSpec((depth, width // tiles), lambda i: (0, i)),
        ],
        out_specs=pl.BlockSpec((rows, width // tiles), lambda i: (0, i)),
        compiler_params=pltpu.CompilerParams(vmem_limit_bytes=24 * 2**20),
    )(core.reshape(1), own, got, weight)


def pick(low, a, b):
    return jnp.where(low, a, b)


def global_quarters(slabs, global_ids, device, core):
    n = lax.axis_size("seq")
    chip = device // 2
    x, y = chip & 1, (chip >> 1) & 1

    def quarter(g, h):
        block = global_ids[g]
        inside = block % CHIP
        slot = ((inside // HERE) ^ core) * HERE + inside % HERE
        rows = lax.dynamic_slice(slabs, (slot, h * (SLAB // 2), 0), (1, SLAB // 2, HEAD_DIM))[0]
        return jnp.where(block // CHIP == chip, rows, jnp.zeros_like(rows))

    total = quarter(x, y)
    total += swap(quarter(1 - x, y), 2) + swap(quarter(x, 1 - y), 4) + swap(quarter(1 - x, 1 - y), 6)
    mask = 8
    while mask < n:
        if 2 * mask < n:
            total = total + swap(total, mask) + swap(total, 2 * mask) + swap(total, 3 * mask)
        else:
            total = total + swap(total, mask)
        mask *= 4
    return [total, swap(total, 2), swap(total, 4), swap(total, 6)]


def local(queries, keys_values, rand_blocks, global_ids, out_weight):
    n = lax.axis_size("seq")
    device = lax.axis_index("seq")
    core = device % 2
    chip = (device // 2) % SEG_CHIPS
    own, mate = pack(core, keys_values)
    got = swap(mate, 1)
    slabs = jnp.concatenate([own, got], axis=0)

    firsts = []
    for part in range(3):
        piece = slabs[:, PART_AT[part] : PART_AT[part] + PART_ROWS[part]]
        firsts.append((piece, swap(piece, 2 * PART_DIMS[part][0])))
    rand_mate = swap(rand_blocks, 1)
    halves = queries.reshape(HERE, BLOCK, 2, HALF, HEAD_DIM).transpose(2, 0, 3, 1, 4)
    q_own = lax.dynamic_index_in_dim(halves, core, 0, keepdims=False)
    q_mate = swap(lax.dynamic_index_in_dim(halves, 1 - core, 0, keepdims=False), 1)
    at = jnp.where(chip == SEG_CHIPS - 1, (1 - core) * HERE + HERE - 1, core * HERE)
    pairs = []
    chips = n // 2
    for c in range(chips):
        if c % SEG_CHIPS == SEG_CHIPS - 1:
            pairs += [(2 * c + k, 2 * ((c + 1) % chips) + k) for k in range(2)]
        if c % SEG_CHIPS == 0:
            pairs += [(2 * c + k, 2 * ((c - 1) % chips) + k) for k in range(2)]
    edge = lax.ppermute(lax.dynamic_index_in_dim(slabs, at, 0, keepdims=False), "seq", pairs)
    quads = global_quarters(slabs, global_ids, device, core)

    nears, sides, fars = [], [], []
    for part in range(3):
        piece, first = firsts[part]
        nears.append(jnp.concatenate([piece, first], axis=0))
        sides.append(swap(nears[part], 2 * PART_DIMS[part][1]))
    for part in range(3):
        whole = jnp.concatenate([nears[part], sides[part]], axis=0)
        fars.append(swap(whole, 2 * PART_DIMS[part][2]))

    where = jnp.stack([chip, core])
    out_mate = attend(False, where, rand_mate, q_mate, nears, sides, fars, quads, edge)
    out_got = swap(out_mate, 1)
    out_own = attend(True, where, rand_blocks, q_own, nears, sides, fars, quads, edge)
    return project(core, out_own, out_got, out_weight)


def solution(mesh):
    placed = (P("seq", None), P(None, "seq", None), P("seq", None), P(), P())
    return jax.shard_map(
        local, mesh=mesh, in_specs=placed, out_specs=P("seq", None), check_vma=False
    )
```

```python
import functools
import math

import jax
import jax.numpy as jnp
from jax import lax
from jax.experimental import pallas as pl
from jax.experimental.pallas import tpu as pltpu
from jax.sharding import PartitionSpec as P

HEADS = 8
HEAD_DIM = 128
BLOCK = 128
RAND = 3
GLOB = 2
SEG_CHIPS = 8
HERE = 3
CHIP = 2 * HERE
HALF = HEADS // 2
SLAB = 2 * HALF * BLOCK

CUT = 80
PART_ROWS = (256 + CUT, 256 + CUT, 256 + 2 * (BLOCK - CUT))
PART_AT = (0, PART_ROWS[0], PART_ROWS[0] + PART_ROWS[1])
PART_DIMS = ((1, 2, 4), (2, 4, 1), (4, 1, 2))
MOST = 2 * SEG_CHIPS + 2
CAPS = (13, 14, 14)
SEG_BLK = SEG_CHIPS * CHIP
IDS = CHIP * RAND
FLAG = IDS
QUARTER = SLAB // 2
NOTE = 16


def swap(value, mask):
    n = lax.axis_size("seq")
    return lax.ppermute(value, "seq", [(i, i ^ mask) for i in range(n)])


def pack_kernel(core_ref, kv_ref, own_ref, mate_ref):
    core = core_ref[0]
    for which, kv_out in ((1 - core, mate_ref), (core, own_ref)):
        first = pl.multiple_of(which * (HALF * HEAD_DIM), HEAD_DIM)

        def unit(pair, block, head, low, high):
            cols = pl.ds(first + head * HEAD_DIM, HEAD_DIM)
            return kv_ref[pair, block * BLOCK + low : block * BLOCK + high, cols]

        for block in range(HERE):
            for part in range(3):
                at = PART_AT[part]
                kv_out[block, at : at + BLOCK] = unit(0, block, part, 0, BLOCK)
                kv_out[block, at + BLOCK : at + 2 * BLOCK] = unit(1, block, part, 0, BLOCK)
            last = HALF - 1
            a, b, c = (at + 2 * BLOCK for at in PART_AT)
            kv_out[block, a : a + CUT] = unit(0, block, last, 0, CUT)
            kv_out[block, b : b + CUT] = unit(1, block, last, 0, CUT)
            rest = BLOCK - CUT
            kv_out[block, c : c + rest] = unit(0, block, last, CUT, BLOCK)
            kv_out[block, c + rest : c + 2 * rest] = unit(1, block, last, CUT, BLOCK)


def pack(core, keys_values):
    slab = jax.ShapeDtypeStruct((HERE, SLAB, HEAD_DIM), jnp.bfloat16)
    vmem = pl.BlockSpec(memory_space=pltpu.VMEM)
    return pl.pallas_call(
        pack_kernel,
        out_shape=(slab, slab),
        in_specs=[pl.BlockSpec(memory_space=pltpu.SMEM), vmem],
        out_specs=(vmem,) * 2,
        compiler_params=pltpu.CompilerParams(vmem_limit_bytes=24 * 2**20),
    )(core.reshape(1), keys_values)


def list_wants(ids, chip, part, slots, base, act):
    dim = PART_DIMS[part][2]

    @pl.loop(0, SEG_BLK)
    def _(k):
        slots[base + k] = -1

    def add(block, count):
        place = base + block
        new = jnp.logical_and(((block // CHIP) ^ chip) & dim != 0, slots[place] < 0)

        @pl.when(new)
        def _():
            slots[place] = count
            if act is not None:
                act(block, count)

        return count + new.astype(jnp.int32)

    count = lax.fori_loop(0, IDS, lambda k, c: add(ids[k], c), jnp.int32(0))
    low, high = chip * CHIP - 1, chip * CHIP + CHIP
    count = add(jnp.where(chip == 0, chip * CHIP, low), count)
    return add(jnp.where(chip == SEG_CHIPS - 1, chip * CHIP, high), count)


def split_kernel(
    where_ref, glob_ref, ids_ref, own_ref, got_ref, piece0, piece1, piece2, mine, to_x, to_y, to_xy, edge, slots
):
    chip, core, chip_all = where_ref[0], where_ref[1], where_ref[2]
    over = jnp.int32(0)
    for part in range(3):
        count = list_wants(ids_ref, chip, part, slots, part * SEG_BLK, None)
        over = jnp.where(count > CAPS[part], 1, over)
    lane = lax.broadcasted_iota(jnp.int32, (NOTE, HEAD_DIM), 1)
    row = jnp.where(lane == FLAG, over, 0)
    for k in range(IDS):
        row = jnp.where(lane == k, ids_ref[k], row)
    note = row.astype(jnp.float32).astype(jnp.bfloat16)

    x, y = chip & 1, (chip >> 1) & 1
    for k, out in enumerate((mine, to_x, to_y, to_xy)):
        block = glob_ref[x ^ (k & 1)]
        half = y ^ (k >> 1)
        owner = block // CHIP
        inside = block - owner * CHIP
        place = lax.rem(inside, HERE)
        rows = pl.ds(pl.multiple_of(half * QUARTER, QUARTER), QUARTER)
        here = owner == chip_all
        mate = (inside // HERE) != core

        @pl.when(jnp.logical_and(here, jnp.logical_not(mate)))
        def _():
            out[0:QUARTER] = own_ref[place, rows]

        @pl.when(jnp.logical_and(here, mate))
        def _():
            out[0:QUARTER] = got_ref[place, rows]

        @pl.when(jnp.logical_not(here))
        def _():
            out[0:QUARTER] = jnp.zeros((QUARTER, HEAD_DIM), jnp.bfloat16)

        out[QUARTER : QUARTER + NOTE] = note

    for part, piece in enumerate((piece0, piece1, piece2)):
        rows = pl.ds(PART_AT[part], PART_ROWS[part])
        for block in range(HERE):
            piece[block] = own_ref[block, rows]
            piece[HERE + block] = got_ref[block, rows]
    last = chip == SEG_CHIPS - 1

    @pl.when(last == (core == 1))
    def _():
        edge[...] = own_ref[jnp.where(last, HERE - 1, 0)]

    @pl.when(last != (core == 1))
    def _():
        edge[...] = got_ref[jnp.where(last, HERE - 1, 0)]


def split(where, global_ids, ids, own, got):
    smem = pl.BlockSpec(memory_space=pltpu.SMEM)
    vmem = pl.BlockSpec(memory_space=pltpu.VMEM)
    message = jax.ShapeDtypeStruct((QUARTER + NOTE, HEAD_DIM), jnp.bfloat16)
    shapes = [jax.ShapeDtypeStruct((CHIP, rows, HEAD_DIM), jnp.bfloat16) for rows in PART_ROWS]
    shapes += [message] * 4 + [jax.ShapeDtypeStruct((SLAB, HEAD_DIM), jnp.bfloat16)]
    shapes += [jax.ShapeDtypeStruct((3 * SEG_BLK,), jnp.int32)]
    return pl.pallas_call(
        split_kernel,
        out_shape=shapes,
        in_specs=[smem] * 3 + [vmem] * 2,
        out_specs=[vmem] * 8 + [smem],
        compiler_params=pltpu.CompilerParams(vmem_limit_bytes=16 * 2**20),
    )(where, global_ids, ids, own, got)


def gather_kernel(part, low, high, where_ref, ids_ref, near, side, out_ref, slots):
    chip, core = where_ref[0], where_ref[1]
    d1, d2, d3 = PART_DIMS[part]

    def act(block, count):
        there = block // CHIP
        inside = block - there * CHIP
        apart = there ^ chip
        place = jnp.where(apart & d1 != 0, CHIP, 0)
        place += ((inside // HERE) ^ core) * HERE + lax.rem(inside, HERE)
        go = jnp.logical_and(count >= low, count < high)
        at = jnp.clip(count - low, 0, high - low - 1)

        @pl.when(jnp.logical_and(go, apart & d2 == 0))
        def _():
            out_ref[at] = near[place]

        @pl.when(jnp.logical_and(go, apart & d2 != 0))
        def _():
            out_ref[at] = side[place]

    list_wants(ids_ref, chip ^ d3, part, slots, 0, act)


def gather(part, low, high, where, ids, near, side):
    smem = pl.BlockSpec(memory_space=pltpu.SMEM)
    vmem = pl.BlockSpec(memory_space=pltpu.VMEM)
    return pl.pallas_call(
        functools.partial(gather_kernel, part, low, high),
        out_shape=jax.ShapeDtypeStruct((high - low, PART_ROWS[part], HEAD_DIM), jnp.bfloat16),
        in_specs=[smem, smem, vmem, vmem],
        out_specs=vmem,
        scratch_shapes=[pltpu.SMEM((SEG_BLK,), jnp.int32)],
        compiler_params=pltpu.CompilerParams(vmem_limit_bytes=16 * 2**20),
    )(where, ids, near, side)


OUTER, INNER, OWN, GLOBAL, RANDOM = 0, 1, 2, 2 + HERE, 2 + HERE + GLOB
N_ENTRY = RANDOM + HERE * RAND


def attend_kernel(
    mine, where_ref, rand_ref, slots_ref, q_ref,
    near0, near1, near2, side0, side1, side2, far0, far1, far2, more0, more1, more2,
    quad0, quad1, quad2, quad3, edge,
    out_ref, buf0, buf1, buf2, sems,
):
    chip, core = where_ref[0], where_ref[1]
    nears, sides, fars, mores = (near0, near1, near2), (side0, side1, side2), (far0, far1, far2), (more0, more1, more2)
    bufs, quads = (buf0, buf1, buf2), (quad0, quad1, quad2, quad3)
    half = core if mine else 1 - core
    base = 0 if mine else HERE

    def slot_of(block):
        return ((block // HERE) ^ core) * HERE + lax.rem(block, HERE)

    def fetch(block, entry, sem):
        there = block // CHIP
        slot = slot_of(block - there * CHIP)
        apart = chip ^ there
        for part in range(3):
            d1, d2, d3 = PART_DIMS[part]
            b1 = jnp.where(apart & d1 != 0, CHIP, 0)
            b2 = apart & d2 != 0
            b3 = apart & d3 != 0

            @pl.when(jnp.logical_and(jnp.logical_not(b2), jnp.logical_not(b3)))
            def _():
                pltpu.make_async_copy(nears[part].at[b1 + slot], bufs[part].at[entry], sem).start()

            @pl.when(jnp.logical_and(b2, jnp.logical_not(b3)))
            def _():
                pltpu.make_async_copy(sides[part].at[b1 + slot], bufs[part].at[entry], sem).start()

            cap = CAPS[part]
            place = slots_ref[part * SEG_BLK + block]

            @pl.when(jnp.logical_and(b3, place < cap))
            def _():
                source = fars[part].at[jnp.clip(place, 0, cap - 1)]
                pltpu.make_async_copy(source, bufs[part].at[entry], sem).start()

            @pl.when(jnp.logical_and(b3, place >= cap))
            def _():
                source = mores[part].at[jnp.clip(place - cap, 0, MOST - cap - 1)]
                pltpu.make_async_copy(source, bufs[part].at[entry], sem).start()

    def fetch_rows(source, low, high, entry, sem):
        for part in range(3):
            a, b = max(low, PART_AT[part]), min(high, PART_AT[part] + PART_ROWS[part])
            if a < b:
                to = bufs[part].at[entry, pl.ds(a - PART_AT[part], b - a)]
                pltpu.make_async_copy(source.at[pl.ds(a - low, b - a)], to, sem).start()

    def wait(low, count, sem):
        for part in range(3):
            of = bufs[part].at[pl.ds(low, count)]
            pltpu.make_async_copy(fars[part].at[pl.ds(0, count)], of, sem).wait()

    shared = sems.at[HERE]
    for part in range(3):
        of = nears[part].at[pl.ds(base, HERE)]
        pltpu.make_async_copy(of, bufs[part].at[pl.ds(OWN, HERE)], shared).start()
        inner = (HERE - base) + jnp.where(half == 0, 0, HERE - 1)
        pltpu.make_async_copy(nears[part].at[inner], bufs[part].at[INNER], shared).start()
    at_edge = chip == jnp.where(half == 0, 0, SEG_CHIPS - 1)

    @pl.when(at_edge)
    def _():
        fetch_rows(edge, 0, SLAB, OUTER, shared)

    @pl.when(jnp.logical_not(at_edge))
    def _():
        fetch(chip * CHIP + jnp.where(half == 0, -1, CHIP), OUTER, shared)

    for k in range(4):
        entry = GLOBAL + ((chip & 1) ^ (k & 1))
        row = ((chip >> 1) & 1) ^ (k >> 1)
        for value in range(2):

            @pl.when(row == value)
            def _():
                fetch_rows(quads[k], value * QUARTER, (value + 1) * QUARTER, entry, shared)

    for row in range(HERE):
        for k in range(RAND):
            fetch(rand_ref[row, k], RANDOM + row * RAND + k, sems.at[row])
    wait(0, RANDOM, shared)

    factor = math.log2(math.e) / math.sqrt(HEAD_DIM)
    rest, tail = BLOCK - CUT, 2 * BLOCK
    first = pl.multiple_of(core * (HALF * HEAD_DIM), HALF * HEAD_DIM) if mine else 0
    for row in range(HERE):
        wait(RANDOM, RAND, sems.at[row])
        outer_first = half == 0
        before = OWN + row - 1 if row else jnp.where(outer_first, OUTER, INNER)
        after = OWN + row + 1 if row < HERE - 1 else jnp.where(outer_first, INNER, OUTER)
        at = RANDOM + row * RAND
        entries = [before, OWN + row, after, GLOBAL, GLOBAL + 1, at, at + 1, at + 2]
        keys, values = [], []
        for head in range(HALF - 1):
            keys.append([bufs[head][i, 0:BLOCK] for i in entries])
            values.append([bufs[head][i, BLOCK : 2 * BLOCK] for i in entries])
        keys.append([v for i in entries for v in (buf0[i, tail : tail + CUT], buf2[i, tail : tail + rest])])
        values.append(
            [v for i in entries for v in (buf1[i, tail : tail + CUT], buf2[i, tail + rest : tail + 2 * rest])]
        )
        scores = [
            lax.dot_general(
                q_ref[row * BLOCK : (row + 1) * BLOCK, pl.ds(first + h * HEAD_DIM, HEAD_DIM)],
                jnp.concatenate(keys[h], axis=0),
                (((1,), (1,)), ((), ())),
                preferred_element_type=jnp.float32,
            )
            for h in range(HALF)
        ]
        probs = []
        for h in range(HALF):
            top = jnp.max(scores[h], axis=-1, keepdims=True)
            one = jnp.exp2((scores[h] - top) * factor)
            one = one * (1.0 / jnp.sum(one, axis=-1, keepdims=True))
            probs.append(one.astype(jnp.bfloat16))
        for h in range(HALF):
            mixed = jnp.dot(probs[h], jnp.concatenate(values[h], axis=0), preferred_element_type=jnp.float32)
            out_ref[row * BLOCK : (row + 1) * BLOCK, h * HEAD_DIM : (h + 1) * HEAD_DIM] = mixed.astype(jnp.bfloat16)


def attend(mine, where, rand, slots, q, nears, sides, fars, mores, quads, edge):
    vmem = pl.BlockSpec(memory_space=pltpu.VMEM)
    smem = pl.BlockSpec(memory_space=pltpu.SMEM)
    anywhere = pl.BlockSpec(memory_space=pl.ANY)
    flops = HERE * BLOCK * HALF * (RANDOM + RAND) * BLOCK * HEAD_DIM * 4
    return pl.pallas_call(
        functools.partial(attend_kernel, mine),
        out_shape=jax.ShapeDtypeStruct((HERE * BLOCK, HALF * HEAD_DIM), jnp.bfloat16),
        in_specs=[smem, smem, smem, vmem] + [anywhere] * 17,
        out_specs=vmem,
        scratch_shapes=[pltpu.VMEM((N_ENTRY, rows, HEAD_DIM), jnp.bfloat16) for rows in PART_ROWS]
        + [pltpu.SemaphoreType.DMA((HERE + 1,))],
        compiler_params=pltpu.CompilerParams(vmem_limit_bytes=32 * 2**20),
        cost_estimate=pl.CostEstimate(flops=flops, bytes_accessed=N_ENTRY * SLAB * 256, transcendentals=0),
    )(where, rand, slots, q, *nears, *sides, *fars, *mores, *quads, edge)


def project_kernel(core_ref, own_ref, got_ref, weight_ref, out_ref):
    core = core_ref[0]
    half = HALF * HEAD_DIM
    mine = weight_ref[pl.ds(pl.multiple_of(core * half, half), half), :]
    other = weight_ref[pl.ds(pl.multiple_of((1 - core) * half, half), half), :]
    total = jnp.dot(own_ref[...], mine, preferred_element_type=jnp.float32)
    total += jnp.dot(got_ref[...], other, preferred_element_type=jnp.float32)
    out_ref[...] = total.astype(out_ref.dtype)


def project(core, own, got, weight, tiles=4):
    depth, width = weight.shape
    rows, half = own.shape
    return pl.pallas_call(
        project_kernel,
        grid=(tiles,),
        out_shape=jax.ShapeDtypeStruct((rows, width), jnp.bfloat16),
        in_specs=[
            pl.BlockSpec(memory_space=pltpu.SMEM),
            pl.BlockSpec((rows, half), lambda i: (0, 0)),
            pl.BlockSpec((rows, half), lambda i: (0, 0)),
            pl.BlockSpec((depth, width // tiles), lambda i: (0, i)),
        ],
        out_specs=pl.BlockSpec((rows, width // tiles), lambda i: (0, i)),
        compiler_params=pltpu.CompilerParams(vmem_limit_bytes=24 * 2**20),
    )(core.reshape(1), own, got, weight)


def local(queries, keys_values, rand_blocks, global_ids, out_weight):
    n = lax.axis_size("seq")
    device = lax.axis_index("seq")
    core = device % 2
    chip = (device // 2) % SEG_CHIPS
    where = jnp.stack([chip, core, device // 2])
    rand_mate = swap(rand_blocks, 1)
    own, mate = pack(core, keys_values)
    got = swap(mate, 1)
    ids = jnp.concatenate([rand_blocks.reshape(-1), rand_mate.reshape(-1)])
    *pieces, mine, to_x, to_y, to_xy, border, slots = split(where, global_ids, ids, own, got)

    nears = [
        jnp.concatenate([pieces[part], swap(pieces[part], 2 * PART_DIMS[part][0])], axis=0) for part in range(3)
    ]

    rows = lax.broadcasted_iota(jnp.int32, mine.shape, 0)
    lanes = lax.broadcasted_iota(jnp.int32, mine.shape, 1)
    summed = jnp.logical_or(rows < QUARTER, lanes == FLAG)
    from_x, from_y, from_xy = swap(to_x, 2), swap(to_y, 4), swap(to_xy, 6)
    total = mine + jnp.where(summed, from_x + from_y + from_xy, 0)
    from_z = None
    mask = 8
    while mask < n:
        parts = [swap(total, mask)]
        if from_z is None:
            from_z = parts[0]
        if 2 * mask < n:
            parts += [swap(total, 2 * mask), swap(total, 3 * mask)]
        total = total + jnp.where(summed, sum(parts[1:], parts[0]), 0)
        mask *= 4
    over = total[QUARTER, FLAG] > 0

    total, nears[1] = lax.optimization_barrier((total, nears[1]))
    sides = [swap(nears[part], 2 * PART_DIMS[part][1]) for part in range(3)]
    quads = [total] + [swap(total, mask) for mask in (2, 4, 6)]
    pairs = []
    chips = n // 2
    for c in range(chips):
        if c % SEG_CHIPS == SEG_CHIPS - 1:
            pairs += [(2 * c + k, 2 * ((c + 1) % chips) + k) for k in range(2)]
        if c % SEG_CHIPS == 0:
            pairs += [(2 * c + k, 2 * ((c - 1) % chips) + k) for k in range(2)]
    edge = lax.ppermute(border, "seq", pairs)
    half = HALF * HEAD_DIM
    q_mate = swap(lax.dynamic_slice_in_dim(queries, (1 - core) * half, half, 1), 1)

    asked = [v[QUARTER, :IDS].astype(jnp.int32) for v in (from_z, from_x, from_y)]
    quads, edge, q_mate, asked[0] = lax.optimization_barrier((quads, edge, q_mate, asked[0]))
    fars = [
        swap(gather(part, 0, CAPS[part], where, asked[part], nears[part], sides[part]), 2 * PART_DIMS[part][2])
        for part in range(3)
    ]

    def send_rest(args):
        asked, nears, sides = args
        return [
            swap(gather(part, CAPS[part], MOST, where, asked[part], nears[part], sides[part]), 2 * PART_DIMS[part][2])
            for part in range(3)
        ]

    def send_none(args):
        return [
            jnp.zeros((MOST - cap, rows, HEAD_DIM), jnp.bfloat16) for cap, rows in zip(CAPS, PART_ROWS)
        ]

    mores = lax.cond(over, send_rest, send_none, (asked, nears, sides))

    out_mate = attend(False, where, rand_mate, slots, q_mate, nears, sides, fars, mores, quads, edge)
    out_got = swap(out_mate, 1)
    out_own = attend(True, where, rand_blocks, slots, queries, nears, sides, fars, mores, quads, edge)
    return project(core, out_own, out_got, out_weight)


def solution(mesh):
    placed = (P("seq", None), P(None, "seq", None), P("seq", None), P(), P())
    return jax.shard_map(
        local, mesh=mesh, in_specs=placed, out_specs=P("seq", None), check_vma=False
    )
```

```python
import functools
import math

import jax
import jax.numpy as jnp
from jax import lax
from jax.experimental import pallas as pl
from jax.experimental.pallas import tpu as pltpu
from jax.sharding import PartitionSpec as P

HEADS = 8
HEAD_DIM = 128
BLOCK = 128
RAND = 3
GLOB = 2
SEG_CHIPS = 8
HERE = 3
CHIP = 2 * HERE
HALF = HEADS // 2
SLAB = 2 * HALF * BLOCK

CUT_K, CUT_V = 80, 80
PART_ROWS = (256 + CUT_K, 256 + CUT_V, 256 + 2 * BLOCK - CUT_K - CUT_V)
PART_AT = (0, PART_ROWS[0], PART_ROWS[0] + PART_ROWS[1])
PART_DIMS = ((1, 2, 4), (2, 4, 1), (4, 1, 2))
MOST = 2 * SEG_CHIPS + 2 + GLOB
CAPS = (14, 14, 14)
SEG_BLK = SEG_CHIPS * CHIP
IDS = CHIP * RAND
FLAG = IDS
QUARTER = SLAB // 2
NOTE = 16


def swap(value, mask):
    n = lax.axis_size("seq")
    return lax.ppermute(value, "seq", [(i, i ^ mask) for i in range(n)])


def pack_kernel(core_ref, kv_ref, own_ref, mate_ref):
    core = core_ref[0]
    for which, kv_out in ((1 - core, mate_ref), (core, own_ref)):
        first = pl.multiple_of(which * (HALF * HEAD_DIM), HEAD_DIM)

        def unit(pair, block, head, low, high):
            cols = pl.ds(first + head * HEAD_DIM, HEAD_DIM)
            return kv_ref[pair, block * BLOCK + low : block * BLOCK + high, cols]

        for block in range(HERE):
            for part in range(3):
                at = PART_AT[part]
                kv_out[block, at : at + BLOCK] = unit(0, block, part, 0, BLOCK)
                kv_out[block, at + BLOCK : at + 2 * BLOCK] = unit(1, block, part, 0, BLOCK)
            last = HALF - 1
            a, b, c = (at + 2 * BLOCK for at in PART_AT)
            kv_out[block, a : a + CUT_K] = unit(0, block, last, 0, CUT_K)
            kv_out[block, b : b + CUT_V] = unit(1, block, last, 0, CUT_V)
            mid = c + BLOCK - CUT_K
            kv_out[block, c:mid] = unit(0, block, last, CUT_K, BLOCK)
            kv_out[block, mid : mid + BLOCK - CUT_V] = unit(1, block, last, CUT_V, BLOCK)


def pack(core, keys_values):
    slab = jax.ShapeDtypeStruct((HERE, SLAB, HEAD_DIM), jnp.bfloat16)
    vmem = pl.BlockSpec(memory_space=pltpu.VMEM)
    return pl.pallas_call(
        pack_kernel,
        out_shape=(slab, slab),
        in_specs=[pl.BlockSpec(memory_space=pltpu.SMEM), vmem],
        out_specs=(vmem,) * 2,
        compiler_params=pltpu.CompilerParams(vmem_limit_bytes=4 * 2**20),
    )(core.reshape(1), keys_values)


def in_segment(where, block):
    inside = block - (where[2] - where[0]) * CHIP
    return jnp.where(jnp.logical_and(inside >= 0, inside < SEG_BLK), inside, -1)


def list_wants(where, ids, globs, chip, part, slots, base, act):
    dim = PART_DIMS[part][2]

    @pl.loop(0, SEG_BLK)
    def _(k):
        slots[base + k] = -1

    def add(block, count):
        place = base + block
        new = jnp.logical_and(((block // CHIP) ^ chip) & dim != 0, slots[place] < 0)

        @pl.when(new)
        def _():
            slots[place] = count
            if act is not None:
                act(block, count)

        return count + new.astype(jnp.int32)

    count = lax.fori_loop(0, IDS, lambda k, c: add(ids[k], c), jnp.int32(0))
    low, high = chip * CHIP - 1, chip * CHIP + CHIP
    count = add(jnp.where(chip == 0, chip * CHIP, low), count)
    count = add(jnp.where(chip == SEG_CHIPS - 1, chip * CHIP, high), count)
    for g in range(GLOB):
        block = in_segment(where, globs[g])
        count = add(jnp.where(block < 0, chip * CHIP, block), count)
    return count


def split_kernel(where_ref, glob_ref, ids_ref, own_ref, got_ref, to_x, to_y, to_z, to_xy, mine, edge):
    chip, core, chip_all = where_ref[0], where_ref[1], where_ref[2]
    lane = lax.broadcasted_iota(jnp.int32, (NOTE, HEAD_DIM), 1)
    wanted = lane == jnp.where(chip == 0, -1, chip * CHIP - 1)
    wanted = jnp.logical_or(wanted, lane == jnp.where(chip == SEG_CHIPS - 1, -1, chip * CHIP + CHIP))
    for g in range(GLOB):
        wanted = jnp.logical_or(wanted, lane == in_segment(where_ref, glob_ref[g]))
    row = jnp.zeros((NOTE, HEAD_DIM), jnp.int32)
    for k in range(IDS):
        wanted = jnp.logical_or(wanted, lane == ids_ref[k])
        row = jnp.where(lane == k, ids_ref[k], row)
    apart = jnp.zeros((NOTE, HEAD_DIM), jnp.int32)
    for k in range(1, SEG_CHIPS):
        apart += (lane >= k * CHIP).astype(jnp.int32)
    apart = apart ^ chip
    over = jnp.zeros((NOTE, 1), jnp.float32)
    for part in range(3):
        far = jnp.logical_and(wanted, apart & PART_DIMS[part][2] != 0)
        count = jnp.sum(jnp.where(far, 1.0, 0.0), axis=1, keepdims=True)
        over = jnp.maximum(over, jnp.where(count > CAPS[part], 1.0, 0.0))
    note = jnp.where(lane == FLAG, over, row.astype(jnp.float32)).astype(jnp.bfloat16)

    def write(out, at, k):
        x, y = chip & 1, (chip >> 1) & 1
        block = glob_ref[x ^ (k & 1)]
        half = y ^ (k >> 1)
        owner = block // CHIP
        inside = block - owner * CHIP
        place = lax.rem(inside, HERE)
        rows = pl.ds(pl.multiple_of(half * QUARTER, QUARTER), QUARTER)
        here = owner == chip_all
        mate = (inside // HERE) != core

        @pl.when(jnp.logical_and(here, jnp.logical_not(mate)))
        def _():
            out[at : at + QUARTER] = own_ref[place, rows]

        @pl.when(jnp.logical_and(here, mate))
        def _():
            out[at : at + QUARTER] = got_ref[place, rows]

        @pl.when(jnp.logical_not(here))
        def _():
            out[at : at + QUARTER] = jnp.zeros((QUARTER, HEAD_DIM), jnp.bfloat16)

        out[at + QUARTER : at + QUARTER + NOTE] = note

    for part, out in enumerate((to_x, to_y, to_z)):
        size = PART_ROWS[part]
        for block in range(HERE):
            out[block * size : (block + 1) * size] = own_ref[block, PART_AT[part] : PART_AT[part] + size]
            low = (HERE + block) * size
            out[low : low + size] = got_ref[block, PART_AT[part] : PART_AT[part] + size]
    write(to_x, CHIP * PART_ROWS[0], 1)
    write(to_y, CHIP * PART_ROWS[1], 2)
    to_z[CHIP * PART_ROWS[2] : CHIP * PART_ROWS[2] + NOTE] = note
    write(to_xy, 0, 3)
    write(mine, 0, 0)
    last = chip == SEG_CHIPS - 1

    @pl.when(last == (core == 1))
    def _():
        edge[...] = own_ref[jnp.where(last, HERE - 1, 0)]

    @pl.when(last != (core == 1))
    def _():
        edge[...] = got_ref[jnp.where(last, HERE - 1, 0)]


def flat(rows):
    return jax.ShapeDtypeStruct((rows, HEAD_DIM), jnp.bfloat16)


def split(where, global_ids, ids, own, got):
    smem = pl.BlockSpec(memory_space=pltpu.SMEM)
    vmem = pl.BlockSpec(memory_space=pltpu.VMEM)
    sizes = [CHIP * rows for rows in PART_ROWS]
    return pl.pallas_call(
        split_kernel,
        out_shape=[
            flat(sizes[0] + QUARTER + NOTE), flat(sizes[1] + QUARTER + NOTE), flat(sizes[2] + NOTE),
            flat(QUARTER + NOTE), flat(QUARTER + NOTE), flat(SLAB),
        ],
        in_specs=[smem] * 3 + [vmem] * 2,
        out_specs=[vmem] * 6,
        compiler_params=pltpu.CompilerParams(vmem_limit_bytes=6 * 2**20),
    )(where, global_ids, ids, own, got)


def join_kernel(sent_x, sent_y, sent_z, mine, from_x, from_y, from_z, from_xy, near0, near1, near2):
    for part, (sent, got, near) in enumerate(
        ((sent_x, from_x, near0), (sent_y, from_y, near1), (sent_z, from_z, near2))
    ):
        size = CHIP * PART_ROWS[part]
        near[0:size] = sent[0:size]
        near[size : 2 * size] = got[0:size]
    x, y = CHIP * PART_ROWS[0], CHIP * PART_ROWS[1]
    total = mine[...] + (from_x[x : x + QUARTER + NOTE] + from_y[y : y + QUARTER + NOTE] + from_xy[...])
    near1[2 * y : 2 * y + QUARTER + NOTE] = total


def join(sent, mine, got):
    vmem = pl.BlockSpec(memory_space=pltpu.VMEM)
    return pl.pallas_call(
        join_kernel,
        out_shape=[flat(2 * CHIP * rows + (QUARTER + NOTE if part == 1 else 0)) for part, rows in enumerate(PART_ROWS)],
        in_specs=[vmem] * 8,
        out_specs=[vmem] * 3,
        compiler_params=pltpu.CompilerParams(vmem_limit_bytes=9 * 2**20),
    )(*sent, mine, *got)


def plan_kernel(where_ref, ids_ref, glob_ref, slots):
    for part in range(3):
        list_wants(where_ref, ids_ref, glob_ref, where_ref[0], part, slots, part * SEG_BLK, None)


def plan(where, ids, global_ids):
    smem = pl.BlockSpec(memory_space=pltpu.SMEM)
    return pl.pallas_call(
        plan_kernel,
        out_shape=jax.ShapeDtypeStruct((3 * SEG_BLK,), jnp.int32),
        in_specs=[smem] * 3,
        out_specs=smem,
        compiler_params=pltpu.CompilerParams(vmem_limit_bytes=2**20),
    )(where, ids, global_ids)


def gather_kernel(part, low, high, where_ref, ids_ref, glob_ref, near, side, out_ref, slots):
    chip, core = where_ref[0], where_ref[1]
    d1, d2, d3 = PART_DIMS[part]
    size = PART_ROWS[part]

    def act(block, count):
        there = block // CHIP
        inside = block - there * CHIP
        apart = there ^ chip
        place = jnp.where(apart & d1 != 0, CHIP, 0)
        place += ((inside // HERE) ^ core) * HERE + lax.rem(inside, HERE)
        go = jnp.logical_and(count >= low, count < high)
        at = jnp.clip(count - low, 0, high - low - 1)
        target = pl.ds(pl.multiple_of(at * size, 16), size)
        source = pl.ds(pl.multiple_of(place * size, 16), size)

        @pl.when(jnp.logical_and(go, apart & d2 == 0))
        def _():
            out_ref[target] = near[source]

        @pl.when(jnp.logical_and(go, apart & d2 != 0))
        def _():
            out_ref[target] = side[source]

    list_wants(where_ref, ids_ref, glob_ref, chip ^ d3, part, slots, 0, act)


def gather(part, low, high, where, ids, global_ids, near, side):
    smem = pl.BlockSpec(memory_space=pltpu.SMEM)
    vmem = pl.BlockSpec(memory_space=pltpu.VMEM)
    return pl.pallas_call(
        functools.partial(gather_kernel, part, low, high),
        out_shape=flat((high - low) * PART_ROWS[part]),
        in_specs=[smem] * 3 + [vmem] * 2,
        out_specs=vmem,
        scratch_shapes=[pltpu.SMEM((SEG_BLK,), jnp.int32)],
        compiler_params=pltpu.CompilerParams(vmem_limit_bytes=5 * 2**20),
    )(where, ids, global_ids, near, side)


def flag_kernel(here, there, over, notes, sem):
    rows = pl.ds(QUARTER, NOTE)
    copies = [pltpu.make_async_copy(v.at[rows], notes.at[k], sem.at[k]) for k, v in enumerate((here, there))]
    for one in copies:
        one.start()
    for one in copies:
        one.wait()
    flags = notes[...].astype(jnp.float32)
    lane = lax.broadcasted_iota(jnp.int32, flags.shape, 2)
    over[0] = (jnp.max(jnp.where(lane == FLAG, flags, 0.0)) > 0).astype(jnp.int32)


def flag(here, there):
    anywhere = pl.BlockSpec(memory_space=pl.ANY)
    return pl.pallas_call(
        flag_kernel,
        out_shape=jax.ShapeDtypeStruct((1,), jnp.int32),
        in_specs=[anywhere] * 2,
        out_specs=pl.BlockSpec(memory_space=pltpu.SMEM),
        scratch_shapes=[pltpu.VMEM((2, NOTE, HEAD_DIM), jnp.bfloat16), pltpu.SemaphoreType.DMA((2,))],
        compiler_params=pltpu.CompilerParams(vmem_limit_bytes=2**20),
    )(here, there)


def nothing(shapes):
    return pl.pallas_call(
        lambda *refs: None,
        out_shape=shapes,
        out_specs=[pl.BlockSpec(memory_space=pl.ANY)] * len(shapes),
        compiler_params=pltpu.CompilerParams(vmem_limit_bytes=2**20),
    )()


OUTER, INNER, OWN, GLOBAL, RANDOM = 0, 1, 2, 2 + HERE, 2 + HERE + GLOB
N_ENTRY = RANDOM + HERE * RAND


def attend_kernel(
    mine, where_ref, rand_ref, glob_ref, slots_ref, q_ref,
    near0, near1, near2, side0, side1, side2, far0, far1, far2, more0, more1, more2,
    quad0, quad1, quad2, edge,
    out_ref, buf0, buf1, buf2, q_buf, sems,
):
    chip, core = where_ref[0], where_ref[1]
    nears, sides, fars, mores = (near0, near1, near2), (side0, side1, side2), (far0, far1, far2), (more0, more1, more2)
    bufs = (buf0, buf1, buf2)
    behind = QUARTER + NOTE
    quads = (quad0, quad1, quad2.at[pl.ds(0, behind)], quad2.at[pl.ds(behind, behind)])
    half = core if mine else 1 - core
    base = 0 if mine else HERE

    def slot_of(block):
        return ((block // HERE) ^ core) * HERE + lax.rem(block, HERE)

    def blocks(ref, part, place, count=1):
        size = PART_ROWS[part]
        return ref.at[pl.ds(pl.multiple_of(place * size, 16), count * size)]

    def copy(ref, part, place, entry, sem, count=1):
        source, target = blocks(ref, part, place, count), blocks(bufs[part], part, entry, count)
        pltpu.make_async_copy(source, target, sem).start()

    def fetch(block, entry, sem):
        there = block // CHIP
        slot = slot_of(block - there * CHIP)
        apart = chip ^ there
        for part in range(3):
            d1, d2, d3 = PART_DIMS[part]
            b1 = jnp.where(apart & d1 != 0, CHIP, 0)
            b2 = apart & d2 != 0
            b3 = apart & d3 != 0

            @pl.when(jnp.logical_and(jnp.logical_not(b2), jnp.logical_not(b3)))
            def _():
                copy(nears[part], part, b1 + slot, entry, sem)

            @pl.when(jnp.logical_and(b2, jnp.logical_not(b3)))
            def _():
                copy(sides[part], part, b1 + slot, entry, sem)

            cap = CAPS[part]
            place = slots_ref[part * SEG_BLK + block]

            @pl.when(jnp.logical_and(b3, place < cap))
            def _():
                copy(fars[part], part, jnp.clip(place, 0, cap - 1), entry, sem)

            @pl.when(jnp.logical_and(b3, place >= cap))
            def _():
                copy(mores[part], part, jnp.clip(place - cap, 0, MOST - cap - 1), entry, sem)

    def fetch_rows(source, low, high, entry, sem):
        for part in range(3):
            a, b = max(low, PART_AT[part]), min(high, PART_AT[part] + PART_ROWS[part])
            if a < b:
                at = pl.multiple_of(entry * PART_ROWS[part], 16) + a - PART_AT[part]
                to = bufs[part].at[pl.ds(pl.multiple_of(at, 16), b - a)]
                pltpu.make_async_copy(source.at[pl.ds(a - low, b - a)], to, sem).start()

    def wait(low, count, sem):
        for part in range(3):
            of = blocks(bufs[part], part, low, count)
            pltpu.make_async_copy(blocks(nears[part], part, 0, count), of, sem).wait()

    shared = sems.at[HERE]
    width = HALF * HEAD_DIM
    q_cols = pl.ds(pl.multiple_of(core * width, width), width) if mine else pl.ds(0, width)
    q_copy = pltpu.make_async_copy(q_ref.at[:, q_cols], q_buf, sems.at[HERE + 1])
    q_copy.start()
    for part in range(3):
        copy(nears[part], part, base, OWN, shared, HERE)
        copy(nears[part], part, (HERE - base) + jnp.where(half == 0, 0, HERE - 1), INNER, shared)
    at_edge = chip == jnp.where(half == 0, 0, SEG_CHIPS - 1)

    @pl.when(at_edge)
    def _():
        fetch_rows(edge, 0, SLAB, OUTER, shared)

    @pl.when(jnp.logical_not(at_edge))
    def _():
        fetch(chip * CHIP + jnp.where(half == 0, -1, CHIP), OUTER, shared)

    for g in range(GLOB):
        block = in_segment(where_ref, glob_ref[g])

        @pl.when(block >= 0)
        def _():
            fetch(jnp.maximum(block, 0), GLOBAL + g, shared)

    for k in range(4):
        g = (chip & 1) ^ (k & 1)
        entry = GLOBAL + g
        row = ((chip >> 1) & 1) ^ (k >> 1)
        outside = in_segment(where_ref, glob_ref[g]) < 0
        for value in range(2):

            @pl.when(jnp.logical_and(outside, row == value))
            def _():
                fetch_rows(quads[k], value * QUARTER, (value + 1) * QUARTER, entry, shared)

    for row in range(HERE):
        for k in range(RAND):
            fetch(rand_ref[row, k], RANDOM + row * RAND + k, sems.at[row])
    q_copy.wait()
    wait(0, RANDOM, shared)

    factor = math.log2(math.e) / math.sqrt(HEAD_DIM)
    tail, mid = 2 * BLOCK, 3 * BLOCK - CUT_K
    for row in range(HERE):
        wait(RANDOM, RAND, sems.at[row])
        outer_first = half == 0
        before = OWN + row - 1 if row else jnp.where(outer_first, OUTER, INNER)
        after = OWN + row + 1 if row < HERE - 1 else jnp.where(outer_first, INNER, OUTER)
        at = RANDOM + row * RAND
        entries = [before, OWN + row, after, GLOBAL, GLOBAL + 1, at, at + 1, at + 2]
        keys, values = [], []

        def rows(part, entry, low, high):
            return bufs[part][pl.ds(pl.multiple_of(entry * PART_ROWS[part] + low, 16), high - low)]

        for head in range(HALF - 1):
            keys.append([rows(head, i, 0, BLOCK) for i in entries])
            values.append([rows(head, i, BLOCK, 2 * BLOCK) for i in entries])
        keys.append([v for i in entries for v in (rows(0, i, tail, tail + CUT_K), rows(2, i, tail, mid))])
        values.append(
            [v for i in entries for v in (rows(1, i, tail, tail + CUT_V), rows(2, i, mid, PART_ROWS[2]))]
        )
        scores = [
            lax.dot_general(
                q_buf[row * BLOCK : (row + 1) * BLOCK, h * HEAD_DIM : (h + 1) * HEAD_DIM],
                jnp.concatenate(keys[h], axis=0),
                (((1,), (1,)), ((), ())),
                preferred_element_type=jnp.float32,
            )
            for h in range(HALF)
        ]
        probs = []
        for h in range(HALF):
            top = jnp.max(scores[h], axis=-1, keepdims=True)
            one = jnp.exp2((scores[h] - top) * factor)
            one = one * (1.0 / jnp.sum(one, axis=-1, keepdims=True))
            probs.append(one.astype(jnp.bfloat16))
        for h in range(HALF):
            mixed = jnp.dot(probs[h], jnp.concatenate(values[h], axis=0), preferred_element_type=jnp.float32)
            out_ref[row * BLOCK : (row + 1) * BLOCK, h * HEAD_DIM : (h + 1) * HEAD_DIM] = mixed.astype(jnp.bfloat16)


def attend(mine, where, rand, global_ids, slots, q, nears, sides, fars, mores, quads, edge):
    vmem = pl.BlockSpec(memory_space=pltpu.VMEM)
    smem = pl.BlockSpec(memory_space=pltpu.SMEM)
    hbm = pl.BlockSpec(memory_space=pltpu.HBM)
    flops = HERE * BLOCK * HALF * (RANDOM + RAND) * BLOCK * HEAD_DIM * 4
    return pl.pallas_call(
        functools.partial(attend_kernel, mine),
        out_shape=jax.ShapeDtypeStruct((HERE * BLOCK, HALF * HEAD_DIM), jnp.bfloat16),
        in_specs=[smem] * 4 + [hbm] * 17,
        out_specs=vmem,
        scratch_shapes=[pltpu.VMEM((N_ENTRY * rows, HEAD_DIM), jnp.bfloat16) for rows in PART_ROWS]
        + [pltpu.VMEM((HERE * BLOCK, HALF * HEAD_DIM), jnp.bfloat16), pltpu.SemaphoreType.DMA((HERE + 2,))],
        compiler_params=pltpu.CompilerParams(vmem_limit_bytes=48 * 2**20),
        cost_estimate=pl.CostEstimate(flops=flops, bytes_accessed=N_ENTRY * SLAB * 256, transcendentals=0),
    )(where, rand, global_ids, slots, q, *nears, *sides, *fars, *mores, *quads, edge)


def project_kernel(tiles, core_ref, own_ref, got_ref, weight_ref, out_ref, tile_ref, sems):
    core = core_ref[0]
    half = HALF * HEAD_DIM
    width = out_ref.shape[1] // tiles
    mine = pl.ds(pl.multiple_of(core * half, half), half)
    other = pl.ds(pl.multiple_of((1 - core) * half, half), half)
    copies = []
    for k in range(tiles):
        cols = pl.ds(k * width, width)
        total = jnp.dot(own_ref[...], weight_ref[mine, cols], preferred_element_type=jnp.float32)
        total += jnp.dot(got_ref[...], weight_ref[other, cols], preferred_element_type=jnp.float32)
        tile_ref[k] = total.astype(out_ref.dtype)
        copies.append(pltpu.make_async_copy(tile_ref.at[k], out_ref.at[:, cols], sems.at[k]))
        copies[k].start()
    for one in copies:
        one.wait()


def project(core, own, got, weight, tiles=4):
    width = weight.shape[1]
    rows = own.shape[0]
    vmem = pl.BlockSpec(memory_space=pltpu.VMEM)
    return pl.pallas_call(
        functools.partial(project_kernel, tiles),
        out_shape=jax.ShapeDtypeStruct((rows, width), jnp.bfloat16),
        in_specs=[pl.BlockSpec(memory_space=pltpu.SMEM), vmem, vmem, vmem],
        out_specs=pl.BlockSpec(memory_space=pl.ANY),
        scratch_shapes=[pltpu.VMEM((tiles, rows, width // tiles), jnp.bfloat16), pltpu.SemaphoreType.DMA((tiles,))],
        compiler_params=pltpu.CompilerParams(vmem_limit_bytes=14 * 2**20),
    )(core.reshape(1), own, got, weight)


def local(queries, keys_values, rand_blocks, global_ids, out_weight):
    n = lax.axis_size("seq")
    device = lax.axis_index("seq")
    core = device % 2
    chip = (device // 2) % SEG_CHIPS
    where = jnp.stack([chip, core, device // 2])
    rand_mate = swap(rand_blocks, 1)
    own, mate = pack(core, keys_values)
    got = swap(mate, 1)
    ids = jnp.concatenate([rand_blocks.reshape(-1), rand_mate.reshape(-1)])
    *sent, to_xy, mine, border = split(where, global_ids, ids, own, got)

    pairs = []
    chips = n // 2
    for c in range(chips):
        if c % SEG_CHIPS == SEG_CHIPS - 1:
            pairs += [(2 * c + k, 2 * ((c + 1) % chips) + k) for k in range(2)]
        if c % SEG_CHIPS == 0:
            pairs += [(2 * c + k, 2 * ((c - 1) % chips) + k) for k in range(2)]
    edge = lax.ppermute(border, "seq", pairs)
    half = HALF * HEAD_DIM
    q_mate = swap(lax.dynamic_slice_in_dim(queries, (1 - core) * half, half, 1), 1)
    got = [swap(v, 2 * PART_DIMS[part][0]) for part, v in enumerate(sent)] + [swap(to_xy, 6)]
    got, q_mate = lax.optimization_barrier((got, q_mate))
    nears = join(sent, mine, got)
    asked = [got[k][CHIP * PART_ROWS[k] + more, :IDS].astype(jnp.int32) for k, more in ((2, 0), (0, QUARTER), (1, QUARTER))]

    sides = [swap(nears[part], 2 * PART_DIMS[part][1]) for part in range(3)]
    slots = plan(where, ids, global_ids)
    slots, asked[2] = lax.optimization_barrier((slots, asked[2]))
    here = nears[1][2 * CHIP * PART_ROWS[1] :] + sides[1][2 * CHIP * PART_ROWS[1] :]
    if n == 4 * SEG_CHIPS:
        total = swap(here, 16)
    else:
        total = here
        mask = 16
        while mask < n:
            total = total + swap(total, mask)
            mask *= 2

    edge, total, asked[0] = lax.optimization_barrier((edge, total, asked[0]))
    from_x = swap(total, 2)
    sides[0], sides[2] = lax.optimization_barrier((sides[0], sides[2]))
    fars = [
        swap(
            gather(part, 0, CAPS[part], where, asked[part], global_ids, nears[part], sides[part]),
            2 * PART_DIMS[part][2],
        )
        for part in range(3)
    ]
    from_y = swap(jnp.concatenate([total, from_x], axis=0), 4)
    over = flag(here, total)[0] > 0
    over, fars[1], from_x = lax.optimization_barrier((over, fars[1], from_x))
    quads = [total, from_x, from_y]

    def send_rest(args):
        asked, nears, sides = args
        return [
            swap(gather(part, CAPS[part], MOST, where, asked[part], global_ids, nears[part], sides[part]), 2 * PART_DIMS[part][2])
            for part in range(3)
        ]

    def send_none(args):
        return list(nothing([flat((MOST - cap) * rows) for cap, rows in zip(CAPS, PART_ROWS)]))

    mores = lax.cond(over, send_rest, send_none, (asked, nears, sides))

    out_mate = attend(False, where, rand_mate, global_ids, slots, q_mate, nears, sides, fars, mores, quads, edge)
    out_got = swap(out_mate, 1)
    out_own = attend(True, where, rand_blocks, global_ids, slots, queries, nears, sides, fars, mores, quads, edge)
    return project(core, out_own, out_got, out_weight)


def solution(mesh):
    placed = (P("seq", None), P(None, "seq", None), P("seq", None), P(), P())
    return jax.shard_map(
        local, mesh=mesh, in_specs=placed, out_specs=P("seq", None), check_vma=False
    )
```

```python
import functools
import math

import jax
import jax.numpy as jnp
from jax import lax
from jax.experimental import pallas as pl
from jax.experimental.pallas import tpu as pltpu
from jax.sharding import PartitionSpec as P

HEADS = 8
HEAD_DIM = 128
BLOCK = 128
RAND = 3
GLOB = 2
SEG_CHIPS = 8
HERE = 3
CHIP = 2 * HERE
HALF = HEADS // 2
SLAB = 2 * HALF * BLOCK

CUT_K, CUT_V = 80, 80
PART_ROWS = (256 + CUT_K, 256 + CUT_V, 256 + 2 * BLOCK - CUT_K - CUT_V)
PART_AT = (0, PART_ROWS[0], PART_ROWS[0] + PART_ROWS[1])
PART_DIMS = ((1, 2, 4), (2, 4, 1), (4, 1, 2))
MOST = 2 * SEG_CHIPS + 2 + GLOB
CAPS = (14, 14, 14)
SEG_BLK = SEG_CHIPS * CHIP
IDS = CHIP * RAND
FLAG = IDS
QUARTER = SLAB // 2
NOTE = 16


def swap(value, mask):
    n = lax.axis_size("seq")
    return lax.ppermute(value, "seq", [(i, i ^ mask) for i in range(n)])


def pack_kernel(core_ref, kv_ref, own_ref, mate_ref):
    core = core_ref[0]
    for which, kv_out in ((1 - core, mate_ref), (core, own_ref)):
        first = pl.multiple_of(which * (HALF * HEAD_DIM), HEAD_DIM)

        def unit(pair, block, head, low, high):
            cols = pl.ds(first + head * HEAD_DIM, HEAD_DIM)
            return kv_ref[pair, block * BLOCK + low : block * BLOCK + high, cols]

        for block in range(HERE):
            for part in range(3):
                at = PART_AT[part]
                kv_out[block, at : at + BLOCK] = unit(0, block, part, 0, BLOCK)
                kv_out[block, at + BLOCK : at + 2 * BLOCK] = unit(1, block, part, 0, BLOCK)
            last = HALF - 1
            a, b, c = (at + 2 * BLOCK for at in PART_AT)
            kv_out[block, a : a + CUT_K] = unit(0, block, last, 0, CUT_K)
            kv_out[block, b : b + CUT_V] = unit(1, block, last, 0, CUT_V)
            mid = c + BLOCK - CUT_K
            kv_out[block, c:mid] = unit(0, block, last, CUT_K, BLOCK)
            kv_out[block, mid : mid + BLOCK - CUT_V] = unit(1, block, last, CUT_V, BLOCK)


def pack(core, keys_values):
    slab = jax.ShapeDtypeStruct((HERE, SLAB, HEAD_DIM), jnp.bfloat16)
    vmem = pl.BlockSpec(memory_space=pltpu.VMEM)
    return pl.pallas_call(
        pack_kernel,
        out_shape=(slab, slab),
        in_specs=[pl.BlockSpec(memory_space=pltpu.SMEM), vmem],
        out_specs=(vmem,) * 2,
        compiler_params=pltpu.CompilerParams(vmem_limit_bytes=4 * 2**20),
    )(core.reshape(1), keys_values)


def in_segment(where, block):
    inside = block - (where[2] - where[0]) * CHIP
    return jnp.where(jnp.logical_and(inside >= 0, inside < SEG_BLK), inside, -1)


def list_wants(where, ids, globs, chip, part, slots, base, act):
    dim = PART_DIMS[part][2]

    @pl.loop(0, SEG_BLK)
    def _(k):
        slots[base + k] = -1

    def add(block, count):
        place = base + block
        new = jnp.logical_and(((block // CHIP) ^ chip) & dim != 0, slots[place] < 0)

        @pl.when(new)
        def _():
            slots[place] = count
            if act is not None:
                act(block, count)

        return count + new.astype(jnp.int32)

    count = lax.fori_loop(0, IDS, lambda k, c: add(ids[k], c), jnp.int32(0))
    low, high = chip * CHIP - 1, chip * CHIP + CHIP
    count = add(jnp.where(chip == 0, chip * CHIP, low), count)
    count = add(jnp.where(chip == SEG_CHIPS - 1, chip * CHIP, high), count)
    for g in range(GLOB):
        block = in_segment(where, globs[g])
        count = add(jnp.where(block < 0, chip * CHIP, block), count)
    return count


def split_kernel(where_ref, glob_ref, ids_ref, own_ref, got_ref, to_x, to_y, to_z, to_xy, mine, edge):
    chip, core, chip_all = where_ref[0], where_ref[1], where_ref[2]
    lane = lax.broadcasted_iota(jnp.int32, (NOTE, HEAD_DIM), 1)
    wanted = lane == jnp.where(chip == 0, -1, chip * CHIP - 1)
    wanted = jnp.logical_or(wanted, lane == jnp.where(chip == SEG_CHIPS - 1, -1, chip * CHIP + CHIP))
    for g in range(GLOB):
        wanted = jnp.logical_or(wanted, lane == in_segment(where_ref, glob_ref[g]))
    row = jnp.zeros((NOTE, HEAD_DIM), jnp.int32)
    for k in range(IDS):
        wanted = jnp.logical_or(wanted, lane == ids_ref[k])
        row = jnp.where(lane == k, ids_ref[k], row)
    apart = jnp.zeros((NOTE, HEAD_DIM), jnp.int32)
    for k in range(1, SEG_CHIPS):
        apart += (lane >= k * CHIP).astype(jnp.int32)
    apart = apart ^ chip
    over = jnp.zeros((NOTE, 1), jnp.float32)
    for part in range(3):
        far = jnp.logical_and(wanted, apart & PART_DIMS[part][2] != 0)
        count = jnp.sum(jnp.where(far, 1.0, 0.0), axis=1, keepdims=True)
        over = jnp.maximum(over, jnp.where(count > CAPS[part], 1.0, 0.0))
    note = jnp.where(lane == FLAG, over, row.astype(jnp.float32)).astype(jnp.bfloat16)

    def write(out, at, k):
        x, y = chip & 1, (chip >> 1) & 1
        block = glob_ref[x ^ (k & 1)]
        half = y ^ (k >> 1)
        owner = block // CHIP
        inside = block - owner * CHIP
        place = lax.rem(inside, HERE)
        rows = pl.ds(pl.multiple_of(half * QUARTER, QUARTER), QUARTER)
        here = owner == chip_all
        mate = (inside // HERE) != core

        @pl.when(jnp.logical_and(here, jnp.logical_not(mate)))
        def _():
            out[at : at + QUARTER] = own_ref[place, rows]

        @pl.when(jnp.logical_and(here, mate))
        def _():
            out[at : at + QUARTER] = got_ref[place, rows]

        @pl.when(jnp.logical_not(here))
        def _():
            out[at : at + QUARTER] = jnp.zeros((QUARTER, HEAD_DIM), jnp.bfloat16)

        out[at + QUARTER : at + QUARTER + NOTE] = note

    for part, out in enumerate((to_x, to_y, to_z)):
        size = PART_ROWS[part]
        for block in range(HERE):
            out[block * size : (block + 1) * size] = own_ref[block, PART_AT[part] : PART_AT[part] + size]
            low = (HERE + block) * size
            out[low : low + size] = got_ref[block, PART_AT[part] : PART_AT[part] + size]
    write(to_x, CHIP * PART_ROWS[0], 1)
    write(to_y, CHIP * PART_ROWS[1], 2)
    to_z[CHIP * PART_ROWS[2] : CHIP * PART_ROWS[2] + NOTE] = note
    write(to_xy, 0, 3)
    write(mine, 0, 0)
    last = chip == SEG_CHIPS - 1

    @pl.when(last == (core == 1))
    def _():
        edge[...] = own_ref[jnp.where(last, HERE - 1, 0)]

    @pl.when(last != (core == 1))
    def _():
        edge[...] = got_ref[jnp.where(last, HERE - 1, 0)]


def flat(rows):
    return jax.ShapeDtypeStruct((rows, HEAD_DIM), jnp.bfloat16)


def split(where, global_ids, ids, own, got):
    smem = pl.BlockSpec(memory_space=pltpu.SMEM)
    vmem = pl.BlockSpec(memory_space=pltpu.VMEM)
    sizes = [CHIP * rows for rows in PART_ROWS]
    return pl.pallas_call(
        split_kernel,
        out_shape=[
            flat(sizes[0] + QUARTER + NOTE), flat(sizes[1] + QUARTER + NOTE), flat(sizes[2] + NOTE),
            flat(QUARTER + NOTE), flat(QUARTER + NOTE), flat(SLAB),
        ],
        in_specs=[smem] * 3 + [vmem] * 2,
        out_specs=[vmem] * 6,
        compiler_params=pltpu.CompilerParams(vmem_limit_bytes=6 * 2**20),
    )(where, global_ids, ids, own, got)


def join_kernel(sent_x, sent_y, sent_z, mine, from_x, from_y, from_z, from_xy, near0, near1, near2):
    for part, (sent, got, near) in enumerate(
        ((sent_x, from_x, near0), (sent_y, from_y, near1), (sent_z, from_z, near2))
    ):
        size = CHIP * PART_ROWS[part]
        near[0:size] = sent[0:size]
        near[size : 2 * size] = got[0:size]
    x, y = CHIP * PART_ROWS[0], CHIP * PART_ROWS[1]
    total = mine[...] + (from_x[x : x + QUARTER + NOTE] + from_y[y : y + QUARTER + NOTE] + from_xy[...])
    near1[2 * y : 2 * y + QUARTER + NOTE] = total


def join(sent, mine, got):
    vmem = pl.BlockSpec(memory_space=pltpu.VMEM)
    return pl.pallas_call(
        join_kernel,
        out_shape=[flat(2 * CHIP * rows + (QUARTER + NOTE if part == 1 else 0)) for part, rows in enumerate(PART_ROWS)],
        in_specs=[vmem] * 8,
        out_specs=[vmem] * 3,
        compiler_params=pltpu.CompilerParams(vmem_limit_bytes=9 * 2**20),
    )(*sent, mine, *got)


def plan_kernel(where_ref, ids_ref, glob_ref, slots):
    for part in range(3):
        list_wants(where_ref, ids_ref, glob_ref, where_ref[0], part, slots, part * SEG_BLK, None)


def plan(where, ids, global_ids):
    smem = pl.BlockSpec(memory_space=pltpu.SMEM)
    return pl.pallas_call(
        plan_kernel,
        out_shape=jax.ShapeDtypeStruct((3 * SEG_BLK,), jnp.int32),
        in_specs=[smem] * 3,
        out_specs=smem,
        compiler_params=pltpu.CompilerParams(vmem_limit_bytes=2**20),
    )(where, ids, global_ids)


def gather_kernel(part, low, high, where_ref, ids_ref, glob_ref, near, side, out_ref, slots):
    chip, core = where_ref[0], where_ref[1]
    d1, d2, d3 = PART_DIMS[part]
    size = PART_ROWS[part]

    def act(block, count):
        there = block // CHIP
        inside = block - there * CHIP
        apart = there ^ chip
        place = jnp.where(apart & d1 != 0, CHIP, 0)
        place += ((inside // HERE) ^ core) * HERE + lax.rem(inside, HERE)
        go = jnp.logical_and(count >= low, count < high)
        at = jnp.clip(count - low, 0, high - low - 1)
        target = pl.ds(pl.multiple_of(at * size, 16), size)
        source = pl.ds(pl.multiple_of(place * size, 16), size)

        @pl.when(jnp.logical_and(go, apart & d2 == 0))
        def _():
            out_ref[target] = near[source]

        @pl.when(jnp.logical_and(go, apart & d2 != 0))
        def _():
            out_ref[target] = side[source]

    list_wants(where_ref, ids_ref, glob_ref, chip ^ d3, part, slots, 0, act)


def gather(part, low, high, where, ids, global_ids, near, side):
    smem = pl.BlockSpec(memory_space=pltpu.SMEM)
    vmem = pl.BlockSpec(memory_space=pltpu.VMEM)
    return pl.pallas_call(
        functools.partial(gather_kernel, part, low, high),
        out_shape=flat((high - low) * PART_ROWS[part]),
        in_specs=[smem] * 3 + [vmem] * 2,
        out_specs=vmem,
        scratch_shapes=[pltpu.SMEM((SEG_BLK,), jnp.int32)],
        compiler_params=pltpu.CompilerParams(vmem_limit_bytes=5 * 2**20),
    )(where, ids, global_ids, near, side)


def flag_kernel(here, there, over, notes, sem):
    rows = pl.ds(QUARTER, NOTE)
    copies = [pltpu.make_async_copy(v.at[rows], notes.at[k], sem.at[k]) for k, v in enumerate((here, there))]
    for one in copies:
        one.start()
    for one in copies:
        one.wait()
    flags = notes[...].astype(jnp.float32)
    lane = lax.broadcasted_iota(jnp.int32, flags.shape, 2)
    over[0] = (jnp.max(jnp.where(lane == FLAG, flags, 0.0)) > 0).astype(jnp.int32)


def flag(here, there):
    anywhere = pl.BlockSpec(memory_space=pl.ANY)
    return pl.pallas_call(
        flag_kernel,
        out_shape=jax.ShapeDtypeStruct((1,), jnp.int32),
        in_specs=[anywhere] * 2,
        out_specs=pl.BlockSpec(memory_space=pltpu.SMEM),
        scratch_shapes=[pltpu.VMEM((2, NOTE, HEAD_DIM), jnp.bfloat16), pltpu.SemaphoreType.DMA((2,))],
        compiler_params=pltpu.CompilerParams(vmem_limit_bytes=2**20),
    )(here, there)


def nothing(shapes):
    return pl.pallas_call(
        lambda *refs: None,
        out_shape=shapes,
        out_specs=[pl.BlockSpec(memory_space=pl.ANY)] * len(shapes),
        compiler_params=pltpu.CompilerParams(vmem_limit_bytes=2**20),
    )()


OUTER, INNER, OWN, GLOBAL, RANDOM = 0, 1, 2, 2 + HERE, 2 + HERE + GLOB
N_ENTRY = RANDOM + HERE * RAND


def rows_of(ref, part, place, count=1):
    size = PART_ROWS[part]
    return ref.at[pl.ds(pl.multiple_of(place * size, 16), count * size)]


def collect(mine, where_ref, rand_ref, glob_ref, slots_ref, sources, bufs, sems):
    chip, core = where_ref[0], where_ref[1]
    nears, sides, fars, mores, (quad, quad_x, quad_y), edge = sources
    behind = QUARTER + NOTE
    quads = (quad, quad_x, quad_y.at[pl.ds(0, behind)], quad_y.at[pl.ds(behind, behind)])
    half = core if mine else 1 - core
    base = 0 if mine else HERE

    def slot_of(block):
        return ((block // HERE) ^ core) * HERE + lax.rem(block, HERE)

    def copy(ref, part, place, entry, sem, count=1):
        source, target = rows_of(ref, part, place, count), rows_of(bufs[part], part, entry, count)
        pltpu.make_async_copy(source, target, sem).start()

    def fetch(block, entry, sem):
        there = block // CHIP
        slot = slot_of(block - there * CHIP)
        apart = chip ^ there
        for part in range(3):
            d1, d2, d3 = PART_DIMS[part]
            b1 = jnp.where(apart & d1 != 0, CHIP, 0)
            b2 = apart & d2 != 0
            b3 = apart & d3 != 0

            @pl.when(jnp.logical_and(jnp.logical_not(b2), jnp.logical_not(b3)))
            def _():
                copy(nears[part], part, b1 + slot, entry, sem)

            @pl.when(jnp.logical_and(b2, jnp.logical_not(b3)))
            def _():
                copy(sides[part], part, b1 + slot, entry, sem)

            cap = CAPS[part]
            place = slots_ref[part * SEG_BLK + block]

            @pl.when(jnp.logical_and(b3, place < cap))
            def _():
                copy(fars[part], part, jnp.clip(place, 0, cap - 1), entry, sem)

            @pl.when(jnp.logical_and(b3, place >= cap))
            def _():
                copy(mores[part], part, jnp.clip(place - cap, 0, MOST - cap - 1), entry, sem)

    def fetch_rows(source, low, high, entry, sem):
        for part in range(3):
            a, b = max(low, PART_AT[part]), min(high, PART_AT[part] + PART_ROWS[part])
            if a < b:
                at = pl.multiple_of(entry * PART_ROWS[part], 16) + a - PART_AT[part]
                to = bufs[part].at[pl.ds(pl.multiple_of(at, 16), b - a)]
                pltpu.make_async_copy(source.at[pl.ds(a - low, b - a)], to, sem).start()

    shared = sems.at[HERE]
    for part in range(3):
        copy(nears[part], part, base, OWN, shared, HERE)
        copy(nears[part], part, (HERE - base) + jnp.where(half == 0, 0, HERE - 1), INNER, shared)
    at_edge = chip == jnp.where(half == 0, 0, SEG_CHIPS - 1)

    @pl.when(at_edge)
    def _():
        fetch_rows(edge, 0, SLAB, OUTER, shared)

    @pl.when(jnp.logical_not(at_edge))
    def _():
        fetch(chip * CHIP + jnp.where(half == 0, -1, CHIP), OUTER, shared)

    for g in range(GLOB):
        block = in_segment(where_ref, glob_ref[g])

        @pl.when(block >= 0)
        def _():
            fetch(jnp.maximum(block, 0), GLOBAL + g, shared)

    for k in range(4):
        g = (chip & 1) ^ (k & 1)
        entry = GLOBAL + g
        row = ((chip >> 1) & 1) ^ (k >> 1)
        outside = in_segment(where_ref, glob_ref[g]) < 0
        for value in range(2):

            @pl.when(jnp.logical_and(outside, row == value))
            def _():
                fetch_rows(quads[k], value * QUARTER, (value + 1) * QUARTER, entry, shared)

    for row in range(HERE):
        for k in range(RAND):
            fetch(rand_ref[row, k], RANDOM + row * RAND + k, sems.at[row])

    def wait(low, count, sem):
        for part in range(3):
            of = rows_of(bufs[part], part, low, count)
            pltpu.make_async_copy(rows_of(nears[part], part, 0, count), of, sem).wait()

    return [lambda row=row: wait(RANDOM, RAND, sems.at[row]) for row in range(HERE)] + [
        lambda: wait(0, RANDOM, shared)
    ]


def attend_rows(mine, core, q_ref, bufs, out_ref, waits):
    outer_first = (core if mine else 1 - core) == 0
    factor = math.log2(math.e) / math.sqrt(HEAD_DIM)
    tail, mid = 2 * BLOCK, 3 * BLOCK - CUT_K

    def rows(part, entry, low, high):
        return bufs[part][pl.ds(pl.multiple_of(entry * PART_ROWS[part] + low, 16), high - low)]

    for row in range(HERE):
        if waits:
            waits[row]()
        before = OWN + row - 1 if row else jnp.where(outer_first, OUTER, INNER)
        after = OWN + row + 1 if row < HERE - 1 else jnp.where(outer_first, INNER, OUTER)
        at = RANDOM + row * RAND
        entries = [before, OWN + row, after, GLOBAL, GLOBAL + 1, at, at + 1, at + 2]
        keys, values = [], []
        for head in range(HALF - 1):
            keys.append([rows(head, i, 0, BLOCK) for i in entries])
            values.append([rows(head, i, BLOCK, 2 * BLOCK) for i in entries])
        keys.append([v for i in entries for v in (rows(0, i, tail, tail + CUT_K), rows(2, i, tail, mid))])
        values.append(
            [v for i in entries for v in (rows(1, i, tail, tail + CUT_V), rows(2, i, mid, PART_ROWS[2]))]
        )
        scores = [
            lax.dot_general(
                q_ref[row * BLOCK : (row + 1) * BLOCK, h * HEAD_DIM : (h + 1) * HEAD_DIM],
                jnp.concatenate(keys[h], axis=0),
                (((1,), (1,)), ((), ())),
                preferred_element_type=jnp.float32,
            )
            for h in range(HALF)
        ]
        probs = []
        for h in range(HALF):
            top = jnp.max(scores[h], axis=-1, keepdims=True)
            one = jnp.exp2((scores[h] - top) * factor)
            one = one * (1.0 / jnp.sum(one, axis=-1, keepdims=True))
            probs.append(one.astype(jnp.bfloat16))
        for h in range(HALF):
            mixed = jnp.dot(probs[h], jnp.concatenate(values[h], axis=0), preferred_element_type=jnp.float32)
            out_ref[row * BLOCK : (row + 1) * BLOCK, h * HEAD_DIM : (h + 1) * HEAD_DIM] = mixed.astype(jnp.bfloat16)


def mate_kernel(
    where_ref, rand_ref, rand_mate_ref, glob_ref, slots_ref, q_ref, q_mate_ref,
    near0, near1, near2, side0, side1, side2, far0, far1, far2, more0, more1, more2,
    quad, quad_x, quad_y, edge,
    out_ref, q_out, own0, own1, own2, buf0, buf1, buf2, q_buf, sems, own_sems, q_sems,
):
    core = where_ref[1]
    width = HALF * HEAD_DIM
    cols = pl.ds(pl.multiple_of(core * width, width), width)
    q_copy = pltpu.make_async_copy(q_mate_ref, q_buf, q_sems.at[0])
    q_own = pltpu.make_async_copy(q_ref.at[:, cols], q_out, q_sems.at[1])
    q_copy.start()
    sources = (
        (near0, near1, near2), (side0, side1, side2), (far0, far1, far2), (more0, more1, more2),
        (quad, quad_x, quad_y), edge,
    )
    bufs, own_bufs = (buf0, buf1, buf2), (own0, own1, own2)
    waits = collect(False, where_ref, rand_mate_ref, glob_ref, slots_ref, sources, bufs, sems)
    q_own.start()
    own_waits = collect(True, where_ref, rand_ref, glob_ref, slots_ref, sources, own_bufs, own_sems)
    q_copy.wait()
    waits[HERE]()
    attend_rows(False, core, q_buf, bufs, out_ref, waits)
    q_own.wait()
    for one in own_waits:
        one()


def own_kernel(where_ref, q_ref, buf0, buf1, buf2, out_ref):
    attend_rows(True, where_ref[1], q_ref, (buf0, buf1, buf2), out_ref, None)


def in_hbm(*arrays):
    return [pltpu.with_memory_space_constraint(v, pltpu.HBM) for v in arrays]


def attend_mate(where, rand, rand_mate, global_ids, slots, q, q_mate, nears, sides, fars, mores, quads, edge):
    vmem = pl.BlockSpec(memory_space=pltpu.VMEM)
    smem = pl.BlockSpec(memory_space=pltpu.SMEM)
    hbm = pl.BlockSpec(memory_space=pltpu.HBM)
    out = jax.ShapeDtypeStruct((HERE * BLOCK, HALF * HEAD_DIM), jnp.bfloat16)
    flops = HERE * BLOCK * HALF * (RANDOM + RAND) * BLOCK * HEAD_DIM * 4
    return pl.pallas_call(
        mate_kernel,
        out_shape=[out, out] + [flat(N_ENTRY * rows) for rows in PART_ROWS],
        in_specs=[smem] * 5 + [hbm] * 18,
        out_specs=[vmem] * 5,
        scratch_shapes=[pltpu.VMEM((N_ENTRY * rows, HEAD_DIM), jnp.bfloat16) for rows in PART_ROWS]
        + [
            pltpu.VMEM(out.shape, jnp.bfloat16),
            pltpu.SemaphoreType.DMA((HERE + 1,)),
            pltpu.SemaphoreType.DMA((HERE + 1,)),
            pltpu.SemaphoreType.DMA((2,)),
        ],
        compiler_params=pltpu.CompilerParams(vmem_limit_bytes=24 * 2**20),
        cost_estimate=pl.CostEstimate(flops=flops, bytes_accessed=N_ENTRY * SLAB * 512, transcendentals=0),
    )(where, rand, rand_mate, global_ids, slots, *in_hbm(q, q_mate, *nears, *sides, *fars, *mores, *quads, edge))


def attend_own(where, q, bufs):
    vmem = pl.BlockSpec(memory_space=pltpu.VMEM)
    flops = HERE * BLOCK * HALF * (RANDOM + RAND) * BLOCK * HEAD_DIM * 4
    return pl.pallas_call(
        own_kernel,
        out_shape=jax.ShapeDtypeStruct((HERE * BLOCK, HALF * HEAD_DIM), jnp.bfloat16),
        in_specs=[pl.BlockSpec(memory_space=pltpu.SMEM)] + [vmem] * 4,
        out_specs=vmem,
        compiler_params=pltpu.CompilerParams(vmem_limit_bytes=20 * 2**20),
        cost_estimate=pl.CostEstimate(flops=flops, bytes_accessed=N_ENTRY * SLAB * 256, transcendentals=0),
    )(where, q, *bufs)


def project_kernel(tiles, core_ref, own_ref, got_ref, weight_ref, out_ref, tile_ref, sems):
    core = core_ref[0]
    half = HALF * HEAD_DIM
    width = out_ref.shape[1] // tiles
    mine = pl.ds(pl.multiple_of(core * half, half), half)
    other = pl.ds(pl.multiple_of((1 - core) * half, half), half)
    copies = []
    for k in range(tiles):
        cols = pl.ds(k * width, width)
        total = jnp.dot(own_ref[...], weight_ref[mine, cols], preferred_element_type=jnp.float32)
        total += jnp.dot(got_ref[...], weight_ref[other, cols], preferred_element_type=jnp.float32)
        tile_ref[k] = total.astype(out_ref.dtype)
        copies.append(pltpu.make_async_copy(tile_ref.at[k], out_ref.at[:, cols], sems.at[k]))
        copies[k].start()
    for one in copies:
        one.wait()


def project(core, own, got, weight, tiles=4):
    width = weight.shape[1]
    rows = own.shape[0]
    vmem = pl.BlockSpec(memory_space=pltpu.VMEM)
    return pl.pallas_call(
        functools.partial(project_kernel, tiles),
        out_shape=jax.ShapeDtypeStruct((rows, width), jnp.bfloat16),
        in_specs=[pl.BlockSpec(memory_space=pltpu.SMEM), vmem, vmem, vmem],
        out_specs=pl.BlockSpec(memory_space=pl.ANY),
        scratch_shapes=[pltpu.VMEM((tiles, rows, width // tiles), jnp.bfloat16), pltpu.SemaphoreType.DMA((tiles,))],
        compiler_params=pltpu.CompilerParams(vmem_limit_bytes=14 * 2**20),
    )(core.reshape(1), own, got, weight)


def local(queries, keys_values, rand_blocks, global_ids, out_weight):
    n = lax.axis_size("seq")
    device = lax.axis_index("seq")
    core = device % 2
    chip = (device // 2) % SEG_CHIPS
    where = jnp.stack([chip, core, device // 2])
    rand_mate = swap(rand_blocks, 1)
    own, mate = pack(core, keys_values)
    got = swap(mate, 1)
    ids = jnp.concatenate([rand_blocks.reshape(-1), rand_mate.reshape(-1)])
    *sent, to_xy, mine, border = split(where, global_ids, ids, own, got)

    pairs = []
    chips = n // 2
    for c in range(chips):
        if c % SEG_CHIPS == SEG_CHIPS - 1:
            pairs += [(2 * c + k, 2 * ((c + 1) % chips) + k) for k in range(2)]
        if c % SEG_CHIPS == 0:
            pairs += [(2 * c + k, 2 * ((c - 1) % chips) + k) for k in range(2)]
    edge = lax.ppermute(border, "seq", pairs)
    half = HALF * HEAD_DIM
    q_mate = swap(lax.dynamic_slice_in_dim(queries, (1 - core) * half, half, 1), 1)
    got = [swap(v, 2 * PART_DIMS[part][0]) for part, v in enumerate(sent)] + [swap(to_xy, 6)]
    got, q_mate = lax.optimization_barrier((got, q_mate))
    nears = join(sent, mine, got)
    asked = [got[k][CHIP * PART_ROWS[k] + more, :IDS].astype(jnp.int32) for k, more in ((2, 0), (0, QUARTER), (1, QUARTER))]

    sides = [swap(nears[part], 2 * PART_DIMS[part][1]) for part in range(3)]
    slots = plan(where, ids, global_ids)
    slots, asked[2] = lax.optimization_barrier((slots, asked[2]))
    here = nears[1][2 * CHIP * PART_ROWS[1] :] + sides[1][2 * CHIP * PART_ROWS[1] :]
    if n == 4 * SEG_CHIPS:
        total = swap(here, 16)
    else:
        total = here
        mask = 16
        while mask < n:
            total = total + swap(total, mask)
            mask *= 2

    edge, total, asked[0] = lax.optimization_barrier((edge, total, asked[0]))
    from_x = swap(total, 2)
    sides[0], sides[2] = lax.optimization_barrier((sides[0], sides[2]))
    fars = [
        swap(
            gather(part, 0, CAPS[part], where, asked[part], global_ids, nears[part], sides[part]),
            2 * PART_DIMS[part][2],
        )
        for part in range(3)
    ]
    from_y = swap(jnp.concatenate([total, from_x], axis=0), 4)
    over = flag(here, total)[0] > 0
    over, fars[1], from_x = lax.optimization_barrier((over, fars[1], from_x))
    quads = [total, from_x, from_y]

    def send_rest(args):
        asked, nears, sides = args
        return [
            swap(gather(part, CAPS[part], MOST, where, asked[part], global_ids, nears[part], sides[part]), 2 * PART_DIMS[part][2])
            for part in range(3)
        ]

    def send_none(args):
        return list(nothing([flat((MOST - cap) * rows) for cap, rows in zip(CAPS, PART_ROWS)]))

    mores = lax.cond(over, send_rest, send_none, (asked, nears, sides))

    out_mate, q_own, *bufs = attend_mate(
        where, rand_blocks, rand_mate, global_ids, slots, queries, q_mate, nears, sides, fars, mores, quads, edge
    )
    out_got = swap(out_mate, 1)
    out_own = attend_own(where, q_own, bufs)
    return project(core, out_own, out_got, out_weight)


def solution(mesh):
    placed = (P("seq", None), P(None, "seq", None), P("seq", None), P(), P())
    return jax.shard_map(
        local, mesh=mesh, in_specs=placed, out_specs=P("seq", None), check_vma=False
    )
```

```python
import functools
import math

import jax
import jax.numpy as jnp
from jax import lax
from jax.experimental import pallas as pl
from jax.experimental.pallas import tpu as pltpu
from jax.sharding import PartitionSpec as P

HEADS = 8
HEAD_DIM = 128
BLOCK = 128
RAND = 3
GLOB = 2
SEG_CHIPS = 8
HERE = 3
CHIP = 2 * HERE
HALF = HEADS // 2
SLAB = 2 * HALF * BLOCK

CUT_K, CUT_V = 80, 80
PART_ROWS = (256 + CUT_K, 256 + CUT_V, 256 + 2 * BLOCK - CUT_K - CUT_V)
PART_AT = (0, PART_ROWS[0], PART_ROWS[0] + PART_ROWS[1])
PART_DIMS = ((1, 2, 4), (2, 4, 1), (4, 1, 2))
MOST = 2 * SEG_CHIPS + 2 + GLOB
CAPS = (14, 14, 14)
SEG_BLK = SEG_CHIPS * CHIP
IDS = CHIP * RAND
FLAG = IDS
QUARTER = SLAB // 2
NOTE = 16


def swap(value, mask):
    n = lax.axis_size("seq")
    return lax.ppermute(value, "seq", [(i, i ^ mask) for i in range(n)])


def pack_kernel(core_ref, kv_ref, own_ref, mate_ref):
    core = core_ref[0]
    for which, kv_out in ((1 - core, mate_ref), (core, own_ref)):
        first = pl.multiple_of(which * (HALF * HEAD_DIM), HEAD_DIM)

        def unit(pair, block, head, low, high):
            cols = pl.ds(first + head * HEAD_DIM, HEAD_DIM)
            return kv_ref[pair, block * BLOCK + low : block * BLOCK + high, cols]

        for block in range(HERE):
            for part in range(3):
                at = PART_AT[part]
                kv_out[block, at : at + BLOCK] = unit(0, block, part, 0, BLOCK)
                kv_out[block, at + BLOCK : at + 2 * BLOCK] = unit(1, block, part, 0, BLOCK)
            last = HALF - 1
            a, b, c = (at + 2 * BLOCK for at in PART_AT)
            kv_out[block, a : a + CUT_K] = unit(0, block, last, 0, CUT_K)
            kv_out[block, b : b + CUT_V] = unit(1, block, last, 0, CUT_V)
            mid = c + BLOCK - CUT_K
            kv_out[block, c:mid] = unit(0, block, last, CUT_K, BLOCK)
            kv_out[block, mid : mid + BLOCK - CUT_V] = unit(1, block, last, CUT_V, BLOCK)


def pack(core, keys_values):
    slab = jax.ShapeDtypeStruct((HERE, SLAB, HEAD_DIM), jnp.bfloat16)
    vmem = pl.BlockSpec(memory_space=pltpu.VMEM)
    return pl.pallas_call(
        pack_kernel,
        out_shape=(slab, slab),
        in_specs=[pl.BlockSpec(memory_space=pltpu.SMEM), vmem],
        out_specs=(vmem,) * 2,
        compiler_params=pltpu.CompilerParams(vmem_limit_bytes=4 * 2**20),
    )(core.reshape(1), keys_values)


def in_segment(where, block):
    inside = block - (where[2] - where[0]) * CHIP
    return jnp.where(jnp.logical_and(inside >= 0, inside < SEG_BLK), inside, -1)


def list_wants(where, ids, globs, chip, part, slots, base, act):
    dim = PART_DIMS[part][2]

    @pl.loop(0, SEG_BLK)
    def _(k):
        slots[base + k] = -1

    def add(block, count):
        place = base + block
        new = jnp.logical_and(((block // CHIP) ^ chip) & dim != 0, slots[place] < 0)

        @pl.when(new)
        def _():
            slots[place] = count
            if act is not None:
                act(block, count)

        return count + new.astype(jnp.int32)

    count = lax.fori_loop(0, IDS, lambda k, c: add(ids[k], c), jnp.int32(0))
    low, high = chip * CHIP - 1, chip * CHIP + CHIP
    count = add(jnp.where(chip == 0, chip * CHIP, low), count)
    count = add(jnp.where(chip == SEG_CHIPS - 1, chip * CHIP, high), count)
    for g in range(GLOB):
        block = in_segment(where, globs[g])
        count = add(jnp.where(block < 0, chip * CHIP, block), count)
    return count


def half_queries_kernel(where_ref, q_ref, out_ref, sem):
    width = HALF * HEAD_DIM
    cols = pl.ds(pl.multiple_of((1 - where_ref[1]) * width, width), width)
    copy = pltpu.make_async_copy(q_ref.at[:, cols], out_ref, sem)
    copy.start()
    copy.wait()


def half_queries(where, queries):
    return pl.pallas_call(
        half_queries_kernel,
        out_shape=jax.ShapeDtypeStruct((queries.shape[0], HALF * HEAD_DIM), queries.dtype),
        in_specs=[pl.BlockSpec(memory_space=pltpu.SMEM), pl.BlockSpec(memory_space=pltpu.HBM)],
        out_specs=pl.BlockSpec(memory_space=pltpu.VMEM),
        scratch_shapes=[pltpu.SemaphoreType.DMA],
        compiler_params=pltpu.CompilerParams(vmem_limit_bytes=2 * 2**20),
    )(where, pltpu.with_memory_space_constraint(queries, pltpu.HBM))


def split_kernel(where_ref, glob_ref, ids_ref, own_ref, got_ref, to_x, to_y, to_z, to_xy, mine, edge):
    chip, core, chip_all = where_ref[0], where_ref[1], where_ref[2]
    lane = lax.broadcasted_iota(jnp.int32, (NOTE, HEAD_DIM), 1)
    wanted = lane == jnp.where(chip == 0, -1, chip * CHIP - 1)
    wanted = jnp.logical_or(wanted, lane == jnp.where(chip == SEG_CHIPS - 1, -1, chip * CHIP + CHIP))
    for g in range(GLOB):
        wanted = jnp.logical_or(wanted, lane == in_segment(where_ref, glob_ref[g]))
    row = jnp.zeros((NOTE, HEAD_DIM), jnp.int32)
    for k in range(IDS):
        wanted = jnp.logical_or(wanted, lane == ids_ref[k])
        row = jnp.where(lane == k, ids_ref[k], row)
    apart = jnp.zeros((NOTE, HEAD_DIM), jnp.int32)
    for k in range(1, SEG_CHIPS):
        apart += (lane >= k * CHIP).astype(jnp.int32)
    apart = apart ^ chip
    over = jnp.zeros((NOTE, 1), jnp.float32)
    for part in range(3):
        far = jnp.logical_and(wanted, apart & PART_DIMS[part][2] != 0)
        count = jnp.sum(jnp.where(far, 1.0, 0.0), axis=1, keepdims=True)
        over = jnp.maximum(over, jnp.where(count > CAPS[part], 1.0, 0.0))
    note = jnp.where(lane == FLAG, over, row.astype(jnp.float32)).astype(jnp.bfloat16)

    def write(out, at, k):
        x, y = chip & 1, (chip >> 1) & 1
        block = glob_ref[x ^ (k & 1)]
        half = y ^ (k >> 1)
        owner = block // CHIP
        inside = block - owner * CHIP
        place = lax.rem(inside, HERE)
        rows = pl.ds(pl.multiple_of(half * QUARTER, QUARTER), QUARTER)
        here = owner == chip_all
        mate = (inside // HERE) != core

        @pl.when(jnp.logical_and(here, jnp.logical_not(mate)))
        def _():
            out[at : at + QUARTER] = own_ref[place, rows]

        @pl.when(jnp.logical_and(here, mate))
        def _():
            out[at : at + QUARTER] = got_ref[place, rows]

        @pl.when(jnp.logical_not(here))
        def _():
            out[at : at + QUARTER] = jnp.zeros((QUARTER, HEAD_DIM), jnp.bfloat16)

        out[at + QUARTER : at + QUARTER + NOTE] = note

    for part, out in enumerate((to_x, to_y, to_z)):
        size = PART_ROWS[part]
        for block in range(HERE):
            out[block * size : (block + 1) * size] = own_ref[block, PART_AT[part] : PART_AT[part] + size]
            low = (HERE + block) * size
            out[low : low + size] = got_ref[block, PART_AT[part] : PART_AT[part] + size]
    write(to_x, CHIP * PART_ROWS[0], 1)
    write(to_y, CHIP * PART_ROWS[1], 2)
    to_z[CHIP * PART_ROWS[2] : CHIP * PART_ROWS[2] + NOTE] = note
    write(to_xy, 0, 3)
    write(mine, 0, 0)
    last = chip == SEG_CHIPS - 1

    @pl.when(last == (core == 1))
    def _():
        edge[...] = own_ref[jnp.where(last, HERE - 1, 0)]

    @pl.when(last != (core == 1))
    def _():
        edge[...] = got_ref[jnp.where(last, HERE - 1, 0)]


def flat(rows):
    return jax.ShapeDtypeStruct((rows, HEAD_DIM), jnp.bfloat16)


def split(where, global_ids, ids, own, got):
    smem = pl.BlockSpec(memory_space=pltpu.SMEM)
    vmem = pl.BlockSpec(memory_space=pltpu.VMEM)
    sizes = [CHIP * rows for rows in PART_ROWS]
    return pl.pallas_call(
        split_kernel,
        out_shape=[
            flat(sizes[0] + QUARTER + NOTE), flat(sizes[1] + QUARTER + NOTE), flat(sizes[2] + NOTE),
            flat(QUARTER + NOTE), flat(QUARTER + NOTE), flat(SLAB),
        ],
        in_specs=[smem] * 3 + [vmem] * 2,
        out_specs=[vmem] * 6,
        compiler_params=pltpu.CompilerParams(vmem_limit_bytes=6 * 2**20),
    )(where, global_ids, ids, own, got)


def join_kernel(sent_x, sent_y, sent_z, mine, from_x, from_y, from_z, from_xy, near0, near1, near2):
    for part, (sent, got, near) in enumerate(
        ((sent_x, from_x, near0), (sent_y, from_y, near1), (sent_z, from_z, near2))
    ):
        size = CHIP * PART_ROWS[part]
        near[0:size] = sent[0:size]
        near[size : 2 * size] = got[0:size]
    x, y = CHIP * PART_ROWS[0], CHIP * PART_ROWS[1]
    total = mine[...] + (from_x[x : x + QUARTER + NOTE] + from_y[y : y + QUARTER + NOTE] + from_xy[...])
    near1[2 * y : 2 * y + QUARTER + NOTE] = total


def join(sent, mine, got):
    vmem = pl.BlockSpec(memory_space=pltpu.VMEM)
    return pl.pallas_call(
        join_kernel,
        out_shape=[flat(2 * CHIP * rows + (QUARTER + NOTE if part == 1 else 0)) for part, rows in enumerate(PART_ROWS)],
        in_specs=[vmem] * 8,
        out_specs=[vmem] * 3,
        compiler_params=pltpu.CompilerParams(vmem_limit_bytes=9 * 2**20),
    )(*sent, mine, *got)


def plan_kernel(where_ref, ids_ref, glob_ref, slots):
    for part in range(3):
        list_wants(where_ref, ids_ref, glob_ref, where_ref[0], part, slots, part * SEG_BLK, None)


def plan(where, ids, global_ids):
    smem = pl.BlockSpec(memory_space=pltpu.SMEM)
    return pl.pallas_call(
        plan_kernel,
        out_shape=jax.ShapeDtypeStruct((3 * SEG_BLK,), jnp.int32),
        in_specs=[smem] * 3,
        out_specs=smem,
        compiler_params=pltpu.CompilerParams(vmem_limit_bytes=2**20),
    )(where, ids, global_ids)


def gather_kernel(part, low, high, where_ref, ids_ref, glob_ref, near, side, out_ref, slots):
    chip, core = where_ref[0], where_ref[1]
    d1, d2, d3 = PART_DIMS[part]
    size = PART_ROWS[part]

    def act(block, count):
        there = block // CHIP
        inside = block - there * CHIP
        apart = there ^ chip
        place = jnp.where(apart & d1 != 0, CHIP, 0)
        place += ((inside // HERE) ^ core) * HERE + lax.rem(inside, HERE)
        go = jnp.logical_and(count >= low, count < high)
        at = jnp.clip(count - low, 0, high - low - 1)
        target = pl.ds(pl.multiple_of(at * size, 16), size)
        source = pl.ds(pl.multiple_of(place * size, 16), size)

        @pl.when(jnp.logical_and(go, apart & d2 == 0))
        def _():
            out_ref[target] = near[source]

        @pl.when(jnp.logical_and(go, apart & d2 != 0))
        def _():
            out_ref[target] = side[source]

    list_wants(where_ref, ids_ref, glob_ref, chip ^ d3, part, slots, 0, act)


def gather(part, low, high, where, ids, global_ids, near, side):
    smem = pl.BlockSpec(memory_space=pltpu.SMEM)
    vmem = pl.BlockSpec(memory_space=pltpu.VMEM)
    return pl.pallas_call(
        functools.partial(gather_kernel, part, low, high),
        out_shape=flat((high - low) * PART_ROWS[part]),
        in_specs=[smem] * 3 + [vmem] * 2,
        out_specs=vmem,
        scratch_shapes=[pltpu.SMEM((SEG_BLK,), jnp.int32)],
        compiler_params=pltpu.CompilerParams(vmem_limit_bytes=5 * 2**20),
    )(where, ids, global_ids, near, side)


def flag_kernel(here, there, over, notes, sem):
    rows = pl.ds(QUARTER, NOTE)
    copies = [pltpu.make_async_copy(v.at[rows], notes.at[k], sem.at[k]) for k, v in enumerate((here, there))]
    for one in copies:
        one.start()
    for one in copies:
        one.wait()
    flags = notes[...].astype(jnp.float32)
    lane = lax.broadcasted_iota(jnp.int32, flags.shape, 2)
    over[0] = (jnp.max(jnp.where(lane == FLAG, flags, 0.0)) > 0).astype(jnp.int32)


def flag(here, there):
    anywhere = pl.BlockSpec(memory_space=pl.ANY)
    return pl.pallas_call(
        flag_kernel,
        out_shape=jax.ShapeDtypeStruct((1,), jnp.int32),
        in_specs=[anywhere] * 2,
        out_specs=pl.BlockSpec(memory_space=pltpu.SMEM),
        scratch_shapes=[pltpu.VMEM((2, NOTE, HEAD_DIM), jnp.bfloat16), pltpu.SemaphoreType.DMA((2,))],
        compiler_params=pltpu.CompilerParams(vmem_limit_bytes=2**20),
    )(here, there)


def nothing(shapes):
    return pl.pallas_call(
        lambda *refs: None,
        out_shape=shapes,
        out_specs=[pl.BlockSpec(memory_space=pl.ANY)] * len(shapes),
        compiler_params=pltpu.CompilerParams(vmem_limit_bytes=2**20),
    )()


OUTER, INNER, OWN, GLOBAL, RANDOM = 0, 1, 2, 2 + HERE, 2 + HERE + GLOB
N_ENTRY = RANDOM + HERE * RAND


def rows_of(ref, part, place, count=1):
    size = PART_ROWS[part]
    return ref.at[pl.ds(pl.multiple_of(place * size, 16), count * size)]


def collect(mine, where_ref, rand_ref, glob_ref, slots_ref, sources, bufs, sems):
    chip, core = where_ref[0], where_ref[1]
    nears, sides, fars, mores, (quad, quad_x, quad_y), edge = sources
    behind = QUARTER + NOTE
    quads = (quad, quad_x, quad_y.at[pl.ds(0, behind)], quad_y.at[pl.ds(behind, behind)])
    half = core if mine else 1 - core
    base = 0 if mine else HERE

    def slot_of(block):
        return ((block // HERE) ^ core) * HERE + lax.rem(block, HERE)

    def copy(ref, part, place, entry, sem, count=1):
        source, target = rows_of(ref, part, place, count), rows_of(bufs[part], part, entry, count)
        pltpu.make_async_copy(source, target, sem).start()

    def fetch(block, entry, sem):
        there = block // CHIP
        slot = slot_of(block - there * CHIP)
        apart = chip ^ there
        for part in range(3):
            d1, d2, d3 = PART_DIMS[part]
            b1 = jnp.where(apart & d1 != 0, CHIP, 0)
            b2 = apart & d2 != 0
            b3 = apart & d3 != 0

            @pl.when(jnp.logical_and(jnp.logical_not(b2), jnp.logical_not(b3)))
            def _():
                copy(nears[part], part, b1 + slot, entry, sem)

            @pl.when(jnp.logical_and(b2, jnp.logical_not(b3)))
            def _():
                copy(sides[part], part, b1 + slot, entry, sem)

            cap = CAPS[part]
            place = slots_ref[part * SEG_BLK + block]

            @pl.when(jnp.logical_and(b3, place < cap))
            def _():
                copy(fars[part], part, jnp.clip(place, 0, cap - 1), entry, sem)

            @pl.when(jnp.logical_and(b3, place >= cap))
            def _():
                copy(mores[part], part, jnp.clip(place - cap, 0, MOST - cap - 1), entry, sem)

    def fetch_rows(source, low, high, entry, sem):
        for part in range(3):
            a, b = max(low, PART_AT[part]), min(high, PART_AT[part] + PART_ROWS[part])
            if a < b:
                at = pl.multiple_of(entry * PART_ROWS[part], 16) + a - PART_AT[part]
                to = bufs[part].at[pl.ds(pl.multiple_of(at, 16), b - a)]
                pltpu.make_async_copy(source.at[pl.ds(a - low, b - a)], to, sem).start()

    shared = sems.at[HERE]
    for part in range(3):
        copy(nears[part], part, base, OWN, shared, HERE)
        copy(nears[part], part, (HERE - base) + jnp.where(half == 0, 0, HERE - 1), INNER, shared)
    at_edge = chip == jnp.where(half == 0, 0, SEG_CHIPS - 1)

    @pl.when(at_edge)
    def _():
        fetch_rows(edge, 0, SLAB, OUTER, shared)

    @pl.when(jnp.logical_not(at_edge))
    def _():
        fetch(chip * CHIP + jnp.where(half == 0, -1, CHIP), OUTER, shared)

    for g in range(GLOB):
        block = in_segment(where_ref, glob_ref[g])

        @pl.when(block >= 0)
        def _():
            fetch(jnp.maximum(block, 0), GLOBAL + g, shared)

    for k in range(4):
        g = (chip & 1) ^ (k & 1)
        entry = GLOBAL + g
        row = ((chip >> 1) & 1) ^ (k >> 1)
        outside = in_segment(where_ref, glob_ref[g]) < 0
        for value in range(2):

            @pl.when(jnp.logical_and(outside, row == value))
            def _():
                fetch_rows(quads[k], value * QUARTER, (value + 1) * QUARTER, entry, shared)

    for row in range(HERE):
        for k in range(RAND):
            fetch(rand_ref[row, k], RANDOM + row * RAND + k, sems.at[row])

    def wait(low, count, sem):
        for part in range(3):
            of = rows_of(bufs[part], part, low, count)
            pltpu.make_async_copy(rows_of(nears[part], part, 0, count), of, sem).wait()

    return [lambda row=row: wait(RANDOM, RAND, sems.at[row]) for row in range(HERE)] + [
        lambda: wait(0, RANDOM, shared)
    ]


def attend_rows(mine, core, q_ref, bufs, out_ref, waits):
    outer_first = (core if mine else 1 - core) == 0
    factor = math.log2(math.e) / math.sqrt(HEAD_DIM)
    tail, mid = 2 * BLOCK, 3 * BLOCK - CUT_K

    def rows(part, entry, low, high):
        return bufs[part][pl.ds(pl.multiple_of(entry * PART_ROWS[part] + low, 16), high - low)]

    for row in range(HERE):
        if waits:
            waits[row]()
        before = OWN + row - 1 if row else jnp.where(outer_first, OUTER, INNER)
        after = OWN + row + 1 if row < HERE - 1 else jnp.where(outer_first, INNER, OUTER)
        at = RANDOM + row * RAND
        entries = [before, OWN + row, after, GLOBAL, GLOBAL + 1, at, at + 1, at + 2]
        keys, values = [], []
        for head in range(HALF - 1):
            keys.append([rows(head, i, 0, BLOCK) for i in entries])
            values.append([rows(head, i, BLOCK, 2 * BLOCK) for i in entries])
        keys.append([v for i in entries for v in (rows(0, i, tail, tail + CUT_K), rows(2, i, tail, mid))])
        values.append(
            [v for i in entries for v in (rows(1, i, tail, tail + CUT_V), rows(2, i, mid, PART_ROWS[2]))]
        )
        scores = [
            lax.dot_general(
                q_ref[row * BLOCK : (row + 1) * BLOCK, h * HEAD_DIM : (h + 1) * HEAD_DIM],
                jnp.concatenate(keys[h], axis=0),
                (((1,), (1,)), ((), ())),
                preferred_element_type=jnp.float32,
            )
            for h in range(HALF)
        ]
        probs = []
        for h in range(HALF):
            top = jnp.max(scores[h], axis=-1, keepdims=True)
            one = jnp.exp2((scores[h] - top) * factor)
            one = one * (1.0 / jnp.sum(one, axis=-1, keepdims=True))
            probs.append(one.astype(jnp.bfloat16))
        for h in range(HALF):
            mixed = jnp.dot(probs[h], jnp.concatenate(values[h], axis=0), preferred_element_type=jnp.float32)
            out_ref[row * BLOCK : (row + 1) * BLOCK, h * HEAD_DIM : (h + 1) * HEAD_DIM] = mixed.astype(jnp.bfloat16)


def mate_kernel(
    where_ref, rand_ref, rand_mate_ref, glob_ref, slots_ref, q_ref, q_mate_ref,
    near0, near1, near2, side0, side1, side2, far0, far1, far2, more0, more1, more2,
    quad, quad_x, quad_y, edge,
    out_ref, q_out, own0, own1, own2, buf0, buf1, buf2, q_buf, sems, own_sems, q_sems,
):
    core = where_ref[1]
    width = HALF * HEAD_DIM
    cols = pl.ds(pl.multiple_of(core * width, width), width)
    q_copy = pltpu.make_async_copy(q_mate_ref, q_buf, q_sems.at[0])
    q_own = pltpu.make_async_copy(q_ref.at[:, cols], q_out, q_sems.at[1])
    q_copy.start()
    sources = (
        (near0, near1, near2), (side0, side1, side2), (far0, far1, far2), (more0, more1, more2),
        (quad, quad_x, quad_y), edge,
    )
    bufs, own_bufs = (buf0, buf1, buf2), (own0, own1, own2)
    waits = collect(False, where_ref, rand_mate_ref, glob_ref, slots_ref, sources, bufs, sems)
    q_own.start()
    own_waits = collect(True, where_ref, rand_ref, glob_ref, slots_ref, sources, own_bufs, own_sems)
    q_copy.wait()
    waits[HERE]()
    attend_rows(False, core, q_buf, bufs, out_ref, waits)
    q_own.wait()
    for one in own_waits:
        one()


def own_kernel(where_ref, q_ref, buf0, buf1, buf2, out_ref):
    attend_rows(True, where_ref[1], q_ref, (buf0, buf1, buf2), out_ref, None)


def in_hbm(*arrays):
    return [pltpu.with_memory_space_constraint(v, pltpu.HBM) for v in arrays]


def attend_mate(where, rand, rand_mate, global_ids, slots, q, q_mate, nears, sides, fars, mores, quads, edge):
    vmem = pl.BlockSpec(memory_space=pltpu.VMEM)
    smem = pl.BlockSpec(memory_space=pltpu.SMEM)
    hbm = pl.BlockSpec(memory_space=pltpu.HBM)
    out = jax.ShapeDtypeStruct((HERE * BLOCK, HALF * HEAD_DIM), jnp.bfloat16)
    flops = HERE * BLOCK * HALF * (RANDOM + RAND) * BLOCK * HEAD_DIM * 4
    return pl.pallas_call(
        mate_kernel,
        out_shape=[out, out] + [flat(N_ENTRY * rows) for rows in PART_ROWS],
        in_specs=[smem] * 5 + [hbm] * 18,
        out_specs=[vmem] * 5,
        scratch_shapes=[pltpu.VMEM((N_ENTRY * rows, HEAD_DIM), jnp.bfloat16) for rows in PART_ROWS]
        + [
            pltpu.VMEM(out.shape, jnp.bfloat16),
            pltpu.SemaphoreType.DMA((HERE + 1,)),
            pltpu.SemaphoreType.DMA((HERE + 1,)),
            pltpu.SemaphoreType.DMA((2,)),
        ],
        compiler_params=pltpu.CompilerParams(vmem_limit_bytes=24 * 2**20),
        cost_estimate=pl.CostEstimate(flops=flops, bytes_accessed=N_ENTRY * SLAB * 512, transcendentals=0),
    )(where, rand, rand_mate, global_ids, slots, *in_hbm(q, q_mate, *nears, *sides, *fars, *mores, *quads, edge))


def attend_own(where, q, bufs):
    vmem = pl.BlockSpec(memory_space=pltpu.VMEM)
    flops = HERE * BLOCK * HALF * (RANDOM + RAND) * BLOCK * HEAD_DIM * 4
    return pl.pallas_call(
        own_kernel,
        out_shape=jax.ShapeDtypeStruct((HERE * BLOCK, HALF * HEAD_DIM), jnp.bfloat16),
        in_specs=[pl.BlockSpec(memory_space=pltpu.SMEM)] + [vmem] * 4,
        out_specs=vmem,
        compiler_params=pltpu.CompilerParams(vmem_limit_bytes=20 * 2**20),
        cost_estimate=pl.CostEstimate(flops=flops, bytes_accessed=N_ENTRY * SLAB * 256, transcendentals=0),
    )(where, q, *bufs)


def project_kernel(tiles, core_ref, own_ref, got_ref, weight_ref, out_ref, tile_ref, sems):
    core = core_ref[0]
    half = HALF * HEAD_DIM
    width = out_ref.shape[1] // tiles
    mine = pl.ds(pl.multiple_of(core * half, half), half)
    other = pl.ds(pl.multiple_of((1 - core) * half, half), half)
    copies = []
    for k in range(tiles):
        cols = pl.ds(k * width, width)
        total = jnp.dot(own_ref[...], weight_ref[mine, cols], preferred_element_type=jnp.float32)
        total += jnp.dot(got_ref[...], weight_ref[other, cols], preferred_element_type=jnp.float32)
        tile_ref[k] = total.astype(out_ref.dtype)
        copies.append(pltpu.make_async_copy(tile_ref.at[k], out_ref.at[:, cols], sems.at[k]))
        copies[k].start()
    for one in copies:
        one.wait()


def project(core, own, got, weight, tiles=4):
    width = weight.shape[1]
    rows = own.shape[0]
    vmem = pl.BlockSpec(memory_space=pltpu.VMEM)
    return pl.pallas_call(
        functools.partial(project_kernel, tiles),
        out_shape=jax.ShapeDtypeStruct((rows, width), jnp.bfloat16),
        in_specs=[pl.BlockSpec(memory_space=pltpu.SMEM), vmem, vmem, vmem],
        out_specs=pl.BlockSpec(memory_space=pl.ANY),
        scratch_shapes=[pltpu.VMEM((tiles, rows, width // tiles), jnp.bfloat16), pltpu.SemaphoreType.DMA((tiles,))],
        compiler_params=pltpu.CompilerParams(vmem_limit_bytes=14 * 2**20),
    )(core.reshape(1), own, got, weight)


def local(queries, keys_values, rand_blocks, global_ids, out_weight):
    n = lax.axis_size("seq")
    device = lax.axis_index("seq")
    core = device % 2
    chip = (device // 2) % SEG_CHIPS
    where = jnp.stack([chip, core, device // 2])
    rand_mate = swap(rand_blocks, 1)
    own, mate = pack(core, keys_values)
    got = swap(mate, 1)
    ids = jnp.concatenate([rand_blocks.reshape(-1), rand_mate.reshape(-1)])
    *sent, to_xy, mine, border = split(where, global_ids, ids, own, got)

    pairs = []
    chips = n // 2
    for c in range(chips):
        if c % SEG_CHIPS == SEG_CHIPS - 1:
            pairs += [(2 * c + k, 2 * ((c + 1) % chips) + k) for k in range(2)]
        if c % SEG_CHIPS == 0:
            pairs += [(2 * c + k, 2 * ((c - 1) % chips) + k) for k in range(2)]
    edge = lax.ppermute(border, "seq", pairs)
    q_mate = swap(half_queries(where, queries), 1)
    got = [swap(v, 2 * PART_DIMS[part][0]) for part, v in enumerate(sent)] + [swap(to_xy, 6)]
    got, q_mate = lax.optimization_barrier((got, q_mate))
    nears = join(sent, mine, got)
    asked = [got[k][CHIP * PART_ROWS[k] + more, :IDS].astype(jnp.int32) for k, more in ((2, 0), (0, QUARTER), (1, QUARTER))]

    sides = [swap(nears[part], 2 * PART_DIMS[part][1]) for part in range(3)]
    slots = plan(where, ids, global_ids)
    here = nears[1][2 * CHIP * PART_ROWS[1] :] + sides[1][2 * CHIP * PART_ROWS[1] :]
    slots, here, asked[2] = lax.optimization_barrier((slots, here, asked[2]))
    if n == 4 * SEG_CHIPS:
        total = swap(here, 16)
    else:
        total = here
        mask = 16
        while mask < n:
            total = total + swap(total, mask)
            mask *= 2

    edge, total, asked[0] = lax.optimization_barrier((edge, total, asked[0]))
    from_x = swap(total, 2)
    sides[0], sides[2] = lax.optimization_barrier((sides[0], sides[2]))
    fars = [
        swap(
            gather(part, 0, CAPS[part], where, asked[part], global_ids, nears[part], sides[part]),
            2 * PART_DIMS[part][2],
        )
        for part in range(3)
    ]
    from_y = swap(jnp.concatenate([total, from_x], axis=0), 4)
    over = flag(here, total)[0] > 0
    over, fars[1], from_x = lax.optimization_barrier((over, fars[1], from_x))
    quads = [total, from_x, from_y]

    def send_rest(args):
        asked, nears, sides = args
        return [
            swap(gather(part, CAPS[part], MOST, where, asked[part], global_ids, nears[part], sides[part]), 2 * PART_DIMS[part][2])
            for part in range(3)
        ]

    def send_none(args):
        return list(nothing([flat((MOST - cap) * rows) for cap, rows in zip(CAPS, PART_ROWS)]))

    mores = lax.cond(over, send_rest, send_none, (asked, nears, sides))

    out_mate, q_own, *bufs = attend_mate(
        where, rand_blocks, rand_mate, global_ids, slots, queries, q_mate, nears, sides, fars, mores, quads, edge
    )
    out_got = swap(out_mate, 1)
    out_own = attend_own(where, q_own, bufs)
    return project(core, out_own, out_got, out_weight)


def solution(mesh):
    placed = (P("seq", None), P(None, "seq", None), P("seq", None), P(), P())
    return jax.shard_map(
        local, mesh=mesh, in_specs=placed, out_specs=P("seq", None), check_vma=False
    )
```

```python
import functools
import math

import jax
import jax.numpy as jnp
from jax import lax
from jax.experimental import pallas as pl
from jax.experimental.pallas import tpu as pltpu
from jax.sharding import PartitionSpec as P

HEADS = 8
HEAD_DIM = 128
BLOCK = 128
RAND = 3
GLOB = 2
SEG_CHIPS = 8
HERE = 3
CHIP = 2 * HERE
HALF = HEADS // 2
SLAB = 2 * HALF * BLOCK

CUT_K, CUT_V = 80, 64
PART_ROWS = (256 + CUT_K, 256 + CUT_V, 256 + 2 * BLOCK - CUT_K - CUT_V)
PART_AT = (0, PART_ROWS[0], PART_ROWS[0] + PART_ROWS[1])
PART_DIMS = ((1, 2, 4), (2, 4, 1), (4, 1, 2))
MOST = 2 * SEG_CHIPS + 2 + GLOB
CAPS = (14, 14, 14)
SEG_BLK = SEG_CHIPS * CHIP
IDS = CHIP * RAND
FLAG = IDS
QUARTER = SLAB // 2
NOTE = 16


def swap(value, mask):
    n = lax.axis_size("seq")
    return lax.ppermute(value, "seq", [(i, i ^ mask) for i in range(n)])


def pack_kernel(core_ref, kv_ref, own_ref, mate_ref):
    core = core_ref[0]
    for which, kv_out in ((1 - core, mate_ref), (core, own_ref)):
        first = pl.multiple_of(which * (HALF * HEAD_DIM), HEAD_DIM)

        def unit(pair, block, head, low, high):
            cols = pl.ds(first + head * HEAD_DIM, HEAD_DIM)
            return kv_ref[pair, block * BLOCK + low : block * BLOCK + high, cols]

        for block in range(HERE):
            for part in range(3):
                at = PART_AT[part]
                kv_out[block, at : at + BLOCK] = unit(0, block, part, 0, BLOCK)
                kv_out[block, at + BLOCK : at + 2 * BLOCK] = unit(1, block, part, 0, BLOCK)
            last = HALF - 1
            a, b, c = (at + 2 * BLOCK for at in PART_AT)
            kv_out[block, a : a + CUT_K] = unit(0, block, last, 0, CUT_K)
            kv_out[block, b : b + CUT_V] = unit(1, block, last, 0, CUT_V)
            mid = c + BLOCK - CUT_K
            kv_out[block, c:mid] = unit(0, block, last, CUT_K, BLOCK)
            kv_out[block, mid : mid + BLOCK - CUT_V] = unit(1, block, last, CUT_V, BLOCK)


def pack(core, keys_values):
    slab = jax.ShapeDtypeStruct((HERE, SLAB, HEAD_DIM), jnp.bfloat16)
    vmem = pl.BlockSpec(memory_space=pltpu.VMEM)
    return pl.pallas_call(
        pack_kernel,
        out_shape=(slab, slab),
        in_specs=[pl.BlockSpec(memory_space=pltpu.SMEM), vmem],
        out_specs=(vmem,) * 2,
        compiler_params=pltpu.CompilerParams(vmem_limit_bytes=4 * 2**20),
    )(core.reshape(1), keys_values)


def in_segment(where, block):
    inside = block - (where[2] - where[0]) * CHIP
    return jnp.where(jnp.logical_and(inside >= 0, inside < SEG_BLK), inside, -1)


def list_wants(where, ids, globs, chip, part, slots, base, act):
    dim = PART_DIMS[part][2]

    @pl.loop(0, SEG_BLK)
    def _(k):
        slots[base + k] = -1

    def add(block, count):
        place = base + block
        new = jnp.logical_and(((block // CHIP) ^ chip) & dim != 0, slots[place] < 0)

        @pl.when(new)
        def _():
            slots[place] = count
            if act is not None:
                act(block, count)

        return count + new.astype(jnp.int32)

    count = lax.fori_loop(0, IDS, lambda k, c: add(ids[k], c), jnp.int32(0))
    low, high = chip * CHIP - 1, chip * CHIP + CHIP
    count = add(jnp.where(chip == 0, chip * CHIP, low), count)
    count = add(jnp.where(chip == SEG_CHIPS - 1, chip * CHIP, high), count)
    for g in range(GLOB):
        block = in_segment(where, globs[g])
        count = add(jnp.where(block < 0, chip * CHIP, block), count)
    return count


def half_queries_kernel(where_ref, q_ref, out_ref, sem):
    width = HALF * HEAD_DIM
    cols = pl.ds(pl.multiple_of((1 - where_ref[1]) * width, width), width)
    copy = pltpu.make_async_copy(q_ref.at[:, cols], out_ref, sem)
    copy.start()
    copy.wait()


def half_queries(where, queries):
    return pl.pallas_call(
        half_queries_kernel,
        out_shape=jax.ShapeDtypeStruct((queries.shape[0], HALF * HEAD_DIM), queries.dtype),
        in_specs=[pl.BlockSpec(memory_space=pltpu.SMEM), pl.BlockSpec(memory_space=pltpu.HBM)],
        out_specs=pl.BlockSpec(memory_space=pltpu.VMEM),
        scratch_shapes=[pltpu.SemaphoreType.DMA],
        compiler_params=pltpu.CompilerParams(vmem_limit_bytes=2 * 2**20),
    )(where, pltpu.with_memory_space_constraint(queries, pltpu.HBM))


def split_kernel(where_ref, glob_ref, ids_ref, own_ref, got_ref, to_x, to_y, to_z, to_xy, mine, edge):
    chip, core, chip_all = where_ref[0], where_ref[1], where_ref[2]
    lane = lax.broadcasted_iota(jnp.int32, (NOTE, HEAD_DIM), 1)
    wanted = lane == jnp.where(chip == 0, -1, chip * CHIP - 1)
    wanted = jnp.logical_or(wanted, lane == jnp.where(chip == SEG_CHIPS - 1, -1, chip * CHIP + CHIP))
    for g in range(GLOB):
        wanted = jnp.logical_or(wanted, lane == in_segment(where_ref, glob_ref[g]))
    row = jnp.zeros((NOTE, HEAD_DIM), jnp.int32)
    for k in range(IDS):
        wanted = jnp.logical_or(wanted, lane == ids_ref[k])
        row = jnp.where(lane == k, ids_ref[k], row)
    apart = jnp.zeros((NOTE, HEAD_DIM), jnp.int32)
    for k in range(1, SEG_CHIPS):
        apart += (lane >= k * CHIP).astype(jnp.int32)
    apart = apart ^ chip
    over = jnp.zeros((NOTE, 1), jnp.float32)
    for part in range(3):
        far = jnp.logical_and(wanted, apart & PART_DIMS[part][2] != 0)
        count = jnp.sum(jnp.where(far, 1.0, 0.0), axis=1, keepdims=True)
        over = jnp.maximum(over, jnp.where(count > CAPS[part], 1.0, 0.0))
    note = jnp.where(lane == FLAG, over, row.astype(jnp.float32)).astype(jnp.bfloat16)

    def write(out, at, k):
        x, y = chip & 1, (chip >> 1) & 1
        block = glob_ref[x ^ (k & 1)]
        half = y ^ (k >> 1)
        owner = block // CHIP
        inside = block - owner * CHIP
        place = lax.rem(inside, HERE)
        rows = pl.ds(pl.multiple_of(half * QUARTER, QUARTER), QUARTER)
        here = owner == chip_all
        mate = (inside // HERE) != core

        @pl.when(jnp.logical_and(here, jnp.logical_not(mate)))
        def _():
            out[at : at + QUARTER] = own_ref[place, rows]

        @pl.when(jnp.logical_and(here, mate))
        def _():
            out[at : at + QUARTER] = got_ref[place, rows]

        @pl.when(jnp.logical_not(here))
        def _():
            out[at : at + QUARTER] = jnp.zeros((QUARTER, HEAD_DIM), jnp.bfloat16)

        out[at + QUARTER : at + QUARTER + NOTE] = note

    for part, out in enumerate((to_x, to_y, to_z)):
        size = PART_ROWS[part]
        for block in range(HERE):
            out[block * size : (block + 1) * size] = own_ref[block, PART_AT[part] : PART_AT[part] + size]
            low = (HERE + block) * size
            out[low : low + size] = got_ref[block, PART_AT[part] : PART_AT[part] + size]
    write(to_x, CHIP * PART_ROWS[0], 1)
    write(to_y, CHIP * PART_ROWS[1], 2)
    to_z[CHIP * PART_ROWS[2] : CHIP * PART_ROWS[2] + NOTE] = note
    write(to_xy, 0, 3)
    write(mine, 0, 0)
    last = chip == SEG_CHIPS - 1

    @pl.when(last == (core == 1))
    def _():
        edge[...] = own_ref[jnp.where(last, HERE - 1, 0)]

    @pl.when(last != (core == 1))
    def _():
        edge[...] = got_ref[jnp.where(last, HERE - 1, 0)]


def flat(rows):
    return jax.ShapeDtypeStruct((rows, HEAD_DIM), jnp.bfloat16)


def split(where, global_ids, ids, own, got):
    smem = pl.BlockSpec(memory_space=pltpu.SMEM)
    vmem = pl.BlockSpec(memory_space=pltpu.VMEM)
    sizes = [CHIP * rows for rows in PART_ROWS]
    return pl.pallas_call(
        split_kernel,
        out_shape=[
            flat(sizes[0] + QUARTER + NOTE), flat(sizes[1] + QUARTER + NOTE), flat(sizes[2] + NOTE),
            flat(QUARTER + NOTE), flat(QUARTER + NOTE), flat(SLAB),
        ],
        in_specs=[smem] * 3 + [vmem] * 2,
        out_specs=[vmem] * 6,
        compiler_params=pltpu.CompilerParams(vmem_limit_bytes=6 * 2**20),
    )(where, global_ids, ids, own, got)


def join_kernel(sent_x, sent_y, sent_z, mine, from_x, from_y, from_z, from_xy, near0, near1, near2):
    for part, (sent, got, near) in enumerate(
        ((sent_x, from_x, near0), (sent_y, from_y, near1), (sent_z, from_z, near2))
    ):
        size = CHIP * PART_ROWS[part]
        near[0:size] = sent[0:size]
        near[size : 2 * size] = got[0:size]
    x, y = CHIP * PART_ROWS[0], CHIP * PART_ROWS[1]
    total = mine[...] + (from_x[x : x + QUARTER + NOTE] + from_y[y : y + QUARTER + NOTE] + from_xy[...])
    near1[2 * y : 2 * y + QUARTER + NOTE] = total


def join(sent, mine, got):
    vmem = pl.BlockSpec(memory_space=pltpu.VMEM)
    return pl.pallas_call(
        join_kernel,
        out_shape=[flat(2 * CHIP * rows + (QUARTER + NOTE if part == 1 else 0)) for part, rows in enumerate(PART_ROWS)],
        in_specs=[vmem] * 8,
        out_specs=[vmem] * 3,
        compiler_params=pltpu.CompilerParams(vmem_limit_bytes=9 * 2**20),
    )(*sent, mine, *got)


def plan_kernel(where_ref, ids_ref, glob_ref, slots):
    for part in range(3):
        list_wants(where_ref, ids_ref, glob_ref, where_ref[0], part, slots, part * SEG_BLK, None)


def plan(where, ids, global_ids):
    smem = pl.BlockSpec(memory_space=pltpu.SMEM)
    return pl.pallas_call(
        plan_kernel,
        out_shape=jax.ShapeDtypeStruct((3 * SEG_BLK,), jnp.int32),
        in_specs=[smem] * 3,
        out_specs=smem,
        compiler_params=pltpu.CompilerParams(vmem_limit_bytes=2**20),
    )(where, ids, global_ids)


def gather_kernel(part, low, high, where_ref, ids_ref, glob_ref, near, side, out_ref, slots):
    chip, core = where_ref[0], where_ref[1]
    d1, d2, d3 = PART_DIMS[part]
    size = PART_ROWS[part]

    def act(block, count):
        there = block // CHIP
        inside = block - there * CHIP
        apart = there ^ chip
        place = jnp.where(apart & d1 != 0, CHIP, 0)
        place += ((inside // HERE) ^ core) * HERE + lax.rem(inside, HERE)
        go = jnp.logical_and(count >= low, count < high)
        at = jnp.clip(count - low, 0, high - low - 1)
        target = pl.ds(pl.multiple_of(at * size, 16), size)
        source = pl.ds(pl.multiple_of(place * size, 16), size)

        @pl.when(jnp.logical_and(go, apart & d2 == 0))
        def _():
            out_ref[target] = near[source]

        @pl.when(jnp.logical_and(go, apart & d2 != 0))
        def _():
            out_ref[target] = side[source]

    list_wants(where_ref, ids_ref, glob_ref, chip ^ d3, part, slots, 0, act)


def gather(part, low, high, where, ids, global_ids, near, side):
    smem = pl.BlockSpec(memory_space=pltpu.SMEM)
    vmem = pl.BlockSpec(memory_space=pltpu.VMEM)
    return pl.pallas_call(
        functools.partial(gather_kernel, part, low, high),
        out_shape=flat((high - low) * PART_ROWS[part]),
        in_specs=[smem] * 3 + [vmem] * 2,
        out_specs=vmem,
        scratch_shapes=[pltpu.SMEM((SEG_BLK,), jnp.int32)],
        compiler_params=pltpu.CompilerParams(vmem_limit_bytes=5 * 2**20),
    )(where, ids, global_ids, near, side)


def flag_kernel(here, there, over, notes, sem):
    rows = pl.ds(QUARTER, NOTE)
    copies = [pltpu.make_async_copy(v.at[rows], notes.at[k], sem.at[k]) for k, v in enumerate((here, there))]
    for one in copies:
        one.start()
    for one in copies:
        one.wait()
    flags = notes[...].astype(jnp.float32)
    lane = lax.broadcasted_iota(jnp.int32, flags.shape, 2)
    over[0] = (jnp.max(jnp.where(lane == FLAG, flags, 0.0)) > 0).astype(jnp.int32)


def flag(here, there):
    anywhere = pl.BlockSpec(memory_space=pl.ANY)
    return pl.pallas_call(
        flag_kernel,
        out_shape=jax.ShapeDtypeStruct((1,), jnp.int32),
        in_specs=[anywhere] * 2,
        out_specs=pl.BlockSpec(memory_space=pltpu.SMEM),
        scratch_shapes=[pltpu.VMEM((2, NOTE, HEAD_DIM), jnp.bfloat16), pltpu.SemaphoreType.DMA((2,))],
        compiler_params=pltpu.CompilerParams(vmem_limit_bytes=2**20),
    )(here, there)


def nothing(shapes):
    return pl.pallas_call(
        lambda *refs: None,
        out_shape=shapes,
        out_specs=[pl.BlockSpec(memory_space=pl.ANY)] * len(shapes),
        compiler_params=pltpu.CompilerParams(vmem_limit_bytes=2**20),
    )()


OUTER, INNER, OWN, GLOBAL, RANDOM = 0, 1, 2, 2 + HERE, 2 + HERE + GLOB
N_ENTRY = RANDOM + HERE * RAND


def rows_of(ref, part, place, count=1):
    size = PART_ROWS[part]
    return ref.at[pl.ds(pl.multiple_of(place * size, 16), count * size)]


def collect(mine, where_ref, rand_ref, glob_ref, slots_ref, sources, bufs, sems):
    chip, core = where_ref[0], where_ref[1]
    nears, sides, fars, mores, quads, edge = sources
    half = core if mine else 1 - core
    base = 0 if mine else HERE

    def slot_of(block):
        return ((block // HERE) ^ core) * HERE + lax.rem(block, HERE)

    def copy(ref, part, place, entry, sem, count=1):
        source, target = rows_of(ref, part, place, count), rows_of(bufs[part], part, entry, count)
        pltpu.make_async_copy(source, target, sem).start()

    def fetch(block, entry, sem):
        there = block // CHIP
        slot = slot_of(block - there * CHIP)
        apart = chip ^ there
        for part in range(3):
            d1, d2, d3 = PART_DIMS[part]
            b1 = jnp.where(apart & d1 != 0, CHIP, 0)
            b2 = apart & d2 != 0
            b3 = apart & d3 != 0

            @pl.when(jnp.logical_and(jnp.logical_not(b2), jnp.logical_not(b3)))
            def _():
                copy(nears[part], part, b1 + slot, entry, sem)

            @pl.when(jnp.logical_and(b2, jnp.logical_not(b3)))
            def _():
                copy(sides[part], part, b1 + slot, entry, sem)

            cap = CAPS[part]
            place = slots_ref[part * SEG_BLK + block]

            @pl.when(jnp.logical_and(b3, place < cap))
            def _():
                copy(fars[part], part, jnp.clip(place, 0, cap - 1), entry, sem)

            @pl.when(jnp.logical_and(b3, place >= cap))
            def _():
                copy(mores[part], part, jnp.clip(place - cap, 0, MOST - cap - 1), entry, sem)

    def fetch_rows(source, low, high, entry, sem):
        for part in range(3):
            a, b = max(low, PART_AT[part]), min(high, PART_AT[part] + PART_ROWS[part])
            if a < b:
                at = pl.multiple_of(entry * PART_ROWS[part], 16) + a - PART_AT[part]
                to = bufs[part].at[pl.ds(pl.multiple_of(at, 16), b - a)]
                pltpu.make_async_copy(source.at[pl.ds(a - low, b - a)], to, sem).start()

    shared = sems.at[HERE]
    for part in range(3):
        copy(nears[part], part, base, OWN, shared, HERE)
        copy(nears[part], part, (HERE - base) + jnp.where(half == 0, 0, HERE - 1), INNER, shared)
    at_edge = chip == jnp.where(half == 0, 0, SEG_CHIPS - 1)

    @pl.when(at_edge)
    def _():
        fetch_rows(edge, 0, SLAB, OUTER, shared)

    @pl.when(jnp.logical_not(at_edge))
    def _():
        fetch(chip * CHIP + jnp.where(half == 0, -1, CHIP), OUTER, shared)

    for g in range(GLOB):
        block = in_segment(where_ref, glob_ref[g])

        @pl.when(block >= 0)
        def _():
            fetch(jnp.maximum(block, 0), GLOBAL + g, shared)

    for k in range(4):
        g = (chip & 1) ^ (k & 1)
        entry = GLOBAL + g
        row = ((chip >> 1) & 1) ^ (k >> 1)
        outside = in_segment(where_ref, glob_ref[g]) < 0
        for value in range(2):

            @pl.when(jnp.logical_and(outside, row == value))
            def _():
                fetch_rows(quads[k], value * QUARTER, (value + 1) * QUARTER, entry, shared)

    for row in range(HERE):
        for k in range(RAND):
            fetch(rand_ref[row, k], RANDOM + row * RAND + k, sems.at[row])

    def wait(low, count, sem):
        for part in range(3):
            of = rows_of(bufs[part], part, low, count)
            pltpu.make_async_copy(rows_of(nears[part], part, 0, count), of, sem).wait()

    return [lambda row=row: wait(RANDOM, RAND, sems.at[row]) for row in range(HERE)] + [
        lambda: wait(0, RANDOM, shared)
    ]


def attend_rows(mine, core, q_ref, bufs, out_ref, waits):
    outer_first = (core if mine else 1 - core) == 0
    factor = math.log2(math.e) / math.sqrt(HEAD_DIM)
    tail, mid = 2 * BLOCK, 3 * BLOCK - CUT_K

    def rows(part, entry, low, high):
        return bufs[part][pl.ds(pl.multiple_of(entry * PART_ROWS[part] + low, 16), high - low)]

    for row in range(HERE):
        if waits:
            waits[row]()
        before = OWN + row - 1 if row else jnp.where(outer_first, OUTER, INNER)
        after = OWN + row + 1 if row < HERE - 1 else jnp.where(outer_first, INNER, OUTER)
        at = RANDOM + row * RAND
        entries = [before, OWN + row, after, GLOBAL, GLOBAL + 1, at, at + 1, at + 2]
        keys, values = [], []
        for head in range(HALF - 1):
            keys.append([rows(head, i, 0, BLOCK) for i in entries])
            values.append([rows(head, i, BLOCK, 2 * BLOCK) for i in entries])
        keys.append([v for i in entries for v in (rows(0, i, tail, tail + CUT_K), rows(2, i, tail, mid))])
        values.append(
            [v for i in entries for v in (rows(1, i, tail, tail + CUT_V), rows(2, i, mid, PART_ROWS[2]))]
        )
        scores = [
            lax.dot_general(
                q_ref[row * BLOCK : (row + 1) * BLOCK, h * HEAD_DIM : (h + 1) * HEAD_DIM],
                jnp.concatenate(keys[h], axis=0),
                (((1,), (1,)), ((), ())),
                preferred_element_type=jnp.float32,
            )
            for h in range(HALF)
        ]
        probs = []
        for h in range(HALF):
            top = jnp.max(scores[h], axis=-1, keepdims=True)
            one = jnp.exp2((scores[h] - top) * factor)
            one = one * (1.0 / jnp.sum(one, axis=-1, keepdims=True))
            probs.append(one.astype(jnp.bfloat16))
        for h in range(HALF):
            mixed = jnp.dot(probs[h], jnp.concatenate(values[h], axis=0), preferred_element_type=jnp.float32)
            out_ref[row * BLOCK : (row + 1) * BLOCK, h * HEAD_DIM : (h + 1) * HEAD_DIM] = mixed.astype(jnp.bfloat16)


def mate_kernel(
    where_ref, rand_ref, rand_mate_ref, glob_ref, slots_ref, q_ref, q_mate_ref,
    near0, near1, near2, side0, side1, side2, far0, far1, far2, more0, more1, more2,
    quad, quad_x, quad_y, quad_xy, edge,
    out_ref, q_out, own0, own1, own2, buf0, buf1, buf2, q_buf, sems, own_sems, q_sems,
):
    core = where_ref[1]
    width = HALF * HEAD_DIM
    cols = pl.ds(pl.multiple_of(core * width, width), width)
    q_copy = pltpu.make_async_copy(q_mate_ref, q_buf, q_sems.at[0])
    q_own = pltpu.make_async_copy(q_ref.at[:, cols], q_out, q_sems.at[1])
    q_copy.start()
    sources = (
        (near0, near1, near2), (side0, side1, side2), (far0, far1, far2), (more0, more1, more2),
        (quad, quad_x, quad_y, quad_xy), edge,
    )
    bufs, own_bufs = (buf0, buf1, buf2), (own0, own1, own2)
    waits = collect(False, where_ref, rand_mate_ref, glob_ref, slots_ref, sources, bufs, sems)
    q_own.start()
    own_waits = collect(True, where_ref, rand_ref, glob_ref, slots_ref, sources, own_bufs, own_sems)
    q_copy.wait()
    waits[HERE]()
    attend_rows(False, core, q_buf, bufs, out_ref, waits)
    q_own.wait()
    for one in own_waits:
        one()


def own_kernel(where_ref, q_ref, buf0, buf1, buf2, out_ref):
    attend_rows(True, where_ref[1], q_ref, (buf0, buf1, buf2), out_ref, None)


def in_hbm(*arrays):
    return [pltpu.with_memory_space_constraint(v, pltpu.HBM) for v in arrays]


def attend_mate(where, rand, rand_mate, global_ids, slots, q, q_mate, nears, sides, fars, mores, quads, edge):
    vmem = pl.BlockSpec(memory_space=pltpu.VMEM)
    smem = pl.BlockSpec(memory_space=pltpu.SMEM)
    hbm = pl.BlockSpec(memory_space=pltpu.HBM)
    out = jax.ShapeDtypeStruct((HERE * BLOCK, HALF * HEAD_DIM), jnp.bfloat16)
    flops = HERE * BLOCK * HALF * (RANDOM + RAND) * BLOCK * HEAD_DIM * 4
    return pl.pallas_call(
        mate_kernel,
        out_shape=[out, out] + [flat(N_ENTRY * rows) for rows in PART_ROWS],
        in_specs=[smem] * 5 + [hbm] * 19,
        out_specs=[vmem] * 5,
        scratch_shapes=[pltpu.VMEM((N_ENTRY * rows, HEAD_DIM), jnp.bfloat16) for rows in PART_ROWS]
        + [
            pltpu.VMEM(out.shape, jnp.bfloat16),
            pltpu.SemaphoreType.DMA((HERE + 1,)),
            pltpu.SemaphoreType.DMA((HERE + 1,)),
            pltpu.SemaphoreType.DMA((2,)),
        ],
        compiler_params=pltpu.CompilerParams(vmem_limit_bytes=24 * 2**20),
        cost_estimate=pl.CostEstimate(flops=flops, bytes_accessed=N_ENTRY * SLAB * 512, transcendentals=0),
    )(where, rand, rand_mate, global_ids, slots, *in_hbm(q, q_mate, *nears, *sides, *fars, *mores, *quads, edge))


def attend_own(where, q, bufs):
    vmem = pl.BlockSpec(memory_space=pltpu.VMEM)
    flops = HERE * BLOCK * HALF * (RANDOM + RAND) * BLOCK * HEAD_DIM * 4
    return pl.pallas_call(
        own_kernel,
        out_shape=jax.ShapeDtypeStruct((HERE * BLOCK, HALF * HEAD_DIM), jnp.bfloat16),
        in_specs=[pl.BlockSpec(memory_space=pltpu.SMEM)] + [vmem] * 4,
        out_specs=vmem,
        compiler_params=pltpu.CompilerParams(vmem_limit_bytes=20 * 2**20),
        cost_estimate=pl.CostEstimate(flops=flops, bytes_accessed=N_ENTRY * SLAB * 256, transcendentals=0),
    )(where, q, *bufs)


def project_kernel(tiles, core_ref, own_ref, got_ref, weight_ref, out_ref, tile_ref, sems):
    core = core_ref[0]
    half = HALF * HEAD_DIM
    width = out_ref.shape[1] // tiles
    mine = pl.ds(pl.multiple_of(core * half, half), half)
    other = pl.ds(pl.multiple_of((1 - core) * half, half), half)
    copies = []
    for k in range(tiles):
        cols = pl.ds(k * width, width)
        total = jnp.dot(own_ref[...], weight_ref[mine, cols], preferred_element_type=jnp.float32)
        total += jnp.dot(got_ref[...], weight_ref[other, cols], preferred_element_type=jnp.float32)
        tile_ref[k] = total.astype(out_ref.dtype)
        copies.append(pltpu.make_async_copy(tile_ref.at[k], out_ref.at[:, cols], sems.at[k]))
        copies[k].start()
    for one in copies:
        one.wait()


def project(core, own, got, weight, tiles=4):
    width = weight.shape[1]
    rows = own.shape[0]
    vmem = pl.BlockSpec(memory_space=pltpu.VMEM)
    return pl.pallas_call(
        functools.partial(project_kernel, tiles),
        out_shape=jax.ShapeDtypeStruct((rows, width), jnp.bfloat16),
        in_specs=[pl.BlockSpec(memory_space=pltpu.SMEM), vmem, vmem, vmem],
        out_specs=pl.BlockSpec(memory_space=pl.ANY),
        scratch_shapes=[pltpu.VMEM((tiles, rows, width // tiles), jnp.bfloat16), pltpu.SemaphoreType.DMA((tiles,))],
        compiler_params=pltpu.CompilerParams(vmem_limit_bytes=14 * 2**20),
    )(core.reshape(1), own, got, weight)


def local(queries, keys_values, rand_blocks, global_ids, out_weight):
    n = lax.axis_size("seq")
    device = lax.axis_index("seq")
    core = device % 2
    chip = (device // 2) % SEG_CHIPS
    where = jnp.stack([chip, core, device // 2])
    rand_mate = swap(rand_blocks, 1)
    own, mate = pack(core, keys_values)
    got = swap(mate, 1)
    ids = jnp.concatenate([rand_blocks.reshape(-1), rand_mate.reshape(-1)])
    *sent, to_xy, mine, border = split(where, global_ids, ids, own, got)

    pairs = []
    chips = n // 2
    for c in range(chips):
        if c % SEG_CHIPS == SEG_CHIPS - 1:
            pairs += [(2 * c + k, 2 * ((c + 1) % chips) + k) for k in range(2)]
        if c % SEG_CHIPS == 0:
            pairs += [(2 * c + k, 2 * ((c - 1) % chips) + k) for k in range(2)]
    edge = lax.ppermute(border, "seq", pairs)
    q_mate = swap(half_queries(where, queries), 1)
    got = [swap(v, 2 * PART_DIMS[part][0]) for part, v in enumerate(sent)] + [swap(to_xy, 6)]
    got, q_mate = lax.optimization_barrier((got, q_mate))
    nears = join(sent, mine, got)
    asked = [got[k][CHIP * PART_ROWS[k] + more, :IDS].astype(jnp.int32) for k, more in ((2, 0), (0, QUARTER), (1, QUARTER))]

    sides = [swap(nears[part], 2 * PART_DIMS[part][1]) for part in range(3)]
    slots = plan(where, ids, global_ids)
    here = nears[1][2 * CHIP * PART_ROWS[1] :] + sides[1][2 * CHIP * PART_ROWS[1] :]
    slots, here, asked[2] = lax.optimization_barrier((slots, here, asked[2]))
    if n == 4 * SEG_CHIPS:
        total = swap(here, 16)
    else:
        total = here
        mask = 16
        while mask < n:
            total = total + swap(total, mask)
            mask *= 2

    edge, total, asked[0] = lax.optimization_barrier((edge, total, asked[0]))
    from_x = swap(total, 2)
    sides[0], sides[2] = lax.optimization_barrier((sides[0], sides[2]))
    fars = [
        swap(
            gather(part, 0, CAPS[part], where, asked[part], global_ids, nears[part], sides[part]),
            2 * PART_DIMS[part][2],
        )
        for part in range(3)
    ]
    from_y, from_xy = swap(total, 4), swap(from_x, 4)
    over = flag(here, total)[0] > 0
    over, fars[1], from_x = lax.optimization_barrier((over, fars[1], from_x))
    quads = [total, from_x, from_y, from_xy]

    def send_rest(args):
        asked, nears, sides = args
        return [
            swap(gather(part, CAPS[part], MOST, where, asked[part], global_ids, nears[part], sides[part]), 2 * PART_DIMS[part][2])
            for part in range(3)
        ]

    def send_none(args):
        return list(nothing([flat((MOST - cap) * rows) for cap, rows in zip(CAPS, PART_ROWS)]))

    mores = lax.cond(over, send_rest, send_none, (asked, nears, sides))

    out_mate, q_own, *bufs = attend_mate(
        where, rand_blocks, rand_mate, global_ids, slots, queries, q_mate, nears, sides, fars, mores, quads, edge
    )
    out_got = swap(out_mate, 1)
    out_own = attend_own(where, q_own, bufs)
    return project(core, out_own, out_got, out_weight)


def solution(mesh):
    placed = (P("seq", None), P(None, "seq", None), P("seq", None), P(), P())
    return jax.shard_map(
        local, mesh=mesh, in_specs=placed, out_specs=P("seq", None), check_vma=False
    )
```

```python
import functools
import math

import jax
import jax.numpy as jnp
from jax import lax
from jax.experimental import pallas as pl
from jax.experimental.pallas import tpu as pltpu
from jax.sharding import PartitionSpec as P

HEADS = 8
HEAD_DIM = 128
BLOCK = 128
RAND = 3
GLOB = 2
SEG_CHIPS = 8
HERE = 3
CHIP = 2 * HERE
HALF = HEADS // 2
SLAB = 2 * HALF * BLOCK

CUT_K, CUT_V = 96, 48
PART_ROWS = (256 + CUT_K, 256 + CUT_V, 256 + 2 * BLOCK - CUT_K - CUT_V)
PART_AT = (0, PART_ROWS[0], PART_ROWS[0] + PART_ROWS[1])
PART_DIMS = ((1, 2, 4), (2, 4, 1), (4, 1, 2))
MOST = 2 * SEG_CHIPS + 2 + GLOB
CAPS = (14, 15, 14)
SEG_BLK = SEG_CHIPS * CHIP
IDS = CHIP * RAND
FLAG = IDS
QUARTER = SLAB // 2
NOTE = 16


def swap(value, mask):
    n = lax.axis_size("seq")
    return lax.ppermute(value, "seq", [(i, i ^ mask) for i in range(n)])


def pack_kernel(core_ref, kv_ref, own_ref, mate_ref):
    core = core_ref[0]
    for which, kv_out in ((1 - core, mate_ref), (core, own_ref)):
        first = pl.multiple_of(which * (HALF * HEAD_DIM), HEAD_DIM)

        def unit(pair, block, head, low, high):
            cols = pl.ds(first + head * HEAD_DIM, HEAD_DIM)
            return kv_ref[pair, block * BLOCK + low : block * BLOCK + high, cols]

        for block in range(HERE):
            for part in range(3):
                at = PART_AT[part]
                kv_out[block, at : at + BLOCK] = unit(0, block, part, 0, BLOCK)
                kv_out[block, at + BLOCK : at + 2 * BLOCK] = unit(1, block, part, 0, BLOCK)
            last = HALF - 1
            a, b, c = (at + 2 * BLOCK for at in PART_AT)
            kv_out[block, a : a + CUT_K] = unit(0, block, last, 0, CUT_K)
            kv_out[block, b : b + CUT_V] = unit(1, block, last, 0, CUT_V)
            mid = c + BLOCK - CUT_K
            kv_out[block, c:mid] = unit(0, block, last, CUT_K, BLOCK)
            kv_out[block, mid : mid + BLOCK - CUT_V] = unit(1, block, last, CUT_V, BLOCK)


def pack(core, keys_values):
    slab = jax.ShapeDtypeStruct((HERE, SLAB, HEAD_DIM), jnp.bfloat16)
    vmem = pl.BlockSpec(memory_space=pltpu.VMEM)
    return pl.pallas_call(
        pack_kernel,
        out_shape=(slab, slab),
        in_specs=[pl.BlockSpec(memory_space=pltpu.SMEM), vmem],
        out_specs=(vmem,) * 2,
        compiler_params=pltpu.CompilerParams(vmem_limit_bytes=4 * 2**20),
    )(core.reshape(1), keys_values)


def in_segment(where, block):
    inside = block - (where[2] - where[0]) * CHIP
    return jnp.where(jnp.logical_and(inside >= 0, inside < SEG_BLK), inside, -1)


def list_wants(where, ids, globs, chip, part, slots, base, act):
    dim = PART_DIMS[part][2]

    @pl.loop(0, SEG_BLK)
    def _(k):
        slots[base + k] = -1

    def add(block, count):
        place = base + block
        new = jnp.logical_and(((block // CHIP) ^ chip) & dim != 0, slots[place] < 0)

        @pl.when(new)
        def _():
            slots[place] = count
            if act is not None:
                act(block, count)

        return count + new.astype(jnp.int32)

    count = lax.fori_loop(0, IDS, lambda k, c: add(ids[k], c), jnp.int32(0))
    low, high = chip * CHIP - 1, chip * CHIP + CHIP
    count = add(jnp.where(chip == 0, chip * CHIP, low), count)
    count = add(jnp.where(chip == SEG_CHIPS - 1, chip * CHIP, high), count)
    for g in range(GLOB):
        block = in_segment(where, globs[g])
        count = add(jnp.where(block < 0, chip * CHIP, block), count)
    return count


def half_queries_kernel(where_ref, q_ref, out_ref, sem):
    width = HALF * HEAD_DIM
    cols = pl.ds(pl.multiple_of((1 - where_ref[1]) * width, width), width)
    copy = pltpu.make_async_copy(q_ref.at[:, cols], out_ref, sem)
    copy.start()
    copy.wait()


def half_queries(where, queries):
    return pl.pallas_call(
        half_queries_kernel,
        out_shape=jax.ShapeDtypeStruct((queries.shape[0], HALF * HEAD_DIM), queries.dtype),
        in_specs=[pl.BlockSpec(memory_space=pltpu.SMEM), pl.BlockSpec(memory_space=pltpu.HBM)],
        out_specs=pl.BlockSpec(memory_space=pltpu.VMEM),
        scratch_shapes=[pltpu.SemaphoreType.DMA],
        compiler_params=pltpu.CompilerParams(vmem_limit_bytes=2 * 2**20),
    )(where, pltpu.with_memory_space_constraint(queries, pltpu.HBM))


def split_kernel(where_ref, glob_ref, ids_ref, own_ref, got_ref, to_x, to_y, to_z, to_xy, mine, edge):
    chip, core, chip_all = where_ref[0], where_ref[1], where_ref[2]
    lane = lax.broadcasted_iota(jnp.int32, (NOTE, HEAD_DIM), 1)
    wanted = lane == jnp.where(chip == 0, -1, chip * CHIP - 1)
    wanted = jnp.logical_or(wanted, lane == jnp.where(chip == SEG_CHIPS - 1, -1, chip * CHIP + CHIP))
    for g in range(GLOB):
        wanted = jnp.logical_or(wanted, lane == in_segment(where_ref, glob_ref[g]))
    row = jnp.zeros((NOTE, HEAD_DIM), jnp.int32)
    for k in range(IDS):
        wanted = jnp.logical_or(wanted, lane == ids_ref[k])
        row = jnp.where(lane == k, ids_ref[k], row)
    apart = jnp.zeros((NOTE, HEAD_DIM), jnp.int32)
    for k in range(1, SEG_CHIPS):
        apart += (lane >= k * CHIP).astype(jnp.int32)
    apart = apart ^ chip
    over = jnp.zeros((NOTE, 1), jnp.float32)
    for part in range(3):
        far = jnp.logical_and(wanted, apart & PART_DIMS[part][2] != 0)
        count = jnp.sum(jnp.where(far, 1.0, 0.0), axis=1, keepdims=True)
        over = jnp.maximum(over, jnp.where(count > CAPS[part], 1.0, 0.0))
    note = jnp.where(lane == FLAG, over, row.astype(jnp.float32)).astype(jnp.bfloat16)

    def write(out, at, k):
        x, y = chip & 1, (chip >> 1) & 1
        block = glob_ref[x ^ (k & 1)]
        half = y ^ (k >> 1)
        owner = block // CHIP
        inside = block - owner * CHIP
        place = lax.rem(inside, HERE)
        rows = pl.ds(pl.multiple_of(half * QUARTER, QUARTER), QUARTER)
        here = owner == chip_all
        mate = (inside // HERE) != core

        @pl.when(jnp.logical_and(here, jnp.logical_not(mate)))
        def _():
            out[at : at + QUARTER] = own_ref[place, rows]

        @pl.when(jnp.logical_and(here, mate))
        def _():
            out[at : at + QUARTER] = got_ref[place, rows]

        @pl.when(jnp.logical_not(here))
        def _():
            out[at : at + QUARTER] = jnp.zeros((QUARTER, HEAD_DIM), jnp.bfloat16)

        out[at + QUARTER : at + QUARTER + NOTE] = note

    for part, out in enumerate((to_x, to_y, to_z)):
        size = PART_ROWS[part]
        for block in range(HERE):
            out[block * size : (block + 1) * size] = own_ref[block, PART_AT[part] : PART_AT[part] + size]
            low = (HERE + block) * size
            out[low : low + size] = got_ref[block, PART_AT[part] : PART_AT[part] + size]
    write(to_x, CHIP * PART_ROWS[0], 1)
    write(to_y, CHIP * PART_ROWS[1], 2)
    to_z[CHIP * PART_ROWS[2] : CHIP * PART_ROWS[2] + NOTE] = note
    write(to_xy, 0, 3)
    write(mine, 0, 0)
    last = chip == SEG_CHIPS - 1

    @pl.when(last == (core == 1))
    def _():
        edge[...] = own_ref[jnp.where(last, HERE - 1, 0)]

    @pl.when(last != (core == 1))
    def _():
        edge[...] = got_ref[jnp.where(last, HERE - 1, 0)]


def flat(rows):
    return jax.ShapeDtypeStruct((rows, HEAD_DIM), jnp.bfloat16)


def split(where, global_ids, ids, own, got):
    smem = pl.BlockSpec(memory_space=pltpu.SMEM)
    vmem = pl.BlockSpec(memory_space=pltpu.VMEM)
    sizes = [CHIP * rows for rows in PART_ROWS]
    return pl.pallas_call(
        split_kernel,
        out_shape=[
            flat(sizes[0] + QUARTER + NOTE), flat(sizes[1] + QUARTER + NOTE), flat(sizes[2] + NOTE),
            flat(QUARTER + NOTE), flat(QUARTER + NOTE), flat(SLAB),
        ],
        in_specs=[smem] * 3 + [vmem] * 2,
        out_specs=[vmem] * 6,
        compiler_params=pltpu.CompilerParams(vmem_limit_bytes=6 * 2**20),
    )(where, global_ids, ids, own, got)


def join_kernel(sent_x, sent_y, sent_z, mine, from_x, from_y, from_z, from_xy, near0, near1, near2):
    for part, (sent, got, near) in enumerate(
        ((sent_x, from_x, near0), (sent_y, from_y, near1), (sent_z, from_z, near2))
    ):
        size = CHIP * PART_ROWS[part]
        near[0:size] = sent[0:size]
        near[size : 2 * size] = got[0:size]
    x, y = CHIP * PART_ROWS[0], CHIP * PART_ROWS[1]
    total = mine[...] + (from_x[x : x + QUARTER + NOTE] + from_y[y : y + QUARTER + NOTE] + from_xy[...])
    near1[2 * y : 2 * y + QUARTER + NOTE] = total


def join(sent, mine, got):
    vmem = pl.BlockSpec(memory_space=pltpu.VMEM)
    return pl.pallas_call(
        join_kernel,
        out_shape=[flat(2 * CHIP * rows + (QUARTER + NOTE if part == 1 else 0)) for part, rows in enumerate(PART_ROWS)],
        in_specs=[vmem] * 8,
        out_specs=[vmem] * 3,
        compiler_params=pltpu.CompilerParams(vmem_limit_bytes=9 * 2**20),
    )(*sent, mine, *got)


def plan_kernel(where_ref, ids_ref, glob_ref, slots):
    for part in range(3):
        list_wants(where_ref, ids_ref, glob_ref, where_ref[0], part, slots, part * SEG_BLK, None)


def plan(where, ids, global_ids):
    smem = pl.BlockSpec(memory_space=pltpu.SMEM)
    return pl.pallas_call(
        plan_kernel,
        out_shape=jax.ShapeDtypeStruct((3 * SEG_BLK,), jnp.int32),
        in_specs=[smem] * 3,
        out_specs=smem,
        compiler_params=pltpu.CompilerParams(vmem_limit_bytes=2**20),
    )(where, ids, global_ids)


def gather_kernel(part, low, high, where_ref, ids_ref, glob_ref, near, side, out_ref, slots):
    chip, core = where_ref[0], where_ref[1]
    d1, d2, d3 = PART_DIMS[part]
    size = PART_ROWS[part]

    def act(block, count):
        there = block // CHIP
        inside = block - there * CHIP
        apart = there ^ chip
        place = jnp.where(apart & d1 != 0, CHIP, 0)
        place += ((inside // HERE) ^ core) * HERE + lax.rem(inside, HERE)
        go = jnp.logical_and(count >= low, count < high)
        at = jnp.clip(count - low, 0, high - low - 1)
        target = pl.ds(pl.multiple_of(at * size, 16), size)
        source = pl.ds(pl.multiple_of(place * size, 16), size)

        @pl.when(jnp.logical_and(go, apart & d2 == 0))
        def _():
            out_ref[target] = near[source]

        @pl.when(jnp.logical_and(go, apart & d2 != 0))
        def _():
            out_ref[target] = side[source]

    list_wants(where_ref, ids_ref, glob_ref, chip ^ d3, part, slots, 0, act)


def gather(part, low, high, where, ids, global_ids, near, side):
    smem = pl.BlockSpec(memory_space=pltpu.SMEM)
    vmem = pl.BlockSpec(memory_space=pltpu.VMEM)
    return pl.pallas_call(
        functools.partial(gather_kernel, part, low, high),
        out_shape=flat((high - low) * PART_ROWS[part]),
        in_specs=[smem] * 3 + [vmem] * 2,
        out_specs=vmem,
        scratch_shapes=[pltpu.SMEM((SEG_BLK,), jnp.int32)],
        compiler_params=pltpu.CompilerParams(vmem_limit_bytes=5 * 2**20),
    )(where, ids, global_ids, near, side)


def flag_kernel(here, there, over, notes, sem):
    rows = pl.ds(QUARTER, NOTE)
    copies = [pltpu.make_async_copy(v.at[rows], notes.at[k], sem.at[k]) for k, v in enumerate((here, there))]
    for one in copies:
        one.start()
    for one in copies:
        one.wait()
    flags = notes[...].astype(jnp.float32)
    lane = lax.broadcasted_iota(jnp.int32, flags.shape, 2)
    over[0] = (jnp.max(jnp.where(lane == FLAG, flags, 0.0)) > 0).astype(jnp.int32)


def flag(here, there):
    anywhere = pl.BlockSpec(memory_space=pl.ANY)
    return pl.pallas_call(
        flag_kernel,
        out_shape=jax.ShapeDtypeStruct((1,), jnp.int32),
        in_specs=[anywhere] * 2,
        out_specs=pl.BlockSpec(memory_space=pltpu.SMEM),
        scratch_shapes=[pltpu.VMEM((2, NOTE, HEAD_DIM), jnp.bfloat16), pltpu.SemaphoreType.DMA((2,))],
        compiler_params=pltpu.CompilerParams(vmem_limit_bytes=2**20),
    )(here, there)


def nothing(shapes):
    return pl.pallas_call(
        lambda *refs: None,
        out_shape=shapes,
        out_specs=[pl.BlockSpec(memory_space=pl.ANY)] * len(shapes),
        compiler_params=pltpu.CompilerParams(vmem_limit_bytes=2**20),
    )()


OUTER, INNER, OWN, GLOBAL, RANDOM = 0, 1, 2, 2 + HERE, 2 + HERE + GLOB
N_ENTRY = RANDOM + HERE * RAND


def rows_of(ref, part, place, count=1):
    size = PART_ROWS[part]
    return ref.at[pl.ds(pl.multiple_of(place * size, 16), count * size)]


def collect(mine, where_ref, rand_ref, glob_ref, slots_ref, sources, bufs, sems):
    chip, core = where_ref[0], where_ref[1]
    nears, sides, fars, mores, quads, edge = sources
    half = core if mine else 1 - core
    base = 0 if mine else HERE

    def slot_of(block):
        return ((block // HERE) ^ core) * HERE + lax.rem(block, HERE)

    def copy(ref, part, place, entry, sem, count=1):
        source, target = rows_of(ref, part, place, count), rows_of(bufs[part], part, entry, count)
        pltpu.make_async_copy(source, target, sem).start()

    def fetch(block, entry, sem):
        there = block // CHIP
        slot = slot_of(block - there * CHIP)
        apart = chip ^ there
        for part in range(3):
            d1, d2, d3 = PART_DIMS[part]
            b1 = jnp.where(apart & d1 != 0, CHIP, 0)
            b2 = apart & d2 != 0
            b3 = apart & d3 != 0

            @pl.when(jnp.logical_and(jnp.logical_not(b2), jnp.logical_not(b3)))
            def _():
                copy(nears[part], part, b1 + slot, entry, sem)

            @pl.when(jnp.logical_and(b2, jnp.logical_not(b3)))
            def _():
                copy(sides[part], part, b1 + slot, entry, sem)

            cap = CAPS[part]
            place = slots_ref[part * SEG_BLK + block]

            @pl.when(jnp.logical_and(b3, place < cap))
            def _():
                copy(fars[part], part, jnp.clip(place, 0, cap - 1), entry, sem)

            @pl.when(jnp.logical_and(b3, place >= cap))
            def _():
                copy(mores[part], part, jnp.clip(place - cap, 0, MOST - cap - 1), entry, sem)

    def fetch_rows(source, low, high, entry, sem):
        for part in range(3):
            a, b = max(low, PART_AT[part]), min(high, PART_AT[part] + PART_ROWS[part])
            if a < b:
                at = pl.multiple_of(entry * PART_ROWS[part], 16) + a - PART_AT[part]
                to = bufs[part].at[pl.ds(pl.multiple_of(at, 16), b - a)]
                pltpu.make_async_copy(source.at[pl.ds(a - low, b - a)], to, sem).start()

    shared = sems.at[HERE]
    for part in range(3):
        copy(nears[part], part, base, OWN, shared, HERE)
        copy(nears[part], part, (HERE - base) + jnp.where(half == 0, 0, HERE - 1), INNER, shared)
    at_edge = chip == jnp.where(half == 0, 0, SEG_CHIPS - 1)

    @pl.when(at_edge)
    def _():
        fetch_rows(edge, 0, SLAB, OUTER, shared)

    @pl.when(jnp.logical_not(at_edge))
    def _():
        fetch(chip * CHIP + jnp.where(half == 0, -1, CHIP), OUTER, shared)

    for g in range(GLOB):
        block = in_segment(where_ref, glob_ref[g])

        @pl.when(block >= 0)
        def _():
            fetch(jnp.maximum(block, 0), GLOBAL + g, shared)

    for k in range(4):
        g = (chip & 1) ^ (k & 1)
        entry = GLOBAL + g
        row = ((chip >> 1) & 1) ^ (k >> 1)
        outside = in_segment(where_ref, glob_ref[g]) < 0
        for value in range(2):

            @pl.when(jnp.logical_and(outside, row == value))
            def _():
                fetch_rows(quads[k], value * QUARTER, (value + 1) * QUARTER, entry, shared)

    for row in range(HERE):
        for k in range(RAND):
            fetch(rand_ref[row, k], RANDOM + row * RAND + k, sems.at[row])

    def wait(low, count, sem):
        for part in range(3):
            of = rows_of(bufs[part], part, low, count)
            pltpu.make_async_copy(rows_of(nears[part], part, 0, count), of, sem).wait()

    return [lambda row=row: wait(RANDOM, RAND, sems.at[row]) for row in range(HERE)] + [
        lambda: wait(0, RANDOM, shared)
    ]


def attend_rows(mine, core, q_ref, bufs, out_ref, waits):
    outer_first = (core if mine else 1 - core) == 0
    factor = math.log2(math.e) / math.sqrt(HEAD_DIM)
    tail, mid = 2 * BLOCK, 3 * BLOCK - CUT_K

    def rows(part, entry, low, high):
        return bufs[part][pl.ds(pl.multiple_of(entry * PART_ROWS[part] + low, 16), high - low)]

    for row in range(HERE):
        if waits:
            waits[row]()
        before = OWN + row - 1 if row else jnp.where(outer_first, OUTER, INNER)
        after = OWN + row + 1 if row < HERE - 1 else jnp.where(outer_first, INNER, OUTER)
        at = RANDOM + row * RAND
        entries = [before, OWN + row, after, GLOBAL, GLOBAL + 1, at, at + 1, at + 2]
        keys, values = [], []
        for head in range(HALF - 1):
            keys.append([rows(head, i, 0, BLOCK) for i in entries])
            values.append([rows(head, i, BLOCK, 2 * BLOCK) for i in entries])
        keys.append([v for i in entries for v in (rows(0, i, tail, tail + CUT_K), rows(2, i, tail, mid))])
        values.append(
            [v for i in entries for v in (rows(1, i, tail, tail + CUT_V), rows(2, i, mid, PART_ROWS[2]))]
        )
        scores = [
            lax.dot_general(
                q_ref[row * BLOCK : (row + 1) * BLOCK, h * HEAD_DIM : (h + 1) * HEAD_DIM],
                jnp.concatenate(keys[h], axis=0),
                (((1,), (1,)), ((), ())),
                preferred_element_type=jnp.float32,
            )
            for h in range(HALF)
        ]
        probs = []
        for h in range(HALF):
            top = jnp.max(scores[h], axis=-1, keepdims=True)
            one = jnp.exp2((scores[h] - top) * factor)
            one = one * (1.0 / jnp.sum(one, axis=-1, keepdims=True))
            probs.append(one.astype(jnp.bfloat16))
        for h in range(HALF):
            mixed = jnp.dot(probs[h], jnp.concatenate(values[h], axis=0), preferred_element_type=jnp.float32)
            out_ref[row * BLOCK : (row + 1) * BLOCK, h * HEAD_DIM : (h + 1) * HEAD_DIM] = mixed.astype(jnp.bfloat16)


def mate_kernel(
    where_ref, rand_ref, rand_mate_ref, glob_ref, slots_ref, q_ref, q_mate_ref,
    near0, near1, near2, side0, side1, side2, far0, far1, far2, more0, more1, more2,
    quad, quad_x, quad_y, quad_xy, edge,
    out_ref, q_out, own0, own1, own2, buf0, buf1, buf2, q_buf, sems, own_sems, q_sems,
):
    core = where_ref[1]
    width = HALF * HEAD_DIM
    cols = pl.ds(pl.multiple_of(core * width, width), width)
    q_copy = pltpu.make_async_copy(q_mate_ref, q_buf, q_sems.at[0])
    q_own = pltpu.make_async_copy(q_ref.at[:, cols], q_out, q_sems.at[1])
    q_copy.start()
    sources = (
        (near0, near1, near2), (side0, side1, side2), (far0, far1, far2), (more0, more1, more2),
        (quad, quad_x, quad_y, quad_xy), edge,
    )
    bufs, own_bufs = (buf0, buf1, buf2), (own0, own1, own2)
    waits = collect(False, where_ref, rand_mate_ref, glob_ref, slots_ref, sources, bufs, sems)
    q_own.start()
    own_waits = collect(True, where_ref, rand_ref, glob_ref, slots_ref, sources, own_bufs, own_sems)
    q_copy.wait()
    waits[HERE]()
    attend_rows(False, core, q_buf, bufs, out_ref, waits)
    q_own.wait()
    for one in own_waits:
        one()


def own_kernel(where_ref, q_ref, buf0, buf1, buf2, out_ref):
    attend_rows(True, where_ref[1], q_ref, (buf0, buf1, buf2), out_ref, None)


def in_hbm(*arrays):
    return [pltpu.with_memory_space_constraint(v, pltpu.HBM) for v in arrays]


def attend_mate(where, rand, rand_mate, global_ids, slots, q, q_mate, nears, sides, fars, mores, quads, edge):
    vmem = pl.BlockSpec(memory_space=pltpu.VMEM)
    smem = pl.BlockSpec(memory_space=pltpu.SMEM)
    hbm = pl.BlockSpec(memory_space=pltpu.HBM)
    out = jax.ShapeDtypeStruct((HERE * BLOCK, HALF * HEAD_DIM), jnp.bfloat16)
    flops = HERE * BLOCK * HALF * (RANDOM + RAND) * BLOCK * HEAD_DIM * 4
    return pl.pallas_call(
        mate_kernel,
        out_shape=[out, out] + [flat(N_ENTRY * rows) for rows in PART_ROWS],
        in_specs=[smem] * 5 + [hbm] * 19,
        out_specs=[vmem] * 5,
        scratch_shapes=[pltpu.VMEM((N_ENTRY * rows, HEAD_DIM), jnp.bfloat16) for rows in PART_ROWS]
        + [
            pltpu.VMEM(out.shape, jnp.bfloat16),
            pltpu.SemaphoreType.DMA((HERE + 1,)),
            pltpu.SemaphoreType.DMA((HERE + 1,)),
            pltpu.SemaphoreType.DMA((2,)),
        ],
        compiler_params=pltpu.CompilerParams(vmem_limit_bytes=24 * 2**20),
        cost_estimate=pl.CostEstimate(flops=flops, bytes_accessed=N_ENTRY * SLAB * 512, transcendentals=0),
    )(where, rand, rand_mate, global_ids, slots, *in_hbm(q, q_mate, *nears, *sides, *fars, *mores, *quads, edge))


def attend_own(where, q, bufs):
    vmem = pl.BlockSpec(memory_space=pltpu.VMEM)
    flops = HERE * BLOCK * HALF * (RANDOM + RAND) * BLOCK * HEAD_DIM * 4
    return pl.pallas_call(
        own_kernel,
        out_shape=jax.ShapeDtypeStruct((HERE * BLOCK, HALF * HEAD_DIM), jnp.bfloat16),
        in_specs=[pl.BlockSpec(memory_space=pltpu.SMEM)] + [vmem] * 4,
        out_specs=vmem,
        compiler_params=pltpu.CompilerParams(vmem_limit_bytes=20 * 2**20),
        cost_estimate=pl.CostEstimate(flops=flops, bytes_accessed=N_ENTRY * SLAB * 256, transcendentals=0),
    )(where, q, *bufs)


def project_kernel(tiles, core_ref, own_ref, got_ref, weight_ref, out_ref, tile_ref, sems):
    core = core_ref[0]
    half = HALF * HEAD_DIM
    width = out_ref.shape[1] // tiles
    mine = pl.ds(pl.multiple_of(core * half, half), half)
    other = pl.ds(pl.multiple_of((1 - core) * half, half), half)
    copies = []
    for k in range(tiles):
        cols = pl.ds(k * width, width)
        total = jnp.dot(own_ref[...], weight_ref[mine, cols], preferred_element_type=jnp.float32)
        total += jnp.dot(got_ref[...], weight_ref[other, cols], preferred_element_type=jnp.float32)
        tile_ref[k] = total.astype(out_ref.dtype)
        copies.append(pltpu.make_async_copy(tile_ref.at[k], out_ref.at[:, cols], sems.at[k]))
        copies[k].start()
    for one in copies:
        one.wait()


def project(core, own, got, weight, tiles=4):
    width = weight.shape[1]
    rows = own.shape[0]
    vmem = pl.BlockSpec(memory_space=pltpu.VMEM)
    return pl.pallas_call(
        functools.partial(project_kernel, tiles),
        out_shape=jax.ShapeDtypeStruct((rows, width), jnp.bfloat16),
        in_specs=[pl.BlockSpec(memory_space=pltpu.SMEM), vmem, vmem, vmem],
        out_specs=pl.BlockSpec(memory_space=pl.ANY),
        scratch_shapes=[pltpu.VMEM((tiles, rows, width // tiles), jnp.bfloat16), pltpu.SemaphoreType.DMA((tiles,))],
        compiler_params=pltpu.CompilerParams(vmem_limit_bytes=14 * 2**20),
    )(core.reshape(1), own, got, weight)


def local(queries, keys_values, rand_blocks, global_ids, out_weight):
    n = lax.axis_size("seq")
    device = lax.axis_index("seq")
    core = device % 2
    chip = (device // 2) % SEG_CHIPS
    where = jnp.stack([chip, core, device // 2])
    rand_mate = swap(rand_blocks, 1)
    own, mate = pack(core, keys_values)
    got = swap(mate, 1)
    ids = jnp.concatenate([rand_blocks.reshape(-1), rand_mate.reshape(-1)])
    *sent, to_xy, mine, border = split(where, global_ids, ids, own, got)

    pairs = []
    chips = n // 2
    for c in range(chips):
        if c % SEG_CHIPS == SEG_CHIPS - 1:
            pairs += [(2 * c + k, 2 * ((c + 1) % chips) + k) for k in range(2)]
        if c % SEG_CHIPS == 0:
            pairs += [(2 * c + k, 2 * ((c - 1) % chips) + k) for k in range(2)]
    edge = lax.ppermute(border, "seq", pairs)
    q_mate = swap(half_queries(where, queries), 1)
    got = [swap(v, 2 * PART_DIMS[part][0]) for part, v in enumerate(sent)] + [swap(to_xy, 6)]
    got, q_mate = lax.optimization_barrier((got, q_mate))
    nears = join(sent, mine, got)
    asked = [got[k][CHIP * PART_ROWS[k] + more, :IDS].astype(jnp.int32) for k, more in ((2, 0), (0, QUARTER), (1, QUARTER))]

    sides = [swap(nears[part], 2 * PART_DIMS[part][1]) for part in range(3)]
    slots = plan(where, ids, global_ids)
    here = nears[1][2 * CHIP * PART_ROWS[1] :] + sides[1][2 * CHIP * PART_ROWS[1] :]
    slots, here, asked[2] = lax.optimization_barrier((slots, here, asked[2]))
    if n == 4 * SEG_CHIPS:
        total = swap(here, 16)
    else:
        total = here
        mask = 16
        while mask < n:
            total = total + swap(total, mask)
            mask *= 2

    edge, total, asked[0] = lax.optimization_barrier((edge, total, asked[0]))
    from_x = swap(total, 2)
    sides[0], sides[2] = lax.optimization_barrier((sides[0], sides[2]))
    fars = [
        swap(
            gather(part, 0, CAPS[part], where, asked[part], global_ids, nears[part], sides[part]),
            2 * PART_DIMS[part][2],
        )
        for part in range(3)
    ]
    from_y, from_xy = swap(total, 4), swap(from_x, 4)
    over = flag(here, total)[0] > 0
    over, fars[1], from_x = lax.optimization_barrier((over, fars[1], from_x))
    quads = [total, from_x, from_y, from_xy]

    def send_rest(args):
        asked, nears, sides = args
        return [
            swap(gather(part, CAPS[part], MOST, where, asked[part], global_ids, nears[part], sides[part]), 2 * PART_DIMS[part][2])
            for part in range(3)
        ]

    def send_none(args):
        return list(nothing([flat((MOST - cap) * rows) for cap, rows in zip(CAPS, PART_ROWS)]))

    mores = lax.cond(over, send_rest, send_none, (asked, nears, sides))

    out_mate, q_own, *bufs = attend_mate(
        where, rand_blocks, rand_mate, global_ids, slots, queries, q_mate, nears, sides, fars, mores, quads, edge
    )
    out_got = swap(out_mate, 1)
    out_own = attend_own(where, q_own, bufs)
    return project(core, out_own, out_got, out_weight)


def solution(mesh):
    placed = (P("seq", None), P(None, "seq", None), P("seq", None), P(), P())
    return jax.shard_map(
        local, mesh=mesh, in_specs=placed, out_specs=P("seq", None), check_vma=False
    )
```

```python
import functools
import math

import jax
import jax.numpy as jnp
from jax import lax
from jax.experimental import pallas as pl
from jax.experimental.pallas import tpu as pltpu
from jax.sharding import PartitionSpec as P

HEADS = 8
HEAD_DIM = 128
BLOCK = 128
RAND = 3
GLOB = 2
SEG_CHIPS = 8
HERE = 3
CHIP = 2 * HERE
HALF = HEADS // 2
SLAB = 2 * HALF * BLOCK

CUT_K, CUT_V = 96, 48
PART_ROWS = (256 + CUT_K, 256 + CUT_V, 256 + 2 * BLOCK - CUT_K - CUT_V)
PART_AT = (0, PART_ROWS[0], PART_ROWS[0] + PART_ROWS[1])
PART_DIMS = ((1, 2, 4), (2, 4, 1), (4, 1, 2))
MOST = 2 * SEG_CHIPS + 2 + GLOB
CAPS = (14, 15, 14)
SEG_BLK = SEG_CHIPS * CHIP
IDS = CHIP * RAND
FLAG = IDS
QUARTER = SLAB // 2
NOTE = 16


def swap(value, mask):
    n = lax.axis_size("seq")
    return lax.ppermute(value, "seq", [(i, i ^ mask) for i in range(n)])


def pack_kernel(mine, where_ref, kv_ref, out_ref, half_ref, sems):
    core = where_ref[1]
    width = HALF * HEAD_DIM
    cols = pl.ds(pl.multiple_of((core if mine else 1 - core) * width, width), width)
    copies = []
    for block in range(HERE):
        rows = pl.ds(block * BLOCK, BLOCK)
        copies.append(pltpu.make_async_copy(kv_ref.at[:, rows, cols], half_ref.at[block], sems.at[block]))
        copies[block].start()

    def unit(pair, block, head, low, high):
        return half_ref[block, pair, low:high, head * HEAD_DIM : (head + 1) * HEAD_DIM]

    for block in range(HERE):
        copies[block].wait()
        for part in range(3):
            at = PART_AT[part]
            out_ref[block, at : at + BLOCK] = unit(0, block, part, 0, BLOCK)
            out_ref[block, at + BLOCK : at + 2 * BLOCK] = unit(1, block, part, 0, BLOCK)
        last = HALF - 1
        a, b, c = (at + 2 * BLOCK for at in PART_AT)
        out_ref[block, a : a + CUT_K] = unit(0, block, last, 0, CUT_K)
        out_ref[block, b : b + CUT_V] = unit(1, block, last, 0, CUT_V)
        mid = c + BLOCK - CUT_K
        out_ref[block, c:mid] = unit(0, block, last, CUT_K, BLOCK)
        out_ref[block, mid : mid + BLOCK - CUT_V] = unit(1, block, last, CUT_V, BLOCK)


def pack(mine, where, keys_values):
    return pl.pallas_call(
        functools.partial(pack_kernel, mine),
        out_shape=jax.ShapeDtypeStruct((HERE, SLAB, HEAD_DIM), jnp.bfloat16),
        in_specs=[pl.BlockSpec(memory_space=pltpu.SMEM), pl.BlockSpec(memory_space=pltpu.HBM)],
        out_specs=pl.BlockSpec(memory_space=pltpu.VMEM),
        scratch_shapes=[
            pltpu.VMEM((HERE, 2, BLOCK, HALF * HEAD_DIM), jnp.bfloat16),
            pltpu.SemaphoreType.DMA((HERE,)),
        ],
        compiler_params=pltpu.CompilerParams(vmem_limit_bytes=4 * 2**20),
    )(where, pltpu.with_memory_space_constraint(keys_values, pltpu.HBM))


def in_segment(where, block):
    inside = block - (where[2] - where[0]) * CHIP
    return jnp.where(jnp.logical_and(inside >= 0, inside < SEG_BLK), inside, -1)


def list_wants(where, ids, globs, chip, part, slots, base, act):
    dim = PART_DIMS[part][2]

    @pl.loop(0, SEG_BLK)
    def _(k):
        slots[base + k] = -1

    def add(block, count):
        place = base + block
        new = jnp.logical_and(((block // CHIP) ^ chip) & dim != 0, slots[place] < 0)

        @pl.when(new)
        def _():
            slots[place] = count
            if act is not None:
                act(block, count)

        return count + new.astype(jnp.int32)

    count = lax.fori_loop(0, IDS, lambda k, c: add(ids[k], c), jnp.int32(0))
    low, high = chip * CHIP - 1, chip * CHIP + CHIP
    count = add(jnp.where(chip == 0, chip * CHIP, low), count)
    count = add(jnp.where(chip == SEG_CHIPS - 1, chip * CHIP, high), count)
    for g in range(GLOB):
        block = in_segment(where, globs[g])
        count = add(jnp.where(block < 0, chip * CHIP, block), count)
    return count


def half_queries_kernel(where_ref, q_ref, out_ref, sem):
    width = HALF * HEAD_DIM
    cols = pl.ds(pl.multiple_of((1 - where_ref[1]) * width, width), width)
    copy = pltpu.make_async_copy(q_ref.at[:, cols], out_ref, sem)
    copy.start()
    copy.wait()


def half_queries(where, queries):
    return pl.pallas_call(
        half_queries_kernel,
        out_shape=jax.ShapeDtypeStruct((queries.shape[0], HALF * HEAD_DIM), queries.dtype),
        in_specs=[pl.BlockSpec(memory_space=pltpu.SMEM), pl.BlockSpec(memory_space=pltpu.HBM)],
        out_specs=pl.BlockSpec(memory_space=pltpu.VMEM),
        scratch_shapes=[pltpu.SemaphoreType.DMA],
        compiler_params=pltpu.CompilerParams(vmem_limit_bytes=2 * 2**20),
    )(where, pltpu.with_memory_space_constraint(queries, pltpu.HBM))


def split_kernel(where_ref, glob_ref, ids_ref, own_ref, got_ref, to_x, to_y, to_z, to_xy, mine, edge):
    chip, core, chip_all = where_ref[0], where_ref[1], where_ref[2]
    lane = lax.broadcasted_iota(jnp.int32, (NOTE, HEAD_DIM), 1)
    wanted = lane == jnp.where(chip == 0, -1, chip * CHIP - 1)
    wanted = jnp.logical_or(wanted, lane == jnp.where(chip == SEG_CHIPS - 1, -1, chip * CHIP + CHIP))
    for g in range(GLOB):
        wanted = jnp.logical_or(wanted, lane == in_segment(where_ref, glob_ref[g]))
    row = jnp.zeros((NOTE, HEAD_DIM), jnp.int32)
    for k in range(IDS):
        wanted = jnp.logical_or(wanted, lane == ids_ref[k])
        row = jnp.where(lane == k, ids_ref[k], row)
    apart = jnp.zeros((NOTE, HEAD_DIM), jnp.int32)
    for k in range(1, SEG_CHIPS):
        apart += (lane >= k * CHIP).astype(jnp.int32)
    apart = apart ^ chip
    over = jnp.zeros((NOTE, 1), jnp.float32)
    for part in range(3):
        far = jnp.logical_and(wanted, apart & PART_DIMS[part][2] != 0)
        count = jnp.sum(jnp.where(far, 1.0, 0.0), axis=1, keepdims=True)
        over = jnp.maximum(over, jnp.where(count > CAPS[part], 1.0, 0.0))
    note = jnp.where(lane == FLAG, over, row.astype(jnp.float32)).astype(jnp.bfloat16)

    def write(out, at, k):
        x, y = chip & 1, (chip >> 1) & 1
        block = glob_ref[x ^ (k & 1)]
        half = y ^ (k >> 1)
        owner = block // CHIP
        inside = block - owner * CHIP
        place = lax.rem(inside, HERE)
        rows = pl.ds(pl.multiple_of(half * QUARTER, QUARTER), QUARTER)
        here = owner == chip_all
        mate = (inside // HERE) != core

        @pl.when(jnp.logical_and(here, jnp.logical_not(mate)))
        def _():
            out[at : at + QUARTER] = own_ref[place, rows]

        @pl.when(jnp.logical_and(here, mate))
        def _():
            out[at : at + QUARTER] = got_ref[place, rows]

        @pl.when(jnp.logical_not(here))
        def _():
            out[at : at + QUARTER] = jnp.zeros((QUARTER, HEAD_DIM), jnp.bfloat16)

        out[at + QUARTER : at + QUARTER + NOTE] = note

    for part, out in enumerate((to_x, to_y, to_z)):
        size = PART_ROWS[part]
        for block in range(HERE):
            out[block * size : (block + 1) * size] = own_ref[block, PART_AT[part] : PART_AT[part] + size]
            low = (HERE + block) * size
            out[low : low + size] = got_ref[block, PART_AT[part] : PART_AT[part] + size]
    write(to_x, CHIP * PART_ROWS[0], 1)
    write(to_y, CHIP * PART_ROWS[1], 2)
    to_z[CHIP * PART_ROWS[2] : CHIP * PART_ROWS[2] + NOTE] = note
    write(to_xy, 0, 3)
    write(mine, 0, 0)
    last = chip == SEG_CHIPS - 1

    @pl.when(last == (core == 1))
    def _():
        edge[...] = own_ref[jnp.where(last, HERE - 1, 0)]

    @pl.when(last != (core == 1))
    def _():
        edge[...] = got_ref[jnp.where(last, HERE - 1, 0)]


def flat(rows):
    return jax.ShapeDtypeStruct((rows, HEAD_DIM), jnp.bfloat16)


def split(where, global_ids, ids, own, got):
    smem = pl.BlockSpec(memory_space=pltpu.SMEM)
    vmem = pl.BlockSpec(memory_space=pltpu.VMEM)
    sizes = [CHIP * rows for rows in PART_ROWS]
    return pl.pallas_call(
        split_kernel,
        out_shape=[
            flat(sizes[0] + QUARTER + NOTE), flat(sizes[1] + QUARTER + NOTE), flat(sizes[2] + NOTE),
            flat(QUARTER + NOTE), flat(QUARTER + NOTE), flat(SLAB),
        ],
        in_specs=[smem] * 3 + [vmem] * 2,
        out_specs=[vmem] * 6,
        compiler_params=pltpu.CompilerParams(vmem_limit_bytes=6 * 2**20),
    )(where, global_ids, ids, own, got)


def join_kernel(sent_x, sent_y, sent_z, mine, from_x, from_y, from_z, from_xy, near0, near1, near2):
    for part, (sent, got, near) in enumerate(
        ((sent_x, from_x, near0), (sent_y, from_y, near1), (sent_z, from_z, near2))
    ):
        size = CHIP * PART_ROWS[part]
        near[0:size] = sent[0:size]
        near[size : 2 * size] = got[0:size]
    x, y = CHIP * PART_ROWS[0], CHIP * PART_ROWS[1]
    total = mine[...] + (from_x[x : x + QUARTER + NOTE] + from_y[y : y + QUARTER + NOTE] + from_xy[...])
    near1[2 * y : 2 * y + QUARTER + NOTE] = total


def join(sent, mine, got):
    vmem = pl.BlockSpec(memory_space=pltpu.VMEM)
    return pl.pallas_call(
        join_kernel,
        out_shape=[flat(2 * CHIP * rows + (QUARTER + NOTE if part == 1 else 0)) for part, rows in enumerate(PART_ROWS)],
        in_specs=[vmem] * 8,
        out_specs=[vmem] * 3,
        compiler_params=pltpu.CompilerParams(vmem_limit_bytes=9 * 2**20),
    )(*sent, mine, *got)


def plan_kernel(where_ref, ids_ref, glob_ref, slots):
    for part in range(3):
        list_wants(where_ref, ids_ref, glob_ref, where_ref[0], part, slots, part * SEG_BLK, None)


def plan(where, ids, global_ids):
    smem = pl.BlockSpec(memory_space=pltpu.SMEM)
    return pl.pallas_call(
        plan_kernel,
        out_shape=jax.ShapeDtypeStruct((3 * SEG_BLK,), jnp.int32),
        in_specs=[smem] * 3,
        out_specs=smem,
        compiler_params=pltpu.CompilerParams(vmem_limit_bytes=2**20),
    )(where, ids, global_ids)


def gather_kernel(part, low, high, where_ref, ids_ref, glob_ref, near, side, out_ref, slots):
    chip, core = where_ref[0], where_ref[1]
    d1, d2, d3 = PART_DIMS[part]
    size = PART_ROWS[part]

    def act(block, count):
        there = block // CHIP
        inside = block - there * CHIP
        apart = there ^ chip
        place = jnp.where(apart & d1 != 0, CHIP, 0)
        place += ((inside // HERE) ^ core) * HERE + lax.rem(inside, HERE)
        go = jnp.logical_and(count >= low, count < high)
        at = jnp.clip(count - low, 0, high - low - 1)
        target = pl.ds(pl.multiple_of(at * size, 16), size)
        source = pl.ds(pl.multiple_of(place * size, 16), size)

        @pl.when(jnp.logical_and(go, apart & d2 == 0))
        def _():
            out_ref[target] = near[source]

        @pl.when(jnp.logical_and(go, apart & d2 != 0))
        def _():
            out_ref[target] = side[source]

    list_wants(where_ref, ids_ref, glob_ref, chip ^ d3, part, slots, 0, act)


def gather(part, low, high, where, ids, global_ids, near, side):
    smem = pl.BlockSpec(memory_space=pltpu.SMEM)
    vmem = pl.BlockSpec(memory_space=pltpu.VMEM)
    return pl.pallas_call(
        functools.partial(gather_kernel, part, low, high),
        out_shape=flat((high - low) * PART_ROWS[part]),
        in_specs=[smem] * 3 + [vmem] * 2,
        out_specs=vmem,
        scratch_shapes=[pltpu.SMEM((SEG_BLK,), jnp.int32)],
        compiler_params=pltpu.CompilerParams(vmem_limit_bytes=5 * 2**20),
    )(where, ids, global_ids, near, side)


def flag_kernel(here, there, over, notes, sem):
    rows = pl.ds(QUARTER, NOTE)
    copies = [pltpu.make_async_copy(v.at[rows], notes.at[k], sem.at[k]) for k, v in enumerate((here, there))]
    for one in copies:
        one.start()
    for one in copies:
        one.wait()
    flags = notes[...].astype(jnp.float32)
    lane = lax.broadcasted_iota(jnp.int32, flags.shape, 2)
    over[0] = (jnp.max(jnp.where(lane == FLAG, flags, 0.0)) > 0).astype(jnp.int32)


def flag(here, there):
    anywhere = pl.BlockSpec(memory_space=pl.ANY)
    return pl.pallas_call(
        flag_kernel,
        out_shape=jax.ShapeDtypeStruct((1,), jnp.int32),
        in_specs=[anywhere] * 2,
        out_specs=pl.BlockSpec(memory_space=pltpu.SMEM),
        scratch_shapes=[pltpu.VMEM((2, NOTE, HEAD_DIM), jnp.bfloat16), pltpu.SemaphoreType.DMA((2,))],
        compiler_params=pltpu.CompilerParams(vmem_limit_bytes=2**20),
    )(here, there)


def nothing(shapes):
    return pl.pallas_call(
        lambda *refs: None,
        out_shape=shapes,
        out_specs=[pl.BlockSpec(memory_space=pl.ANY)] * len(shapes),
        compiler_params=pltpu.CompilerParams(vmem_limit_bytes=2**20),
    )()


OUTER, INNER, OWN, GLOBAL, RANDOM = 0, 1, 2, 2 + HERE, 2 + HERE + GLOB
N_ENTRY = RANDOM + HERE * RAND


def rows_of(ref, part, place, count=1):
    size = PART_ROWS[part]
    return ref.at[pl.ds(pl.multiple_of(place * size, 16), count * size)]


def collect(mine, where_ref, rand_ref, glob_ref, slots_ref, sources, bufs, sems):
    chip, core = where_ref[0], where_ref[1]
    nears, sides, fars, mores, quads, edge = sources
    half = core if mine else 1 - core
    base = 0 if mine else HERE

    def slot_of(block):
        return ((block // HERE) ^ core) * HERE + lax.rem(block, HERE)

    def copy(ref, part, place, entry, sem, count=1):
        source, target = rows_of(ref, part, place, count), rows_of(bufs[part], part, entry, count)
        pltpu.make_async_copy(source, target, sem).start()

    def fetch(block, entry, sem):
        there = block // CHIP
        slot = slot_of(block - there * CHIP)
        apart = chip ^ there
        for part in range(3):
            d1, d2, d3 = PART_DIMS[part]
            b1 = jnp.where(apart & d1 != 0, CHIP, 0)
            b2 = apart & d2 != 0
            b3 = apart & d3 != 0

            @pl.when(jnp.logical_and(jnp.logical_not(b2), jnp.logical_not(b3)))
            def _():
                copy(nears[part], part, b1 + slot, entry, sem)

            @pl.when(jnp.logical_and(b2, jnp.logical_not(b3)))
            def _():
                copy(sides[part], part, b1 + slot, entry, sem)

            cap = CAPS[part]
            place = slots_ref[part * SEG_BLK + block]

            @pl.when(jnp.logical_and(b3, place < cap))
            def _():
                copy(fars[part], part, jnp.clip(place, 0, cap - 1), entry, sem)

            @pl.when(jnp.logical_and(b3, place >= cap))
            def _():
                copy(mores[part], part, jnp.clip(place - cap, 0, MOST - cap - 1), entry, sem)

    def fetch_rows(source, low, high, entry, sem):
        for part in range(3):
            a, b = max(low, PART_AT[part]), min(high, PART_AT[part] + PART_ROWS[part])
            if a < b:
                at = pl.multiple_of(entry * PART_ROWS[part], 16) + a - PART_AT[part]
                to = bufs[part].at[pl.ds(pl.multiple_of(at, 16), b - a)]
                pltpu.make_async_copy(source.at[pl.ds(a - low, b - a)], to, sem).start()

    shared = sems.at[HERE]
    for part in range(3):
        copy(nears[part], part, base, OWN, shared, HERE)
        copy(nears[part], part, (HERE - base) + jnp.where(half == 0, 0, HERE - 1), INNER, shared)
    at_edge = chip == jnp.where(half == 0, 0, SEG_CHIPS - 1)

    @pl.when(at_edge)
    def _():
        fetch_rows(edge, 0, SLAB, OUTER, shared)

    @pl.when(jnp.logical_not(at_edge))
    def _():
        fetch(chip * CHIP + jnp.where(half == 0, -1, CHIP), OUTER, shared)

    for g in range(GLOB):
        block = in_segment(where_ref, glob_ref[g])

        @pl.when(block >= 0)
        def _():
            fetch(jnp.maximum(block, 0), GLOBAL + g, shared)

    for k in range(4):
        g = (chip & 1) ^ (k & 1)
        entry = GLOBAL + g
        row = ((chip >> 1) & 1) ^ (k >> 1)
        outside = in_segment(where_ref, glob_ref[g]) < 0
        for value in range(2):

            @pl.when(jnp.logical_and(outside, row == value))
            def _():
                fetch_rows(quads[k], value * QUARTER, (value + 1) * QUARTER, entry, shared)

    for row in range(HERE):
        for k in range(RAND):
            fetch(rand_ref[row, k], RANDOM + row * RAND + k, sems.at[row])

    def wait(low, count, sem):
        for part in range(3):
            of = rows_of(bufs[part], part, low, count)
            pltpu.make_async_copy(rows_of(nears[part], part, 0, count), of, sem).wait()

    return [lambda row=row: wait(RANDOM, RAND, sems.at[row]) for row in range(HERE)] + [
        lambda: wait(0, RANDOM, shared)
    ]


def attend_rows(mine, core, q_ref, bufs, out_ref, waits):
    outer_first = (core if mine else 1 - core) == 0
    factor = math.log2(math.e) / math.sqrt(HEAD_DIM)
    tail, mid = 2 * BLOCK, 3 * BLOCK - CUT_K

    def rows(part, entry, low, high):
        return bufs[part][pl.ds(pl.multiple_of(entry * PART_ROWS[part] + low, 16), high - low)]

    for row in range(HERE):
        if waits:
            waits[row]()
        before = OWN + row - 1 if row else jnp.where(outer_first, OUTER, INNER)
        after = OWN + row + 1 if row < HERE - 1 else jnp.where(outer_first, INNER, OUTER)
        at = RANDOM + row * RAND
        entries = [before, OWN + row, after, GLOBAL, GLOBAL + 1, at, at + 1, at + 2]
        keys, values = [], []
        for head in range(HALF - 1):
            keys.append([rows(head, i, 0, BLOCK) for i in entries])
            values.append([rows(head, i, BLOCK, 2 * BLOCK) for i in entries])
        keys.append([v for i in entries for v in (rows(0, i, tail, tail + CUT_K), rows(2, i, tail, mid))])
        values.append(
            [v for i in entries for v in (rows(1, i, tail, tail + CUT_V), rows(2, i, mid, PART_ROWS[2]))]
        )
        scores = [
            lax.dot_general(
                q_ref[row * BLOCK : (row + 1) * BLOCK, h * HEAD_DIM : (h + 1) * HEAD_DIM],
                jnp.concatenate(keys[h], axis=0),
                (((1,), (1,)), ((), ())),
                preferred_element_type=jnp.float32,
            )
            for h in range(HALF)
        ]
        probs = []
        for h in range(HALF):
            top = jnp.max(scores[h], axis=-1, keepdims=True)
            one = jnp.exp2((scores[h] - top) * factor)
            one = one * (1.0 / jnp.sum(one, axis=-1, keepdims=True))
            probs.append(one.astype(jnp.bfloat16))
        for h in range(HALF):
            mixed = jnp.dot(probs[h], jnp.concatenate(values[h], axis=0), preferred_element_type=jnp.float32)
            out_ref[row * BLOCK : (row + 1) * BLOCK, h * HEAD_DIM : (h + 1) * HEAD_DIM] = mixed.astype(jnp.bfloat16)


def mate_kernel(
    where_ref, rand_ref, rand_mate_ref, glob_ref, slots_ref, q_ref, q_mate_ref,
    near0, near1, near2, side0, side1, side2, far0, far1, far2, more0, more1, more2,
    quad, quad_x, quad_y, quad_xy, edge,
    out_ref, q_out, own0, own1, own2, buf0, buf1, buf2, q_buf, sems, own_sems, q_sems,
):
    core = where_ref[1]
    width = HALF * HEAD_DIM
    cols = pl.ds(pl.multiple_of(core * width, width), width)
    q_copy = pltpu.make_async_copy(q_mate_ref, q_buf, q_sems.at[0])
    q_own = pltpu.make_async_copy(q_ref.at[:, cols], q_out, q_sems.at[1])
    q_copy.start()
    sources = (
        (near0, near1, near2), (side0, side1, side2), (far0, far1, far2), (more0, more1, more2),
        (quad, quad_x, quad_y, quad_xy), edge,
    )
    bufs, own_bufs = (buf0, buf1, buf2), (own0, own1, own2)
    waits = collect(False, where_ref, rand_mate_ref, glob_ref, slots_ref, sources, bufs, sems)
    q_own.start()
    own_waits = collect(True, where_ref, rand_ref, glob_ref, slots_ref, sources, own_bufs, own_sems)
    q_copy.wait()
    waits[HERE]()
    attend_rows(False, core, q_buf, bufs, out_ref, waits)
    q_own.wait()
    for one in own_waits:
        one()


def own_kernel(where_ref, q_ref, buf0, buf1, buf2, out_ref):
    attend_rows(True, where_ref[1], q_ref, (buf0, buf1, buf2), out_ref, None)


def in_hbm(*arrays):
    return [pltpu.with_memory_space_constraint(v, pltpu.HBM) for v in arrays]


def attend_mate(where, rand, rand_mate, global_ids, slots, q, q_mate, nears, sides, fars, mores, quads, edge):
    vmem = pl.BlockSpec(memory_space=pltpu.VMEM)
    smem = pl.BlockSpec(memory_space=pltpu.SMEM)
    hbm = pl.BlockSpec(memory_space=pltpu.HBM)
    out = jax.ShapeDtypeStruct((HERE * BLOCK, HALF * HEAD_DIM), jnp.bfloat16)
    flops = HERE * BLOCK * HALF * (RANDOM + RAND) * BLOCK * HEAD_DIM * 4
    return pl.pallas_call(
        mate_kernel,
        out_shape=[out, out] + [flat(N_ENTRY * rows) for rows in PART_ROWS],
        in_specs=[smem] * 5 + [hbm] * 19,
        out_specs=[vmem] * 5,
        scratch_shapes=[pltpu.VMEM((N_ENTRY * rows, HEAD_DIM), jnp.bfloat16) for rows in PART_ROWS]
        + [
            pltpu.VMEM(out.shape, jnp.bfloat16),
            pltpu.SemaphoreType.DMA((HERE + 1,)),
            pltpu.SemaphoreType.DMA((HERE + 1,)),
            pltpu.SemaphoreType.DMA((2,)),
        ],
        compiler_params=pltpu.CompilerParams(vmem_limit_bytes=24 * 2**20),
        cost_estimate=pl.CostEstimate(flops=flops, bytes_accessed=N_ENTRY * SLAB * 512, transcendentals=0),
    )(where, rand, rand_mate, global_ids, slots, *in_hbm(q, q_mate, *nears, *sides, *fars, *mores, *quads, edge))


def attend_own(where, q, bufs):
    vmem = pl.BlockSpec(memory_space=pltpu.VMEM)
    flops = HERE * BLOCK * HALF * (RANDOM + RAND) * BLOCK * HEAD_DIM * 4
    return pl.pallas_call(
        own_kernel,
        out_shape=jax.ShapeDtypeStruct((HERE * BLOCK, HALF * HEAD_DIM), jnp.bfloat16),
        in_specs=[pl.BlockSpec(memory_space=pltpu.SMEM)] + [vmem] * 4,
        out_specs=vmem,
        compiler_params=pltpu.CompilerParams(vmem_limit_bytes=20 * 2**20),
        cost_estimate=pl.CostEstimate(flops=flops, bytes_accessed=N_ENTRY * SLAB * 256, transcendentals=0),
    )(where, q, *bufs)


def project_kernel(tiles, core_ref, own_ref, got_ref, weight_ref, out_ref, tile_ref, sems):
    core = core_ref[0]
    half = HALF * HEAD_DIM
    width = out_ref.shape[1] // tiles
    mine = pl.ds(pl.multiple_of(core * half, half), half)
    other = pl.ds(pl.multiple_of((1 - core) * half, half), half)
    copies = []
    for k in range(tiles):
        cols = pl.ds(k * width, width)
        total = jnp.dot(own_ref[...], weight_ref[mine, cols], preferred_element_type=jnp.float32)
        total += jnp.dot(got_ref[...], weight_ref[other, cols], preferred_element_type=jnp.float32)
        tile_ref[k] = total.astype(out_ref.dtype)
        copies.append(pltpu.make_async_copy(tile_ref.at[k], out_ref.at[:, cols], sems.at[k]))
        copies[k].start()
    for one in copies:
        one.wait()


def project(core, own, got, weight, tiles=4):
    width = weight.shape[1]
    rows = own.shape[0]
    vmem = pl.BlockSpec(memory_space=pltpu.VMEM)
    return pl.pallas_call(
        functools.partial(project_kernel, tiles),
        out_shape=jax.ShapeDtypeStruct((rows, width), jnp.bfloat16),
        in_specs=[pl.BlockSpec(memory_space=pltpu.SMEM), vmem, vmem, vmem],
        out_specs=pl.BlockSpec(memory_space=pl.ANY),
        scratch_shapes=[pltpu.VMEM((tiles, rows, width // tiles), jnp.bfloat16), pltpu.SemaphoreType.DMA((tiles,))],
        compiler_params=pltpu.CompilerParams(vmem_limit_bytes=14 * 2**20),
    )(core.reshape(1), own, got, weight)


def local(queries, keys_values, rand_blocks, global_ids, out_weight):
    n = lax.axis_size("seq")
    device = lax.axis_index("seq")
    core = device % 2
    chip = (device // 2) % SEG_CHIPS
    where = jnp.stack([chip, core, device // 2])
    rand_mate = swap(rand_blocks, 1)
    got = swap(pack(False, where, keys_values), 1)
    own = pack(True, where, keys_values)
    ids = jnp.concatenate([rand_blocks.reshape(-1), rand_mate.reshape(-1)])
    *sent, to_xy, mine, border = split(where, global_ids, ids, own, got)

    pairs = []
    chips = n // 2
    for c in range(chips):
        if c % SEG_CHIPS == SEG_CHIPS - 1:
            pairs += [(2 * c + k, 2 * ((c + 1) % chips) + k) for k in range(2)]
        if c % SEG_CHIPS == 0:
            pairs += [(2 * c + k, 2 * ((c - 1) % chips) + k) for k in range(2)]
    edge = lax.ppermute(border, "seq", pairs)
    q_mate = swap(half_queries(where, queries), 1)
    got = [swap(v, 2 * PART_DIMS[part][0]) for part, v in enumerate(sent)] + [swap(to_xy, 6)]
    got, q_mate = lax.optimization_barrier((got, q_mate))
    nears = join(sent, mine, got)
    asked = [got[k][CHIP * PART_ROWS[k] + more, :IDS].astype(jnp.int32) for k, more in ((2, 0), (0, QUARTER), (1, QUARTER))]

    sides = [swap(nears[part], 2 * PART_DIMS[part][1]) for part in range(3)]
    slots = plan(where, ids, global_ids)
    here = nears[1][2 * CHIP * PART_ROWS[1] :] + sides[1][2 * CHIP * PART_ROWS[1] :]
    slots, here, asked[2] = lax.optimization_barrier((slots, here, asked[2]))
    if n == 4 * SEG_CHIPS:
        total = swap(here, 16)
    else:
        total = here
        mask = 16
        while mask < n:
            total = total + swap(total, mask)
            mask *= 2

    edge, total, asked[0] = lax.optimization_barrier((edge, total, asked[0]))
    from_x = swap(total, 2)
    sides[0], sides[2] = lax.optimization_barrier((sides[0], sides[2]))
    fars = [
        swap(
            gather(part, 0, CAPS[part], where, asked[part], global_ids, nears[part], sides[part]),
            2 * PART_DIMS[part][2],
        )
        for part in range(3)
    ]
    from_y, from_xy = swap(total, 4), swap(from_x, 4)
    over = flag(here, total)[0] > 0
    over, fars[1], from_x = lax.optimization_barrier((over, fars[1], from_x))
    quads = [total, from_x, from_y, from_xy]

    def send_rest(args):
        asked, nears, sides = args
        return [
            swap(gather(part, CAPS[part], MOST, where, asked[part], global_ids, nears[part], sides[part]), 2 * PART_DIMS[part][2])
            for part in range(3)
        ]

    def send_none(args):
        return list(nothing([flat((MOST - cap) * rows) for cap, rows in zip(CAPS, PART_ROWS)]))

    mores = lax.cond(over, send_rest, send_none, (asked, nears, sides))

    out_mate, q_own, *bufs = attend_mate(
        where, rand_blocks, rand_mate, global_ids, slots, queries, q_mate, nears, sides, fars, mores, quads, edge
    )
    out_got = swap(out_mate, 1)
    out_own = attend_own(where, q_own, bufs)
    return project(core, out_own, out_got, out_weight)


def solution(mesh):
    placed = (P("seq", None), P(None, "seq", None), P("seq", None), P(), P())
    return jax.shard_map(
        local, mesh=mesh, in_specs=placed, out_specs=P("seq", None), check_vma=False
    )
```
